32 devices in a mesh: section: 4 (over y, x), dp: 8 (over z, core).
Axes of the slice: x: 2, y: 2, z: 4, core: 2. Of those that a mesh axis runs over, the one named last changes fastest.
Arguments:
- tokens: bfloat16 [2, 4096, 768], P(None, 'dp'), may hold values from -6 to 6
- cotangent: bfloat16 [2, 4096, 768], P(None, 'dp'), may hold values from -6 to 6
- norm_gain: bfloat16 [4, 768], P('section'), may hold values from 0.25 to 1.75
- norm_shift: bfloat16 [4, 768], P('section'), may hold values from -1.796875 to 1.796875
- in_weight: bfloat16 [4, 768, 3072], P('section'), may hold values from -1 to 1
- out_bias: bfloat16 [4, 768], P('section'), may hold values from -1.796875 to 1.796875
- down_weight: bfloat16 [6144, 768], P('section'), may hold values from -0.109375 to 0.109375
- hidden_bias: bfloat16 [6144], P('section'), may hold values from -3 to 3
- frame_device: int32 [2, 8], replicated, may hold values from 0 to 7, each once within a row
- tube_device: int32 [2, 8], replicated, may hold values from 0 to 7, each once within a row
- clip_kind: int32 [2], replicated, may hold values from 0 to 1
Outputs:
- output: bfloat16 [2, 4096, 768], P(None, 'dp', 'section')
- input_grad: float32 [2, 4096, 768], P(None, 'dp', 'section')
- grad_norm_gain: float32 [4, 768], P('section')
- grad_norm_shift: float32 [4, 768], P('section')
- grad_in_weight: float32 [4, 768, 3072], P('section')
- grad_out_bias: float32 [4, 768], P('section')
- grad_down_weight: float32 [6144, 768], P('section')
- grad_hidden_bias: float32 [6144], P('section')
The draws below stay inside these ranges and needn't reach their ends.
Inputs may be any that keep to these rules, and one draw needn't show every extreme that they name: `frame_device`: each row is a permutation. `tube_device`: each row is a permutation. `clip_kind`: 0 stands for 16x16 clips, 1 for 8x8 clips.
All inputs are finite; a program needn't handle non-finite values.
Results may differ from the reference program's by a relative error of at most 0.018.
Values may be sent and summed in bfloat16 or wider, within the bound.
A program may use at most 384 MiB of HBM per device.

```python
import jax
import jax.numpy as jnp
from jax import lax

D = 768
HEADS = 12
HEAD_DIM = 64
FF = 3072
SLOTS = 2
MICRO = 2
SUBLAYERS = 4
WINDOW = 256
TOK_DEV = 512
TOKENS = 4096
N_DP = 8


def draw_in_weight(key, part):
    key = jax.random.fold_in(key, 7)
    samples = jax.random.normal(key, (SUBLAYERS, D, FF), jnp.float32) * D ** (-0.5)
    column = jnp.arange(FF)
    sublayer = jnp.arange(SUBLAYERS)
    factor_table = jnp.where((sublayer[:, None] % 2 == 0) & (column[None, :] >= 3 * D), 8.0, 1.0)
    return jnp.clip(samples * factor_table[:, None, :], -1.0, 1.0).astype(jnp.bfloat16)


def levels(own_key, extent, shards, least, high):
    gain, own = 1.0, jax.random.fold_in(own_key, 6)
    for axis_at, shards_of in shards:
        steps = jnp.exp(jax.random.uniform(jax.random.fold_in(own, axis_at), (shards_of,), jnp.float32, least / len(shards), high / len(shards)))
        gain = gain * jnp.repeat(steps, extent[axis_at] // shards_of).reshape([-1 if axis == axis_at else 1 for axis in range(len(extent))])
    return gain


def normal_values(own_key, shape, deviation, most, cuts=(), kind=jnp.bfloat16):
    level = levels(own_key, shape, cuts, -0.22, 0.18) if cuts else 1.0
    entries = jax.random.normal(own_key, shape, jnp.float32) * deviation * level
    return jnp.minimum(jnp.maximum(entries, -most), most).astype(kind)


def setup_inputs(seed: int = 0) -> dict:
    keys = jax.random.split(jax.random.key(seed), 12)
    return {
        "tokens": normal_values(keys[0], (MICRO, TOKENS, D), 1.0, 6.0, ((1, 8),)),
        "cotangent": normal_values(keys[1], (MICRO, TOKENS, D), 1.0, 6.0, ((1, 8),)),
        "norm_gain": jnp.clip(1.0 + 0.15 * jax.random.normal(keys[2], (SUBLAYERS, D), jnp.float32), 0.25, 1.75).astype(jnp.bfloat16),
        "norm_shift": normal_values(keys[3], (SUBLAYERS, D), 0.3, 1.796875, ((0, 4),)),
        "in_weight": draw_in_weight(jax.random.fold_in(keys[11], 71), 0),
        "out_bias": normal_values(keys[5], (SUBLAYERS, D), 0.3, 1.796875, ((0, 4),)),
        "down_weight": normal_values(keys[6], (2 * FF, D), FF ** -0.5, 0.109375, ((0, 4),)),
        "hidden_bias": normal_values(keys[7], (2 * FF,), 0.5, 3.0, ((0, 4),)),
        "frame_device": jax.vmap(lambda own: jax.random.permutation(own, N_DP))(jax.random.split(keys[8], MICRO)).reshape((MICRO, N_DP)).astype(jnp.int32),
        "tube_device": jax.vmap(lambda own: jax.random.permutation(own, N_DP))(jax.random.split(keys[9], MICRO)).reshape((MICRO, N_DP)).astype(jnp.int32),
        "clip_kind": jax.random.randint(keys[10], (MICRO,), 0, 2).astype(jnp.int32),
    }


EPS = 1e-06
NEGATIVE = -1e+30

@jax.custom_vjp
def low(v):
    return lax.optimization_barrier(v.astype(jnp.bfloat16)).astype(jnp.float32)

@jax.custom_vjp
def low_back(v):
    return v

def low_keep(v):
    return (low(v), None)

def low_pass(kept, grad):
    return (grad,)

def back_keep(v):
    return (v, None)

def back_low(kept, grad):
    return (low(grad),)
low.defvjp(low_keep, low_pass)
low_back.defvjp(back_keep, back_low)

def matmul(left_side, right_side):
    return jnp.dot(left_side, right_side, precision=lax.Precision.HIGHEST, preferred_element_type=jnp.float32)

def layer_norm(hidden, gain_row, shift_row):
    average = lax.optimization_barrier(jnp.mean(hidden, axis=-1, keepdims=True))
    centred = hidden - average
    variance = lax.optimization_barrier(jnp.mean(centred * centred, axis=-1, keepdims=True))
    return centred * lax.rsqrt(variance + EPS) * gain_row + shift_row

def window_mask(clip_type):
    window_id = jnp.arange(WINDOW) % 16 // 4
    return jnp.logical_or(window_id[:, None] == window_id[None, :], clip_type == 0)

def attention(hidden, gain_row, shift_row, weight, bias_row, allowed):
    row_count = hidden.shape[0]
    normed = low(layer_norm(hidden, gain_row, shift_row))
    projected = matmul(normed, weight[:, :3 * D])
    queries = low(low_back(projected[:, :D]))
    key_rows = low(low_back(projected[:, D:2 * D]))
    value_rows = low(low_back(projected[:, 2 * D:3 * D]))

    def grouped(matrix):
        return matrix.reshape(row_count // (16 * WINDOW), 16, WINDOW, HEADS, HEAD_DIM)

    def one_group(blocks):
        query_block, key_block, value_block = blocks
        scores = low_back(jnp.einsum('gqhd,gkhd->ghqk', query_block, key_block, precision=lax.Precision.HIGHEST))
        scaled = jnp.where(allowed, scores * HEAD_DIM ** (-0.5), NEGATIVE)
        row_max = lax.optimization_barrier(jnp.max(scaled, axis=-1, keepdims=True))
        exponent = jnp.exp(scaled - row_max)
        attend_probs = exponent / lax.optimization_barrier(jnp.sum(exponent, axis=-1, keepdims=True))
        return jnp.einsum('ghqk,gkhd->gqhd', low(attend_probs), value_block, precision=lax.Precision.HIGHEST)
    attended = lax.map(jax.checkpoint(one_group), (grouped(queries), grouped(key_rows), grouped(value_rows)))
    attended = low(low_back(attended.reshape(row_count, D)))
    return hidden + low_back(matmul(attended, weight[:, 3 * D:]) + bias_row)

def feed_forward(hidden, gain_row, shift_row, weight, down_rows, hidden_bias_rows, bias_row):
    normed = low(layer_norm(hidden, gain_row, shift_row))
    pre_gelu = low_back(matmul(normed, weight) + hidden_bias_rows)
    active = low(low_back(jax.nn.gelu(pre_gelu, approximate=False)))
    return hidden + low_back(matmul(active, down_rows) + bias_row)

def relayout(hidden, frame_row, tube_row):
    devices = N_DP
    across = min(devices, 16)
    groups = devices // across
    repeat = 16 // across
    per_group = SLOTS // repeat
    by_device = hidden.reshape(devices, per_group, repeat, repeat, across, 16, D)
    by_role = by_device[frame_row].reshape(groups, across, per_group, repeat, repeat, across, 16, D)
    regrouped = by_role.transpose(0, 5, 2, 4, 1, 3, 6, 7).reshape(devices, TOK_DEV, D)
    placed = jnp.zeros_like(regrouped).at[tube_row].set(regrouped)
    return placed.reshape(TOKENS, D)

def reference(tokens, cotangent, norm_gain, norm_shift, in_weight, out_bias, down_weight, hidden_bias, frame_device, tube_device, clip_kind):
    floats = tuple((array.astype(jnp.float32) for array in (tokens, norm_gain, norm_shift, in_weight, out_bias, down_weight, hidden_bias)))

    def forward(tokens, norm_gain, norm_shift, in_weight, out_bias, down_weight, hidden_bias):
        outputs = []
        for micro_index in range(MICRO):
            allowed = window_mask(clip_kind[micro_index])
            hidden_state = tokens[micro_index]
            hidden_state = low(low_back(attention(hidden_state, norm_gain[0], norm_shift[0], in_weight[0], out_bias[0], allowed)))
            hidden_state = low(low_back(feed_forward(hidden_state, norm_gain[1], norm_shift[1], in_weight[1], down_weight[:FF], hidden_bias[:FF], out_bias[1])))
            hidden_state = relayout(hidden_state, frame_device[micro_index], tube_device[micro_index])
            hidden_state = low(low_back(attention(hidden_state, norm_gain[2], norm_shift[2], in_weight[2], out_bias[2], allowed)))
            hidden_state = low(feed_forward(hidden_state, norm_gain[3], norm_shift[3], in_weight[3], down_weight[FF:], hidden_bias[FF:], out_bias[3]))
            outputs.append(hidden_state)
        return jnp.stack(outputs)
    result, pullback = jax.vjp(forward, *floats)
    gradients = pullback(cotangent.astype(jnp.float32))
    return (result.astype(jnp.bfloat16), gradients[0], gradients[1], gradients[2], gradients[3], gradients[4], gradients[5], gradients[6])
```

```python
import functools

import jax
import jax.numpy as jnp
from jax import lax
from jax.experimental import pallas as pl
from jax.experimental.pallas import tpu as pltpu
from jax.sharding import PartitionSpec as P

HEAD_DIM = 64
WINDOW = 256
BLOCK = 16
SECTIONS = 4
EPS = 1e-06
NEGATIVE = -1e30
MESH = pl.DeviceIdType.MESH
F32 = jnp.float32
BF16 = jnp.bfloat16


def mm(left, right):
    return lax.dot_general(left, right, (((1,), (0,)), ((), ())), preferred_element_type=F32)


def mm_nt(left, right):
    return lax.dot_general(left, right, (((1,), (1,)), ((), ())), preferred_element_type=F32)


def mm_tn(left, right):
    return lax.dot_general(left, right, (((0,), (0,)), ((), ())), preferred_element_type=F32)


def remote(src, dst, send_sem, recv_sem, section, dp):
    return pltpu.make_async_remote_copy(
        src_ref=src,
        dst_ref=dst,
        send_sem=send_sem,
        recv_sem=recv_sem,
        device_id=(section, dp),
        device_id_type=MESH,
    )


def normalise(hidden):
    average = jnp.mean(hidden, axis=-1, keepdims=True)
    centred = hidden - average
    inverse = lax.rsqrt(jnp.mean(centred * centred, axis=-1, keepdims=True) + EPS)
    return centred * inverse, inverse


def gelu_and_slope(u):
    size = jnp.abs(u)
    bell = jnp.exp(-0.5 * u * u)
    t = 1.0 / (1.0 + (0.3275911 * 0.7071067811865476) * size)
    poly = t * (
        0.127414796
        + t * (-0.142248368 + t * (0.7107068705 + t * (-0.7265760135 + t * 0.5307027145)))
    )
    tail = poly * bell
    cdf = jnp.where(u >= 0, 1.0 - tail, tail)
    return u * cdf, cdf + u * bell * 0.3989422804014327


def main_kernel(
    cfg,
    tok_hbm,
    cot_hbm,
    gain_ref,
    shift_ref,
    w_hbm,
    bias_ref,
    down_hbm,
    hb_ref,
    ftab,
    ttab,
    kind,
    out_ref,
    gcol_ref,
    grad_hbm,
    small_ref,
    weight,
    down,
    grads,
    keep_a,
    keep_b,
    hin,
    gin,
    leave,
    nrm,
    work,
    xsend,
    xrecv0,
    xrecv1,
    blocks,
    bias_early,
    bias_late,
    mask_add,
    load_sem,
    w_send,
    w_recv,
    h_send,
    h_recv,
    g_send,
    g_recv,
    x_send,
    x_recv,
    o_send,
    o_recv,
):
    n, across, repeat, slots, chunks, width, wide, depth = cfg
    section = lax.axis_index("section")
    me = lax.axis_index("dp")
    core = lax.rem(me, 2)
    sibling = me + 1 - 2 * core
    is_attn = lax.rem(section, 2) == 0
    xrecv = (xrecv0, xrecv1)
    half = wide // 2
    part = half // 2
    quarter = width // SECTIONS

    load_w = pltpu.make_async_copy(w_hbm, weight, load_sem.at[0])
    load_d = pltpu.make_async_copy(down_hbm, down.at[pl.ds(half, half)], load_sem.at[1])
    load_t = pltpu.make_async_copy(tok_hbm, hin, load_sem.at[2])
    load_c = pltpu.make_async_copy(cot_hbm, gin, load_sem.at[3])

    @pl.when(section == 0)
    def _():
        load_t.start()

    load_w.start()

    @pl.when(section == 3)
    def _():
        load_c.start()

    @pl.when(jnp.logical_not(is_attn))
    def _():
        load_d.start()

    barrier = pltpu.get_barrier_semaphore()

    def greet(s, d):
        pl.semaphore_signal(barrier, inc=1, device_id=(s, d), device_id_type=MESH)

    @pl.when(section == 0)
    def _():
        greet(1, me)
        greet(3, me)
        pl.semaphore_wait(barrier, 2)

    @pl.when(section == 1)
    def _():
        greet(0, me)
        greet(1, sibling)
        greet(3, me)

        @pl.loop(0, n)
        def _(d):
            greet(2, d)

        pl.semaphore_wait(barrier, 3 + n)

    @pl.when(section == 2)
    def _():
        greet(3, me)

        @pl.loop(0, n)
        def _(d):
            greet(1, d)

        pl.semaphore_wait(barrier, 1 + n)

    @pl.when(section == 3)
    def _():
        greet(0, me)
        greet(1, me)
        greet(2, me)
        greet(3, sibling)
        pl.semaphore_wait(barrier, 4)

    bias_late[...] = hb_ref[...].astype(F32)
    own_part = pl.ds(core * part, part)
    other_part = pl.ds((1 - core) * part, part)
    send_down = remote(
        down_hbm.at[own_part], down.at[own_part], w_send.at[0], w_recv.at[0], section + 1, me
    )
    send_bias = remote(
        bias_late, bias_early, w_send.at[1], w_recv.at[1], section + 1, me
    )
    pass_down = remote(
        down.at[own_part], down.at[own_part], w_send.at[0], w_recv.at[2], section, sibling
    )

    gain = gain_ref[...].astype(F32)
    shift = shift_ref[...].astype(F32)
    bias = bias_ref[...].astype(F32)
    small_ref[...] = jnp.zeros_like(small_ref)

    def clear_grads(count):
        @pl.loop(0, count)
        def _(j):
            grads[j] = jnp.zeros((width, width), F32)

    def role_of(table, micro, device):
        def step(r, found):
            return found + jnp.where(table[micro, r] == device, r, 0)

        return lax.fori_loop(0, n, step, 0)

    def send_blocks(c, rows, table, to_section, forward):
        blocks[...] = rows.reshape(blocks.shape)
        micro = lax.div(c, slots)
        slot = lax.rem(c, depth)

        @pl.when(c >= depth)
        def _():
            remote(
                xsend.at[slot], xsend.at[slot], x_send.at[c - depth], x_recv.at[0], to_section, me
            ).wait_send()

        @pl.loop(0, n)
        def _(d):
            spot = lax.rem(role_of(table, micro, d), across)
            for g in range(repeat):
                block = g * across + spot if forward else spot * repeat + g
                xsend[slot, d, g] = blocks[block]

        for m in range(2):

            @pl.when(micro == m)
            def _():
                @pl.loop(0, n)
                def _(d):
                    remote(
                        xsend.at[slot, d],
                        xrecv[m].at[lax.rem(c, slots), me],
                        x_send.at[c],
                        x_recv.at[m],
                        to_section,
                        d,
                    ).start()

    def gather_blocks(c, own_table, their_table, target, from_section, forward):
        for m in range(2):

            @pl.when(c == m * slots)
            def _():
                remote(xrecv[m], xrecv[m], x_send.at[0], x_recv.at[m], from_section, me).wait_recv()
                family = lax.rem(lax.div(role_of(own_table, m, me), across), n // across)

                @pl.loop(0, slots)
                def _(s):
                    group, inner = lax.div(s, repeat), lax.rem(s, repeat)

                    @pl.loop(0, across)
                    def _(r):
                        source = their_table[m, family * across + r]
                        for f in range(repeat):
                            block = r * repeat + f if forward else f * across + r
                            rows = pl.ds(pl.multiple_of(block * BLOCK, BLOCK), BLOCK)
                            target[m * slots + s, rows] = xrecv[m][
                                group * repeat + f, source, inner
                            ]

    def norm_back(c, dn, gb):
        nh, inverse = normalise(hin[c].astype(F32))
        weighted = dn * gain
        first = jnp.mean(weighted, axis=-1, keepdims=True)
        second = jnp.mean(weighted * nh, axis=-1, keepdims=True)
        grad = gb.astype(F32) + inverse * (weighted - first - nh * second)
        small_ref[0:1] += jnp.sum(dn * nh, axis=0, keepdims=True)
        small_ref[1:2] += jnp.sum(dn, axis=0, keepdims=True)
        small_ref[2:3] += jnp.sum(gb.astype(F32), axis=0, keepdims=True)
        return grad

    @pl.when(is_attn)
    def _():
        send_down.start()
        send_bias.start()
        load_w.wait()

        @pl.when(section == 0)
        def _():
            load_t.wait()

        lane = lax.broadcasted_iota(jnp.int32, (1, 2 * HEAD_DIM), 1)
        first_head = jnp.where(lane < HEAD_DIM, 1.0, 0.0)
        pick = [first_head.astype(BF16), (1.0 - first_head).astype(BF16)]
        scale = HEAD_DIM ** (-0.5)
        pick_scaled = [
            (first_head * scale).astype(BF16),
            ((1.0 - first_head) * scale).astype(BF16),
        ]
        key_window = lax.broadcasted_iota(jnp.int32, (WINDOW, WINDOW), 0) % 16 // 4
        query_window = lax.broadcasted_iota(jnp.int32, (WINDOW, WINDOW), 1) % 16 // 4
        barred = jnp.where(key_window == query_window, 0.0, NEGATIVE)
        for m in range(2):
            mask_add[m] = barred * kind[m].astype(F32)

        def forward(c):
            @pl.when(section == 2)
            def _():
                gather_blocks(c, ttab, ftab, hin, 1, True)

            micro = lax.div(c, slots)
            hidden = hin[c].astype(F32)
            nh, _ = normalise(hidden)
            normed = (nh * gain + shift).astype(BF16)
            nrm[c] = normed
            for j in range(3):
                columns = pl.ds(j * width, width)
                keep_b[c, :, columns] = mm(normed, weight[:, columns]).astype(BF16)

            @pl.loop(0, width // (2 * HEAD_DIM))
            def _(pair):
                offset = pl.multiple_of(pair * 2 * HEAD_DIM, 2 * HEAD_DIM)
                q = keep_b[c, :, pl.ds(offset, 2 * HEAD_DIM)]
                k = keep_b[c, :, pl.ds(width + offset, 2 * HEAD_DIM)]
                v = keep_b[c, :, pl.ds(2 * width + offset, 2 * HEAD_DIM)]
                o = None
                for one in range(2):
                    z = mm_nt(k, q * pick_scaled[one]) + mask_add[micro]
                    top = jnp.max(z, axis=0, keepdims=True)
                    e = jnp.exp(z - top)
                    p = e * (1.0 / jnp.sum(e, axis=0, keepdims=True))
                    pb = p.astype(BF16)
                    spot = pl.multiple_of((2 * pair + one) * WINDOW, WINDOW)
                    keep_a[c, :, pl.ds(spot, WINDOW)] = pb
                    term = mm_tn(pb, v * pick[one])
                    o = term if o is None else o + term
                keep_b[c, :, pl.ds(3 * width + offset, 2 * HEAD_DIM)] = o.astype(BF16)

            branch = mm(keep_b[c, :, pl.ds(3 * width, width)], weight[:, pl.ds(3 * width, width)])
            leave[c] = (hin[c].astype(F32) + branch + bias).astype(BF16)
            remote(
                leave.at[c], hin.at[c], h_send.at[c], h_recv.at[c], section + 1, me
            ).start()

        def backward(c):
            @pl.when(c == 0)
            def _():
                clear_grads(4)

            remote(gin.at[c], gin.at[c], g_send.at[c], g_recv.at[c], section + 1, me).wait_recv()
            remote(
                leave.at[c], hin.at[c], h_send.at[c], h_recv.at[c], section + 1, me
            ).wait_send()
            gb = gin[c]
            work[...] = mm_nt(gb, weight[:, pl.ds(3 * width, width)]).astype(BF16)

            @pl.loop(0, width // (2 * HEAD_DIM))
            def _(pair):
                offset = pl.multiple_of(pair * 2 * HEAD_DIM, 2 * HEAD_DIM)
                q_at = pl.ds(offset, 2 * HEAD_DIM)
                k_at = pl.ds(width + offset, 2 * HEAD_DIM)
                v_at = pl.ds(2 * width + offset, 2 * HEAD_DIM)
                q, k, v = keep_b[c, :, q_at], keep_b[c, :, k_at], keep_b[c, :, v_at]
                go = work[:, q_at]
                dq = dk = dv = None
                for one in range(2):
                    spot = pl.multiple_of((2 * pair + one) * WINDOW, WINDOW)
                    pb = keep_a[c, :, pl.ds(spot, WINDOW)]
                    p = pb.astype(F32)
                    dp = mm_nt(v, go * pick[one])
                    pdp = p * dp
                    ds = (pdp - p * jnp.sum(pdp, axis=0, keepdims=True)).astype(BF16)
                    tv = mm(pb, go * pick[one])
                    tk = mm(ds, q * pick_scaled[one])
                    tq = mm_tn(ds, k * pick_scaled[one])
                    dv = tv if dv is None else dv + tv
                    dk = tk if dk is None else dk + tk
                    dq = tq if dq is None else dq + tq
                keep_b[c, :, q_at] = dq.astype(BF16)
                keep_b[c, :, k_at] = dk.astype(BF16)
                keep_b[c, :, v_at] = dv.astype(BF16)

            dn = mm_nt(keep_b[c, :, pl.ds(0, 3 * width)], weight[:, pl.ds(0, 3 * width)])
            leaving = norm_back(c, dn, gb).astype(BF16)

            @pl.when(section == 2)
            def _():
                send_blocks(c, leaving, ftab, 1, False)

            @pl.when(section == 0)
            def _():
                for s in range(SECTIONS):
                    gcol_ref[s, c] = leaving[:, s * quarter : (s + 1) * quarter]

            normed = nrm[c]
            for j in range(3):
                grads[j] += mm_tn(normed, keep_b[c, :, pl.ds(j * width, width)])
            grads[3] += mm_tn(keep_b[c, :, pl.ds(3 * width, width)], gin[c])

        @pl.loop(0, 2 * chunks)
        def _(step):
            c = lax.rem(step, chunks)

            @pl.when(step < chunks)
            def _():
                forward(c)

            @pl.when(step >= chunks)
            def _():
                backward(c)

    @pl.when(jnp.logical_not(is_attn))
    def _():
        early = remote(
            down_hbm.at[own_part], down.at[own_part], w_send.at[0], w_recv.at[0], section - 1, me
        )
        early_bias = remote(
            bias_late, bias_early, w_send.at[1], w_recv.at[1], section - 1, me
        )
        other = remote(
            down.at[other_part], down.at[other_part], w_send.at[0], w_recv.at[2], section, sibling
        )
        load_w.wait()
        early_bias.wait_recv()

        @pl.when(section == 3)
        def _():
            load_c.wait()
            clear_grads(8)

        def forward(c):
            remote(hin.at[c], hin.at[c], h_send.at[c], h_recv.at[c], section - 1, me).wait_recv()
            hidden = hin[c].astype(F32)
            nh, _ = normalise(hidden)
            normed = (nh * gain + shift).astype(BF16)
            nrm[c] = normed
            for j in range(4):
                columns = pl.ds(j * width, width)
                u = mm(normed, weight[:, columns])
                u = u + (bias_early, bias_late)[j // 2][:, pl.ds((j % 2) * width, width)]
                active, slope = gelu_and_slope(u)
                keep_a[c, :, columns] = active.astype(BF16)
                keep_b[c, :, columns] = slope.astype(BF16)

            @pl.when(c == 0)
            def _():
                early.wait_recv()
                pass_down.start()
                load_d.wait()
                other.wait_recv()

            branch = mm(keep_a[c], down[...])
            leaving = (hin[c].astype(F32) + branch + bias).astype(BF16)

            @pl.when(section == 1)
            def _():
                send_blocks(c, leaving, ttab, 2, True)

            @pl.when(section == 3)
            def _():
                for s in range(SECTIONS - 1):
                    gcol_ref[s, c] = leaving[:, s * quarter : (s + 1) * quarter]
                out_ref[c] = leaving[:, (SECTIONS - 1) * quarter :]
                for s in range(SECTIONS - 1):
                    remote(
                        gcol_ref.at[s, c], out_ref.at[c], o_send.at[s, c], o_recv.at[0], s, me
                    ).start()

        def backward(c):
            @pl.when(section == 1)
            def _():
                @pl.when(c == 0)
                def _():
                    clear_grads(8)

                gather_blocks(c, ftab, ttab, gin, 2, False)

            gb = gin[c]
            for j in range(4):
                columns = pl.ds(j * width, width)
                da = mm_nt(gb, down[columns])
                du = da * keep_b[c, :, columns].astype(F32)
                keep_b[c, :, columns] = du.astype(BF16)
                small_ref[3 + j : 4 + j] += jnp.sum(du, axis=0, keepdims=True)
            dn = mm_nt(keep_b[c], weight[...])
            leave[c] = norm_back(c, dn, gb).astype(BF16)
            remote(
                leave.at[c], gin.at[c], g_send.at[c], g_recv.at[c], section - 1, me
            ).start()
            normed = nrm[c]
            for j in range(4):
                columns = pl.ds(j * width, width)
                grads[j] += mm_tn(normed, keep_b[c, :, columns])
                grads[4 + j] += mm_tn(keep_a[c, :, columns], gin[c])

        @pl.loop(0, 2 * chunks)
        def _(step):
            last = lax.div(section, 2)
            c = last * lax.div(step, 2) + (1 - last) * lax.rem(step, chunks)
            back = last * lax.rem(step, 2) + (1 - last) * lax.div(step, chunks)

            @pl.when(back == 0)
            def _():
                forward(c)

            @pl.when(back == 1)
            def _():
                backward(c)

    @pl.when(is_attn)
    def _():
        send_down.wait_send()
        send_bias.wait_send()

    @pl.when(jnp.logical_not(is_attn))
    def _():
        pass_down.wait_send()

    stores = []
    for j in range(4):
        weight[:, pl.ds(j * width, width)] = grads[j].astype(BF16)
    for j in range(4):
        columns = pl.ds(j * width, width)
        store = pltpu.make_async_copy(
            weight.at[:, columns], grad_hbm.at[columns], load_sem.at[j]
        )
        store.start()
        stores.append(store)

    @pl.when(jnp.logical_not(is_attn))
    def _():
        more = []
        for j in range(4):
            rows = pl.ds(j * width, width)
            down[rows] = grads[4 + j].astype(BF16)
            store = pltpu.make_async_copy(
                down.at[rows], grad_hbm.at[pl.ds((4 + j) * width, width)], load_sem.at[4 + j]
            )
            store.start()
            more.append(store)
        for store in more:
            store.wait()

        @pl.loop(0, chunks)
        def _(c):
            remote(
                leave.at[c], gin.at[c], g_send.at[c], g_recv.at[c], section - 1, me
            ).wait_send()

    for store in stores:
        store.wait()

    @pl.when((section == 1) | (section == 2))
    def _():
        @pl.loop(chunks - depth, chunks)
        def _(c):
            slot = lax.rem(c, depth)
            remote(
                xsend.at[slot], xsend.at[slot], x_send.at[c], x_recv.at[0], 3 - section, me
            ).wait_send()

    @pl.when(section == 3)
    def _():
        @pl.loop(0, chunks)
        def _(c):
            for s in range(SECTIONS - 1):
                remote(
                    gcol_ref.at[s, c], out_ref.at[c], o_send.at[s, c], o_recv.at[0], s, me
                ).wait_send()

    @pl.when(section != 3)
    def _():
        remote(out_ref, out_ref, o_send.at[0, 0], o_recv.at[0], 3, me).wait_recv()


def pipeline(tokens, cotangent, gain, shift, weight, bias, down, hidden_bias, ftab, ttab, kind):
    micro, rows, width = tokens.shape
    wide = weight.shape[1]
    n = lax.axis_size("dp")
    across = min(n, 16)
    repeat = 16 // across
    slots = rows // WINDOW
    chunks = micro * slots
    quarter = width // SECTIONS
    depth = chunks if n <= 8 else slots
    cfg = (n, across, repeat, slots, chunks, width, wide, depth)
    vmem = pl.BlockSpec(memory_space=pltpu.VMEM)
    smem = pl.BlockSpec(memory_space=pltpu.SMEM)
    anywhere = pl.BlockSpec(memory_space=pl.ANY)
    dma = pltpu.SemaphoreType.DMA
    chunked = (chunks, WINDOW, width)
    return pl.pallas_call(
        functools.partial(main_kernel, cfg),
        out_shape=(
            jax.ShapeDtypeStruct((chunks, WINDOW, quarter), BF16),
            jax.ShapeDtypeStruct((SECTIONS, chunks, WINDOW, quarter), BF16),
            jax.ShapeDtypeStruct((8 * width, width), BF16),
            jax.ShapeDtypeStruct((8, width), F32),
        ),
        in_specs=[anywhere, anywhere, vmem, vmem, anywhere, vmem, anywhere, vmem, smem, smem, smem],
        out_specs=(vmem, vmem, anywhere, vmem),
        scratch_shapes=[
            pltpu.VMEM((width, wide), BF16),
            pltpu.VMEM((wide, width), BF16),
            pltpu.VMEM((8, width, width), F32),
            pltpu.VMEM((chunks, WINDOW, wide), BF16),
            pltpu.VMEM((chunks, WINDOW, wide), BF16),
            pltpu.VMEM(chunked, BF16),
            pltpu.VMEM(chunked, BF16),
            pltpu.VMEM(chunked, BF16),
            pltpu.VMEM(chunked, BF16),
            pltpu.VMEM((WINDOW, width), BF16),
            pltpu.VMEM((depth, n, repeat, BLOCK, width), BF16),
            pltpu.VMEM((slots, n, repeat, BLOCK, width), BF16),
            pltpu.VMEM((slots, n, repeat, BLOCK, width), BF16),
            pltpu.VMEM((WINDOW // BLOCK, BLOCK, width), BF16),
            pltpu.VMEM((1, wide // 2), F32),
            pltpu.VMEM((1, wide // 2), F32),
            pltpu.VMEM((2, WINDOW, WINDOW), F32),
            dma((8,)),
            dma((2,)),
            dma((3,)),
            dma((chunks,)),
            dma((chunks,)),
            dma((chunks,)),
            dma((chunks,)),
            dma((chunks,)),
            dma((micro,)),
            dma((SECTIONS - 1, chunks)),
            dma((1,)),
        ],
        compiler_params=pltpu.CompilerParams(
            collective_id=0, has_side_effects=True, vmem_limit_bytes=62 * 1024 * 1024
        ),
        name="pipeline",
    )(
        tokens.reshape(chunked),
        cotangent.reshape(chunked),
        gain,
        shift,
        weight,
        bias,
        down,
        hidden_bias.reshape(1, -1),
        ftab,
        ttab,
        kind,
    )


def reduce_kernel(
    cfg,
    grad_hbm,
    small_in,
    gcol_hbm,
    total_hbm,
    small_out,
    ig_ref,
    mine,
    theirs,
    from_low,
    from_high,
    acc,
    small_all,
    small_pair,
    load_sem,
    sib_send,
    sib_recv,
    up_send,
    low_recv,
    down_send,
    high_recv,
    left_send,
    right_send,
    total_recv,
    pair_send,
    pair_recv,
    local_sem,
    x_send,
    x_recv,
    small_send,
    small_recv,
    spair_send,
    spair_recv,
    ig_send,
    ig_recv,
    x_ready,
):
    n, chunk, w_chunks, d_chunks, lag, begin = cfg
    section = lax.axis_index("section")
    me = lax.axis_index("dp")
    core = lax.rem(me, 2)
    place = lax.div(me, 2)
    places = n // 2
    sibling = me + 1 - 2 * core
    is_attn = lax.rem(section, 2) == 0
    not_attn = jnp.logical_not(is_attn)
    partner = section + 1 - 2 * lax.rem(section, 2)
    lines = w_chunks + d_chunks
    half_w = w_chunks * chunk
    half_d = d_chunks * chunk

    def pieces(of_core):
        return (
            grad_hbm.at[pl.ds(of_core * half_w, half_w)],
            grad_hbm.at[pl.ds(2 * half_w + 2 * half_d + of_core * half_d, half_d)],
            grad_hbm.at[pl.ds(2 * half_w + of_core * half_d, half_d)],
        )

    spans = ((0, w_chunks), (w_chunks, d_chunks), (lines, d_chunks))
    loads = [
        pltpu.make_async_copy(
            piece, mine.at[pl.ds(first * chunk, count * chunk)], load_sem.at[at]
        )
        for at, (piece, (first, count)) in enumerate(zip(pieces(core), spans))
    ]

    loads[0].start()

    @pl.when(not_attn)
    def _():
        loads[1].start()
        loads[2].start()

    barrier = pltpu.get_barrier_semaphore()

    def greet(s, d):
        pl.semaphore_signal(barrier, inc=1, device_id=(s, d), device_id_type=MESH)

    @pl.loop(0, n)
    def _(d):
        @pl.when(d != me)
        def _():
            greet(section, d)

    @pl.when(section != 0)
    def _():
        greet(0, me)

    @pl.when(section == 3)
    def _():
        greet(2, me)

    pl.semaphore_wait(
        barrier, n - 1 + jnp.where(section == 0, 3, jnp.where(section == 2, 1, 0))
    )

    @pl.when(is_attn)
    def _():
        pl.semaphore_signal(x_ready, inc=1, device_id=(partner, me), device_id_type=MESH)

    def rows(i):
        return pl.ds(pl.multiple_of(i * chunk, chunk), chunk)

    def sib_copy(i, source_row):
        return remote(
            grad_hbm.at[pl.ds(pl.multiple_of(source_row, chunk), chunk)],
            theirs.at[rows(i)],
            sib_send.at[i],
            sib_recv.at[i],
            section,
            sibling,
        )

    def sib_row(i):
        from_w = (1 - core) * half_w + i * chunk
        late = 2 * half_w + 2 * half_d + (1 - core) * half_d + (i - w_chunks) * chunk
        early = 2 * half_w + (1 - core) * half_d + (i - lines) * chunk
        return jnp.where(i < w_chunks, from_w, jnp.where(i < lines, late, early))

    sib_count = jnp.where(is_attn, w_chunks, lines + d_chunks)

    @pl.loop(0, lines + d_chunks)
    def _(i):
        @pl.when(i < sib_count)
        def _():
            sib_copy(i, sib_row(i)).start()

    small_all[me] = small_in[...]

    def small_copy(d):
        return remote(
            small_in, small_all.at[me], small_send.at[d], small_recv.at[0], section, d
        )

    @pl.loop(0, n)
    def _(d):
        @pl.when(d != me)
        def _():
            small_copy(d).start()

    def ig_copy(s):
        return remote(gcol_hbm.at[s], ig_ref, ig_send.at[s], ig_recv.at[0], s, me)

    ig_own = pltpu.make_async_copy(gcol_hbm.at[0], ig_ref, ig_send.at[0])

    @pl.when(section == 0)
    def _():
        ig_own.start()
        for s in range(1, SECTIONS):
            ig_copy(s).start()

    def root_of(i):
        return places // 2 - 1 + lax.rem(i, 2)

    def total_rows(i):
        return total_hbm.at[core, rows(i)]

    def up_copy(i):
        return remote(
            mine.at[rows(i)], from_low.at[rows(i)], up_send.at[i], low_recv.at[i], section, me + 2
        )

    def down_copy(i):
        return remote(
            mine.at[rows(i)],
            from_high.at[rows(i)],
            down_send.at[i],
            high_recv.at[i],
            section,
            me - 2,
        )

    def left_copy(i, source):
        return remote(
            source, total_rows(i), left_send.at[i], total_recv.at[i], section, me - 2
        )

    def right_copy(i, source):
        return remote(
            source, total_rows(i), right_send.at[i], total_recv.at[i], section, me + 2
        )

    def pair_copy(i, source):
        return remote(
            source, total_rows(i), pair_send.at[i], pair_recv.at[0], section, sibling
        )

    def own_copy(i):
        return pltpu.make_async_copy(mine.at[rows(i)], total_rows(i), local_sem.at[i])

    def x_copy(e):
        return remote(
            mine.at[rows(lines + e)],
            mine.at[rows(w_chunks + e)],
            x_send.at[e],
            x_recv.at[e],
            partner,
            me,
        )

    def reduce_stage(i):
        root = root_of(i)
        summed = is_attn & (i >= w_chunks)

        @pl.when(i == 0)
        def _():
            loads[0].wait()

        @pl.when((i == w_chunks) & not_attn)
        def _():
            loads[1].wait()

        @pl.when(summed)
        def _():
            x_copy(i - w_chunks).wait_recv()
            acc[...] = mine[rows(i)].astype(F32)

        @pl.when(jnp.logical_not(summed))
        def _():
            sib_copy(i, 0).wait_recv()
            acc[...] = mine[rows(i)].astype(F32) + theirs[rows(i)].astype(F32)

        @pl.when((place <= root) & (place > 0))
        def _():
            up_copy(i).wait_recv()
            acc[...] += from_low[rows(i)].astype(F32)

        @pl.when((place >= root) & (place < places - 1))
        def _():
            down_copy(i).wait_recv()
            acc[...] += from_high[rows(i)].astype(F32)

        mine[rows(i)] = acc[...].astype(BF16)

        @pl.when(place < root)
        def _():
            up_copy(i).start()

        @pl.when(place > root)
        def _():
            down_copy(i).start()

        @pl.when(place == root)
        def _():
            source = mine.at[rows(i)]

            @pl.when(place > 0)
            def _():
                left_copy(i, source).start()

            @pl.when(place < places - 1)
            def _():
                right_copy(i, source).start()

            pair_copy(i, source).start()
            own_copy(i).start()

    def early_stage(e):
        @pl.when(e == 0)
        def _():
            loads[2].wait()
            pl.semaphore_wait(x_ready, 1)

        sib_copy(lines + e, 0).wait_recv()
        here = rows(lines + e)
        mine[here] = (mine[here].astype(F32) + theirs[here].astype(F32)).astype(BF16)
        x_copy(e).start()

    def spread_stage(i):
        root = root_of(i)

        @pl.when(place != root)
        def _():
            left_copy(i, total_rows(i)).wait_recv()

            @pl.when((place < root) & (place > 0))
            def _():
                left_copy(i, total_rows(i)).start()

            @pl.when((place > root) & (place < places - 1))
            def _():
                right_copy(i, total_rows(i)).start()

            pair_copy(i, total_rows(i)).start()

    @pl.loop(0, lines + lag)
    def _(i):
        @pl.when(i < lines)
        def _():
            reduce_stage(i)

        @pl.when(not_attn & (i >= begin) & (i < begin + d_chunks))
        def _():
            early_stage(i - begin)

        @pl.when(i >= lag)
        def _():
            spread_stage(i - lag)

    remote(
        small_all.at[pl.ds(0, n - 1)],
        small_all.at[pl.ds(0, n - 1)],
        small_send.at[0],
        small_recv.at[0],
        section,
        sibling,
    ).wait_recv()

    def add(d, so_far):
        return so_far + small_all[d]

    small_out[...] = lax.fori_loop(1, n, add, small_all[0])
    to_pair = remote(
        small_out, small_pair, spair_send.at[0], spair_recv.at[0], partner, me
    )

    @pl.when(not_attn)
    def _():
        to_pair.start()
        to_pair.wait_send()

    @pl.when(is_attn)
    def _():
        to_pair.wait_recv()
        small_out[5:7] = small_pair[3:5]

    @pl.loop(0, lines)
    def _(i):
        root = root_of(i)

        @pl.when(place < root)
        def _():
            up_copy(i).wait_send()

        @pl.when(place > root)
        def _():
            down_copy(i).wait_send()

        @pl.when((place <= root) & (place > 0))
        def _():
            left_copy(i, total_rows(i)).wait_send()

        @pl.when((place >= root) & (place < places - 1))
        def _():
            right_copy(i, total_rows(i)).wait_send()

        pair_copy(i, total_rows(i)).wait_send()

        @pl.when(place == root)
        def _():
            own_copy(i).wait()

    @pl.loop(0, lines + d_chunks)
    def _(i):
        @pl.when(i < sib_count)
        def _():
            sib_copy(i, 0).wait_send()

    @pl.when(not_attn)
    def _():
        @pl.loop(0, d_chunks)
        def _(e):
            x_copy(e).wait_send()

    @pl.loop(0, n)
    def _(d):
        @pl.when(d != me)
        def _():
            small_copy(d).wait_send()

    @pl.when(section == 0)
    def _():
        ig_own.wait()
        for s in range(1, SECTIONS):
            ig_copy(s).wait_send()

    @pl.when(section != 0)
    def _():
        ig_copy(0).wait_recv()

    remote(
        total_hbm.at[1 - core],
        total_hbm.at[1 - core],
        pair_send.at[0],
        pair_recv.at[0],
        section,
        sibling,
    ).wait_recv()


def reduction(grads, small, gcol, chunk=96):
    width = grads.shape[1]
    half_w = 2 * width
    half_d = width
    n = lax.axis_size("dp")
    w_chunks, d_chunks = half_w // chunk, half_d // chunk
    lines = w_chunks + d_chunks
    cfg = (n, chunk, w_chunks, d_chunks, min(6, lines), d_chunks)
    vmem = pl.BlockSpec(memory_space=pltpu.VMEM)
    anywhere = pl.BlockSpec(memory_space=pl.ANY)
    dma = pltpu.SemaphoreType.DMA
    every = lines + d_chunks
    return pl.pallas_call(
        functools.partial(reduce_kernel, cfg),
        out_shape=(
            jax.ShapeDtypeStruct((2, half_w + half_d, width), BF16),
            jax.ShapeDtypeStruct((8, width), F32),
            jax.ShapeDtypeStruct(gcol.shape[1:], BF16),
        ),
        in_specs=[anywhere, vmem, anywhere],
        out_specs=(anywhere, vmem, vmem),
        scratch_shapes=[
            pltpu.VMEM((every * chunk, width), BF16),
            pltpu.VMEM((every * chunk, width), BF16),
            pltpu.VMEM((lines * chunk, width), BF16),
            pltpu.VMEM((lines * chunk, width), BF16),
            pltpu.VMEM((chunk, width), F32),
            pltpu.VMEM((n, 8, width), F32),
            pltpu.VMEM((8, width), F32),
            dma((3,)),
            dma((every,)),
            dma((every,)),
            dma((lines,)),
            dma((lines,)),
            dma((lines,)),
            dma((lines,)),
            dma((lines,)),
            dma((lines,)),
            dma((lines,)),
            dma((lines,)),
            dma((1,)),
            dma((lines,)),
            dma((d_chunks,)),
            dma((d_chunks,)),
            dma((n,)),
            dma((1,)),
            dma((1,)),
            dma((1,)),
            dma((SECTIONS,)),
            dma((1,)),
            pltpu.SemaphoreType.REGULAR,
        ],
        compiler_params=pltpu.CompilerParams(
            collective_id=1, has_side_effects=True, vmem_limit_bytes=40 * 1024 * 1024
        ),
        name="reduction",
    )(grads, small, gcol)


def on_device(
    tokens,
    cotangent,
    norm_gain,
    norm_shift,
    in_weight,
    out_bias,
    down_weight,
    hidden_bias,
    frame_device,
    tube_device,
    clip_kind,
):
    micro, rows, width = tokens.shape
    output, gcol, grads, small = pipeline(
        tokens,
        cotangent,
        norm_gain,
        norm_shift,
        in_weight[0],
        out_bias,
        down_weight,
        hidden_bias,
        frame_device,
        tube_device,
        clip_kind,
    )
    total, small_total, input_grad = reduction(grads, small, gcol)
    split = total.shape[1] * 2 // 3
    grad_weight = total[:, :split].reshape(SECTIONS, width, width).transpose(1, 0, 2)
    quarter = width // SECTIONS
    return (
        output.reshape(micro, rows, quarter),
        input_grad.astype(F32).reshape(micro, rows, quarter),
        small_total[0:1],
        small_total[1:2],
        grad_weight.reshape(1, width, -1).astype(F32),
        small_total[2:3],
        total[:, split:].reshape(-1, width).astype(F32),
        small_total[5:7].reshape(-1),
    )


def solution(mesh):
    return jax.shard_map(
        on_device,
        mesh=mesh,
        in_specs=(
            P(None, "dp", None),
            P(None, "dp", None),
            P("section", None),
            P("section", None),
            P("section", None, None),
            P("section", None),
            P("section", None),
            P("section"),
            P(),
            P(),
            P(),
        ),
        out_specs=(
            P(None, "dp", "section"),
            P(None, "dp", "section"),
            P("section", None),
            P("section", None),
            P("section", None, None),
            P("section", None),
            P("section", None),
            P("section"),
        ),
        check_vma=False,
    )
```

```python
import functools

import jax
import jax.numpy as jnp
from jax import lax
from jax.experimental import pallas as pl
from jax.experimental.pallas import tpu as pltpu
from jax.sharding import PartitionSpec as P

HEAD_DIM = 64
WINDOW = 256
BLOCK = 16
SECTIONS = 4
EPS = 1e-06
NEGATIVE = -1e30
MESH = pl.DeviceIdType.MESH
F32 = jnp.float32
BF16 = jnp.bfloat16


def mm(left, right):
    return lax.dot_general(left, right, (((1,), (0,)), ((), ())), preferred_element_type=F32)


def mm_nt(left, right):
    return lax.dot_general(left, right, (((1,), (1,)), ((), ())), preferred_element_type=F32)


def mm_tn(left, right):
    return lax.dot_general(left, right, (((0,), (0,)), ((), ())), preferred_element_type=F32)


def remote(src, dst, send_sem, recv_sem, section, dp):
    return pltpu.make_async_remote_copy(
        src_ref=src,
        dst_ref=dst,
        send_sem=send_sem,
        recv_sem=recv_sem,
        device_id=(section, dp),
        device_id_type=MESH,
    )


def normalise(hidden):
    average = jnp.mean(hidden, axis=-1, keepdims=True)
    centred = hidden - average
    inverse = lax.rsqrt(jnp.mean(centred * centred, axis=-1, keepdims=True) + EPS)
    return centred * inverse, inverse


def gelu_and_slope(u):
    size = jnp.abs(u)
    bell = jnp.exp(-0.5 * u * u)
    t = 1.0 / (1.0 + (0.3275911 * 0.7071067811865476) * size)
    poly = t * (
        0.127414796
        + t * (-0.142248368 + t * (0.7107068705 + t * (-0.7265760135 + t * 0.5307027145)))
    )
    tail = poly * bell
    cdf = jnp.where(u >= 0, 1.0 - tail, tail)
    return u * cdf, cdf + u * bell * 0.3989422804014327


def main_kernel(
    cfg,
    tok_hbm,
    cot_hbm,
    gain_ref,
    shift_ref,
    w_hbm,
    bias_ref,
    down_hbm,
    hb_ref,
    ftab,
    ttab,
    kind,
    out_ref,
    gcol_ref,
    grad_hbm,
    small_ref,
    weight,
    down,
    grads,
    keep_a,
    keep_b,
    hin,
    gin,
    leave,
    nrm,
    work,
    xsend,
    xrecv0,
    xrecv1,
    blocks,
    bias_early,
    bias_late,
    mask_add,
    load_sem,
    w_send,
    w_recv,
    h_send,
    h_recv,
    g_send,
    g_recv,
    x_send,
    x_recv,
    o_send,
    o_recv,
):
    n, across, repeat, slots, chunks, width, wide, depth = cfg
    section = lax.axis_index("section")
    me = lax.axis_index("dp")
    core = lax.rem(me, 2)
    sibling = me + 1 - 2 * core
    is_attn = lax.rem(section, 2) == 0
    xrecv = (xrecv0, xrecv1)
    half = wide // 2
    part = half // 2
    quarter = width // SECTIONS

    load_w = pltpu.make_async_copy(w_hbm, weight, load_sem.at[0])
    load_d = pltpu.make_async_copy(down_hbm, down.at[pl.ds(half, half)], load_sem.at[1])
    load_t = pltpu.make_async_copy(tok_hbm, hin, load_sem.at[2])
    load_c = pltpu.make_async_copy(cot_hbm, gin, load_sem.at[3])

    @pl.when(section == 0)
    def _():
        load_t.start()

    load_w.start()

    @pl.when(section == 3)
    def _():
        load_c.start()

    @pl.when(jnp.logical_not(is_attn))
    def _():
        load_d.start()

    barrier = pltpu.get_barrier_semaphore()

    def greet(s, d):
        pl.semaphore_signal(barrier, inc=1, device_id=(s, d), device_id_type=MESH)

    @pl.when(section == 0)
    def _():
        greet(1, me)
        greet(3, me)
        pl.semaphore_wait(barrier, 2)

    @pl.when(section == 1)
    def _():
        greet(0, me)
        greet(1, sibling)
        greet(3, me)

        @pl.loop(0, n)
        def _(d):
            greet(2, d)

        pl.semaphore_wait(barrier, 3 + n)

    @pl.when(section == 2)
    def _():
        greet(3, me)

        @pl.loop(0, n)
        def _(d):
            greet(1, d)

        pl.semaphore_wait(barrier, 1 + n)

    @pl.when(section == 3)
    def _():
        greet(0, me)
        greet(1, me)
        greet(2, me)
        greet(3, sibling)
        pl.semaphore_wait(barrier, 4)

    bias_late[...] = hb_ref[...].astype(F32)
    own_part = pl.ds(core * part, part)
    other_part = pl.ds((1 - core) * part, part)
    send_down = remote(
        down_hbm.at[own_part], down.at[own_part], w_send.at[0], w_recv.at[0], section + 1, me
    )
    send_bias = remote(
        bias_late, bias_early, w_send.at[1], w_recv.at[1], section + 1, me
    )
    pass_down = remote(
        down.at[own_part], down.at[own_part], w_send.at[0], w_recv.at[2], section, sibling
    )

    gain = gain_ref[...].astype(F32)
    shift = shift_ref[...].astype(F32)
    bias = bias_ref[...].astype(F32)
    small_ref[...] = jnp.zeros_like(small_ref)

    def clear_grads(count):
        @pl.loop(0, count)
        def _(j):
            grads[j] = jnp.zeros((width, width), F32)

    def role_of(table, micro, device):
        def step(r, found):
            return found + jnp.where(table[micro, r] == device, r, 0)

        return lax.fori_loop(0, n, step, 0)

    def send_blocks(c, rows, table, to_section, forward):
        blocks[...] = rows.reshape(blocks.shape)
        micro = lax.div(c, slots)
        slot = lax.rem(c, depth)

        @pl.when(c >= depth)
        def _():
            remote(
                xsend.at[slot], xsend.at[slot], x_send.at[c - depth], x_recv.at[0], to_section, me
            ).wait_send()

        @pl.loop(0, n)
        def _(d):
            spot = lax.rem(role_of(table, micro, d), across)
            for g in range(repeat):
                block = g * across + spot if forward else spot * repeat + g
                xsend[slot, d, g] = blocks[block]

        for m in range(2):

            @pl.when(micro == m)
            def _():
                @pl.loop(0, n)
                def _(d):
                    remote(
                        xsend.at[slot, d],
                        xrecv[m].at[lax.rem(c, slots), me],
                        x_send.at[c],
                        x_recv.at[m],
                        to_section,
                        d,
                    ).start()

    def gather_blocks(c, own_table, their_table, target, from_section, forward):
        for m in range(2):

            @pl.when(c == m * slots)
            def _():
                remote(xrecv[m], xrecv[m], x_send.at[0], x_recv.at[m], from_section, me).wait_recv()
                family = lax.rem(lax.div(role_of(own_table, m, me), across), n // across)

                @pl.loop(0, slots)
                def _(s):
                    group, inner = lax.div(s, repeat), lax.rem(s, repeat)

                    @pl.loop(0, across)
                    def _(r):
                        source = their_table[m, family * across + r]
                        for f in range(repeat):
                            block = r * repeat + f if forward else f * across + r
                            rows = pl.ds(pl.multiple_of(block * BLOCK, BLOCK), BLOCK)
                            target[m * slots + s, rows] = xrecv[m][
                                group * repeat + f, source, inner
                            ]

    def norm_back(c, dn, gb):
        nh, inverse = normalise(hin[c].astype(F32))
        weighted = dn * gain
        first = jnp.mean(weighted, axis=-1, keepdims=True)
        second = jnp.mean(weighted * nh, axis=-1, keepdims=True)
        grad = gb.astype(F32) + inverse * (weighted - first - nh * second)
        small_ref[0:1] += jnp.sum(dn * nh, axis=0, keepdims=True)
        small_ref[1:2] += jnp.sum(dn, axis=0, keepdims=True)
        small_ref[2:3] += jnp.sum(gb.astype(F32), axis=0, keepdims=True)
        return grad

    @pl.when(is_attn)
    def _():
        send_down.start()
        send_bias.start()
        load_w.wait()

        @pl.when(section == 0)
        def _():
            load_t.wait()

        lane = lax.broadcasted_iota(jnp.int32, (1, 2 * HEAD_DIM), 1)
        first_head = jnp.where(lane < HEAD_DIM, 1.0, 0.0)
        pick = [first_head.astype(BF16), (1.0 - first_head).astype(BF16)]
        scale = HEAD_DIM ** (-0.5)
        pick_scaled = [
            (first_head * scale).astype(BF16),
            ((1.0 - first_head) * scale).astype(BF16),
        ]
        key_window = lax.broadcasted_iota(jnp.int32, (WINDOW, WINDOW), 0) % 16 // 4
        query_window = lax.broadcasted_iota(jnp.int32, (WINDOW, WINDOW), 1) % 16 // 4
        barred = jnp.where(key_window == query_window, 0.0, NEGATIVE)
        for m in range(2):
            mask_add[m] = barred * kind[m].astype(F32)

        def forward(c):
            @pl.when(section == 2)
            def _():
                gather_blocks(c, ttab, ftab, hin, 1, True)

            micro = lax.div(c, slots)
            hidden = hin[c].astype(F32)
            nh, _ = normalise(hidden)
            normed = (nh * gain + shift).astype(BF16)
            nrm[c] = normed
            for j in range(3):
                columns = pl.ds(j * width, width)
                keep_b[c, :, columns] = mm(normed, weight[:, columns]).astype(BF16)

            @pl.loop(0, width // (2 * HEAD_DIM))
            def _(pair):
                offset = pl.multiple_of(pair * 2 * HEAD_DIM, 2 * HEAD_DIM)
                q = keep_b[c, :, pl.ds(offset, 2 * HEAD_DIM)]
                k = keep_b[c, :, pl.ds(width + offset, 2 * HEAD_DIM)]
                v = keep_b[c, :, pl.ds(2 * width + offset, 2 * HEAD_DIM)]
                o = None
                for one in range(2):
                    z = mm_nt(k, q * pick_scaled[one]) + mask_add[micro]
                    top = jnp.max(z, axis=0, keepdims=True)
                    e = jnp.exp(z - top)
                    p = e * (1.0 / jnp.sum(e, axis=0, keepdims=True))
                    pb = p.astype(BF16)
                    spot = pl.multiple_of((2 * pair + one) * WINDOW, WINDOW)
                    keep_a[c, :, pl.ds(spot, WINDOW)] = pb
                    term = mm_tn(pb, v * pick[one])
                    o = term if o is None else o + term
                keep_b[c, :, pl.ds(3 * width + offset, 2 * HEAD_DIM)] = o.astype(BF16)

            branch = mm(keep_b[c, :, pl.ds(3 * width, width)], weight[:, pl.ds(3 * width, width)])
            leave[c] = (hin[c].astype(F32) + branch + bias).astype(BF16)
            remote(
                leave.at[c], hin.at[c], h_send.at[c], h_recv.at[c], section + 1, me
            ).start()

        def backward(c):
            @pl.when(c == 0)
            def _():
                clear_grads(4)

            remote(gin.at[c], gin.at[c], g_send.at[c], g_recv.at[c], section + 1, me).wait_recv()
            remote(
                leave.at[c], hin.at[c], h_send.at[c], h_recv.at[c], section + 1, me
            ).wait_send()
            gb = gin[c]
            work[...] = mm_nt(gb, weight[:, pl.ds(3 * width, width)]).astype(BF16)

            @pl.loop(0, width // (2 * HEAD_DIM))
            def _(pair):
                offset = pl.multiple_of(pair * 2 * HEAD_DIM, 2 * HEAD_DIM)
                q_at = pl.ds(offset, 2 * HEAD_DIM)
                k_at = pl.ds(width + offset, 2 * HEAD_DIM)
                v_at = pl.ds(2 * width + offset, 2 * HEAD_DIM)
                q, k, v = keep_b[c, :, q_at], keep_b[c, :, k_at], keep_b[c, :, v_at]
                go = work[:, q_at]
                dq = dk = dv = None
                for one in range(2):
                    spot = pl.multiple_of((2 * pair + one) * WINDOW, WINDOW)
                    pb = keep_a[c, :, pl.ds(spot, WINDOW)]
                    p = pb.astype(F32)
                    dp = mm_nt(v, go * pick[one])
                    pdp = p * dp
                    ds = (pdp - p * jnp.sum(pdp, axis=0, keepdims=True)).astype(BF16)
                    tv = mm(pb, go * pick[one])
                    tk = mm(ds, q * pick_scaled[one])
                    tq = mm_tn(ds, k * pick_scaled[one])
                    dv = tv if dv is None else dv + tv
                    dk = tk if dk is None else dk + tk
                    dq = tq if dq is None else dq + tq
                keep_b[c, :, q_at] = dq.astype(BF16)
                keep_b[c, :, k_at] = dk.astype(BF16)
                keep_b[c, :, v_at] = dv.astype(BF16)

            dn = mm_nt(keep_b[c, :, pl.ds(0, 3 * width)], weight[:, pl.ds(0, 3 * width)])
            leaving = norm_back(c, dn, gb).astype(BF16)

            @pl.when(section == 2)
            def _():
                send_blocks(c, leaving, ftab, 1, False)

            @pl.when(section == 0)
            def _():
                for s in range(SECTIONS):
                    gcol_ref[s, c] = leaving[:, s * quarter : (s + 1) * quarter]

            normed = nrm[c]
            for j in range(3):
                grads[j] += mm_tn(normed, keep_b[c, :, pl.ds(j * width, width)])
            grads[3] += mm_tn(keep_b[c, :, pl.ds(3 * width, width)], gin[c])

        @pl.loop(0, 2 * chunks)
        def _(step):
            c = lax.rem(step, chunks)

            @pl.when(step < chunks)
            def _():
                forward(c)

            @pl.when(step >= chunks)
            def _():
                backward(c)

    @pl.when(jnp.logical_not(is_attn))
    def _():
        early = remote(
            down_hbm.at[own_part], down.at[own_part], w_send.at[0], w_recv.at[0], section - 1, me
        )
        early_bias = remote(
            bias_late, bias_early, w_send.at[1], w_recv.at[1], section - 1, me
        )
        other = remote(
            down.at[other_part], down.at[other_part], w_send.at[0], w_recv.at[2], section, sibling
        )
        load_w.wait()
        early_bias.wait_recv()

        @pl.when(section == 3)
        def _():
            load_c.wait()
            clear_grads(8)

        def forward(c):
            remote(hin.at[c], hin.at[c], h_send.at[c], h_recv.at[c], section - 1, me).wait_recv()
            hidden = hin[c].astype(F32)
            nh, _ = normalise(hidden)
            normed = (nh * gain + shift).astype(BF16)
            nrm[c] = normed
            for j in range(4):
                columns = pl.ds(j * width, width)
                u = mm(normed, weight[:, columns])
                u = u + (bias_early, bias_late)[j // 2][:, pl.ds((j % 2) * width, width)]
                active, slope = gelu_and_slope(u)
                keep_a[c, :, columns] = active.astype(BF16)
                keep_b[c, :, columns] = slope.astype(BF16)

            @pl.when(c == 0)
            def _():
                early.wait_recv()
                pass_down.start()
                load_d.wait()
                other.wait_recv()

            branch = mm(keep_a[c], down[...])
            leaving = (hin[c].astype(F32) + branch + bias).astype(BF16)

            @pl.when(section == 1)
            def _():
                send_blocks(c, leaving, ttab, 2, True)

            @pl.when(section == 3)
            def _():
                for s in range(SECTIONS - 1):
                    gcol_ref[s, c] = leaving[:, s * quarter : (s + 1) * quarter]
                out_ref[c] = leaving[:, (SECTIONS - 1) * quarter :]
                for s in range(SECTIONS - 1):
                    remote(
                        gcol_ref.at[s, c], out_ref.at[c], o_send.at[s, c], o_recv.at[0], s, me
                    ).start()

        def backward(c):
            @pl.when(section == 1)
            def _():
                @pl.when(c == 0)
                def _():
                    clear_grads(8)

                gather_blocks(c, ftab, ttab, gin, 2, False)

            gb = gin[c]
            for j in range(4):
                columns = pl.ds(j * width, width)
                da = mm_nt(gb, down[columns])
                du = da * keep_b[c, :, columns].astype(F32)
                keep_b[c, :, columns] = du.astype(BF16)
                small_ref[3 + j : 4 + j] += jnp.sum(du, axis=0, keepdims=True)
            dn = mm_nt(keep_b[c], weight[...])
            leave[c] = norm_back(c, dn, gb).astype(BF16)
            remote(
                leave.at[c], gin.at[c], g_send.at[c], g_recv.at[c], section - 1, me
            ).start()
            normed = nrm[c]
            for j in range(4):
                columns = pl.ds(j * width, width)
                grads[j] += mm_tn(normed, keep_b[c, :, columns])
                grads[4 + j] += mm_tn(keep_a[c, :, columns], gin[c])

        @pl.loop(0, 2 * chunks)
        def _(step):
            last = lax.div(section, 2)
            c = last * lax.div(step, 2) + (1 - last) * lax.rem(step, chunks)
            back = last * lax.rem(step, 2) + (1 - last) * lax.div(step, chunks)

            @pl.when(back == 0)
            def _():
                forward(c)

            @pl.when(back == 1)
            def _():
                backward(c)

    @pl.when(is_attn)
    def _():
        send_down.wait_send()
        send_bias.wait_send()

    @pl.when(jnp.logical_not(is_attn))
    def _():
        pass_down.wait_send()

    stores = []
    for j in range(4):
        weight[:, pl.ds(j * width, width)] = grads[j].astype(BF16)
    for j in range(4):
        columns = pl.ds(j * width, width)
        store = pltpu.make_async_copy(
            weight.at[:, columns], grad_hbm.at[columns], load_sem.at[j]
        )
        store.start()
        stores.append(store)

    @pl.when(jnp.logical_not(is_attn))
    def _():
        more = []
        for j in range(4):
            rows = pl.ds(j * width, width)
            down[rows] = grads[4 + j].astype(BF16)
            store = pltpu.make_async_copy(
                down.at[rows], grad_hbm.at[pl.ds((4 + j) * width, width)], load_sem.at[4 + j]
            )
            store.start()
            more.append(store)
        for store in more:
            store.wait()

        @pl.loop(0, chunks)
        def _(c):
            remote(
                leave.at[c], gin.at[c], g_send.at[c], g_recv.at[c], section - 1, me
            ).wait_send()

    for store in stores:
        store.wait()

    @pl.when((section == 1) | (section == 2))
    def _():
        @pl.loop(chunks - depth, chunks)
        def _(c):
            slot = lax.rem(c, depth)
            remote(
                xsend.at[slot], xsend.at[slot], x_send.at[c], x_recv.at[0], 3 - section, me
            ).wait_send()

    @pl.when(section == 3)
    def _():
        @pl.loop(0, chunks)
        def _(c):
            for s in range(SECTIONS - 1):
                remote(
                    gcol_ref.at[s, c], out_ref.at[c], o_send.at[s, c], o_recv.at[0], s, me
                ).wait_send()

    @pl.when(section != 3)
    def _():
        remote(out_ref, out_ref, o_send.at[0, 0], o_recv.at[0], 3, me).wait_recv()


def pipeline(tokens, cotangent, gain, shift, weight, bias, down, hidden_bias, ftab, ttab, kind):
    micro, rows, width = tokens.shape
    wide = weight.shape[1]
    n = lax.axis_size("dp")
    across = min(n, 16)
    repeat = 16 // across
    slots = rows // WINDOW
    chunks = micro * slots
    quarter = width // SECTIONS
    depth = chunks if n <= 8 else slots
    cfg = (n, across, repeat, slots, chunks, width, wide, depth)
    vmem = pl.BlockSpec(memory_space=pltpu.VMEM)
    smem = pl.BlockSpec(memory_space=pltpu.SMEM)
    anywhere = pl.BlockSpec(memory_space=pl.ANY)
    dma = pltpu.SemaphoreType.DMA
    chunked = (chunks, WINDOW, width)
    return pl.pallas_call(
        functools.partial(main_kernel, cfg),
        out_shape=(
            jax.ShapeDtypeStruct((chunks, WINDOW, quarter), BF16),
            jax.ShapeDtypeStruct((SECTIONS, chunks, WINDOW, quarter), BF16),
            jax.ShapeDtypeStruct((8 * width, width), BF16),
            jax.ShapeDtypeStruct((8, width), F32),
        ),
        in_specs=[anywhere, anywhere, vmem, vmem, anywhere, vmem, anywhere, vmem, smem, smem, smem],
        out_specs=(vmem, vmem, anywhere, vmem),
        scratch_shapes=[
            pltpu.VMEM((width, wide), BF16),
            pltpu.VMEM((wide, width), BF16),
            pltpu.VMEM((8, width, width), F32),
            pltpu.VMEM((chunks, WINDOW, wide), BF16),
            pltpu.VMEM((chunks, WINDOW, wide), BF16),
            pltpu.VMEM(chunked, BF16),
            pltpu.VMEM(chunked, BF16),
            pltpu.VMEM(chunked, BF16),
            pltpu.VMEM(chunked, BF16),
            pltpu.VMEM((WINDOW, width), BF16),
            pltpu.VMEM((depth, n, repeat, BLOCK, width), BF16),
            pltpu.VMEM((slots, n, repeat, BLOCK, width), BF16),
            pltpu.VMEM((slots, n, repeat, BLOCK, width), BF16),
            pltpu.VMEM((WINDOW // BLOCK, BLOCK, width), BF16),
            pltpu.VMEM((1, wide // 2), F32),
            pltpu.VMEM((1, wide // 2), F32),
            pltpu.VMEM((2, WINDOW, WINDOW), F32),
            dma((8,)),
            dma((2,)),
            dma((3,)),
            dma((chunks,)),
            dma((chunks,)),
            dma((chunks,)),
            dma((chunks,)),
            dma((chunks,)),
            dma((micro,)),
            dma((SECTIONS - 1, chunks)),
            dma((1,)),
        ],
        compiler_params=pltpu.CompilerParams(
            collective_id=0, has_side_effects=True, vmem_limit_bytes=62 * 1024 * 1024
        ),
        name="pipeline",
    )(
        tokens.reshape(chunked),
        cotangent.reshape(chunked),
        gain,
        shift,
        weight,
        bias,
        down,
        hidden_bias.reshape(1, -1),
        ftab,
        ttab,
        kind,
    )


def reduce_kernel(
    cfg,
    grad_hbm,
    small_in,
    gcol_hbm,
    total_hbm,
    small_out,
    ig_ref,
    mine,
    theirs,
    from_low,
    from_high,
    acc,
    small_all,
    small_pair,
    load_sem,
    sib_send,
    sib_recv,
    up_send,
    low_recv,
    down_send,
    high_recv,
    left_send,
    right_send,
    total_recv,
    pair_send,
    pair_recv,
    local_sem,
    x_send,
    x_recv,
    small_send,
    small_recv,
    spair_send,
    spair_recv,
    ig_send,
    ig_recv,
    x_ready,
):
    n, chunk, w_chunks, d_chunks, lag, begin = cfg
    section = lax.axis_index("section")
    me = lax.axis_index("dp")
    core = lax.rem(me, 2)
    place = lax.div(me, 2)
    places = n // 2
    sibling = me + 1 - 2 * core
    is_attn = lax.rem(section, 2) == 0
    not_attn = jnp.logical_not(is_attn)
    partner = section + 1 - 2 * lax.rem(section, 2)
    lines = w_chunks + d_chunks
    half_w = w_chunks * chunk
    half_d = d_chunks * chunk

    def pieces(of_core):
        return (
            grad_hbm.at[pl.ds(of_core * half_w, half_w)],
            grad_hbm.at[pl.ds(2 * half_w + 2 * half_d + of_core * half_d, half_d)],
            grad_hbm.at[pl.ds(2 * half_w + of_core * half_d, half_d)],
        )

    spans = ((0, w_chunks), (w_chunks, d_chunks), (lines, d_chunks))
    loads = [
        pltpu.make_async_copy(
            piece, mine.at[pl.ds(first * chunk, count * chunk)], load_sem.at[at]
        )
        for at, (piece, (first, count)) in enumerate(zip(pieces(core), spans))
    ]

    loads[0].start()

    @pl.when(not_attn)
    def _():
        loads[1].start()
        loads[2].start()

    barrier = pltpu.get_barrier_semaphore()

    def greet(s, d):
        pl.semaphore_signal(barrier, inc=1, device_id=(s, d), device_id_type=MESH)

    @pl.loop(0, n)
    def _(d):
        @pl.when(d != me)
        def _():
            greet(section, d)

    @pl.when(section != 0)
    def _():
        greet(0, me)

    @pl.when(section == 3)
    def _():
        greet(2, me)

    pl.semaphore_wait(
        barrier, n - 1 + jnp.where(section == 0, 3, jnp.where(section == 2, 1, 0))
    )

    @pl.when(is_attn)
    def _():
        pl.semaphore_signal(x_ready, inc=1, device_id=(partner, me), device_id_type=MESH)

    def rows(i):
        return pl.ds(pl.multiple_of(i * chunk, chunk), chunk)

    def sib_copy(i, source_row):
        return remote(
            grad_hbm.at[pl.ds(pl.multiple_of(source_row, chunk), chunk)],
            theirs.at[rows(i)],
            sib_send.at[i],
            sib_recv.at[i],
            section,
            sibling,
        )

    def sib_row(i):
        from_w = (1 - core) * half_w + i * chunk
        late = 2 * half_w + 2 * half_d + (1 - core) * half_d + (i - w_chunks) * chunk
        early = 2 * half_w + (1 - core) * half_d + (i - lines) * chunk
        return jnp.where(i < w_chunks, from_w, jnp.where(i < lines, late, early))

    sib_count = jnp.where(is_attn, w_chunks, lines + d_chunks)

    @pl.loop(0, lines + d_chunks)
    def _(i):
        @pl.when(i < sib_count)
        def _():
            sib_copy(i, sib_row(i)).start()

    small_all[me] = small_in[...]

    def small_copy(d):
        return remote(
            small_in, small_all.at[me], small_send.at[d], small_recv.at[0], section, d
        )

    @pl.loop(0, n)
    def _(d):
        @pl.when(d != me)
        def _():
            small_copy(d).start()

    def ig_copy(s):
        return remote(gcol_hbm.at[s], ig_ref, ig_send.at[s], ig_recv.at[0], s, me)

    ig_own = pltpu.make_async_copy(gcol_hbm.at[0], ig_ref, ig_send.at[0])

    @pl.when(section == 0)
    def _():
        ig_own.start()
        for s in range(1, SECTIONS):
            ig_copy(s).start()

    def root_of(i):
        return places // 2 - 1 + lax.rem(i, 2)

    def total_rows(i):
        return total_hbm.at[core, rows(i)]

    def up_copy(i):
        return remote(
            mine.at[rows(i)], from_low.at[rows(i)], up_send.at[i], low_recv.at[i], section, me + 2
        )

    def down_copy(i):
        return remote(
            mine.at[rows(i)],
            from_high.at[rows(i)],
            down_send.at[i],
            high_recv.at[i],
            section,
            me - 2,
        )

    def left_copy(i, source):
        return remote(
            source, total_rows(i), left_send.at[i], total_recv.at[i], section, me - 2
        )

    def right_copy(i, source):
        return remote(
            source, total_rows(i), right_send.at[i], total_recv.at[i], section, me + 2
        )

    def pair_copy(i, source):
        return remote(
            source, total_rows(i), pair_send.at[i], pair_recv.at[0], section, sibling
        )

    def own_copy(i):
        return pltpu.make_async_copy(mine.at[rows(i)], total_rows(i), local_sem.at[i])

    def x_copy(e):
        return remote(
            mine.at[rows(lines + e)],
            mine.at[rows(w_chunks + e)],
            x_send.at[e],
            x_recv.at[e],
            partner,
            me,
        )

    def reduce_stage(i, root):
        summed = is_attn & (i >= w_chunks)

        @pl.when(summed)
        def _():
            x_copy(i - w_chunks).wait_recv()
            acc[...] = mine[rows(i)].astype(F32)

        @pl.when(jnp.logical_not(summed))
        def _():
            sib_copy(i, 0).wait_recv()
            acc[...] = mine[rows(i)].astype(F32) + theirs[rows(i)].astype(F32)

        @pl.when((place <= root) & (place > 0))
        def _():
            up_copy(i).wait_recv()
            acc[...] += from_low[rows(i)].astype(F32)

        @pl.when((place >= root) & (place < places - 1))
        def _():
            down_copy(i).wait_recv()
            acc[...] += from_high[rows(i)].astype(F32)

        mine[rows(i)] = acc[...].astype(BF16)

        @pl.when(place < root)
        def _():
            up_copy(i).start()

        @pl.when(place > root)
        def _():
            down_copy(i).start()

        @pl.when(place == root)
        def _():
            source = mine.at[rows(i)]

            @pl.when(place > 0)
            def _():
                left_copy(i, source).start()

            @pl.when(place < places - 1)
            def _():
                right_copy(i, source).start()

            pair_copy(i, source).start()
            own_copy(i).start()

    def early_stage(e):
        @pl.when(e == 0)
        def _():
            loads[2].wait()
            pl.semaphore_wait(x_ready, 1)

        sib_copy(lines + e, 0).wait_recv()
        here = rows(lines + e)
        mine[here] = (mine[here].astype(F32) + theirs[here].astype(F32)).astype(BF16)
        x_copy(e).start()

    def spread_stage(i, root):
        @pl.when(place != root)
        def _():
            left_copy(i, total_rows(i)).wait_recv()

            @pl.when((place < root) & (place > 0))
            def _():
                left_copy(i, total_rows(i)).start()

            @pl.when((place > root) & (place < places - 1))
            def _():
                right_copy(i, total_rows(i)).start()

            pair_copy(i, total_rows(i)).start()

    loads[0].wait()

    @pl.when(not_attn)
    def _():
        loads[1].wait()

    height = places // 2
    pairs = lines // 2

    @pl.loop(0, pairs + 2 * height * lag)
    def _(step):
        @pl.when(not_attn & (step >= begin) & (step < begin + d_chunks // 2))
        def _():
            for stream in range(2):
                early_stage(2 * (step - begin) + stream)

        for stream in range(2):
            root = height - 1 + stream
            now = step - lag * (height - jnp.abs(place - root))

            @pl.when((now >= 0) & (now < pairs))
            def _():
                reduce_stage(2 * now + stream, root)

        for stream in range(2):
            root = height - 1 + stream
            past = step - lag * (height + jnp.abs(place - root))

            @pl.when((past >= 0) & (past < pairs))
            def _():
                spread_stage(2 * past + stream, root)

    remote(
        small_all.at[pl.ds(0, n - 1)],
        small_all.at[pl.ds(0, n - 1)],
        small_send.at[0],
        small_recv.at[0],
        section,
        sibling,
    ).wait_recv()

    def add(d, so_far):
        return so_far + small_all[d]

    small_out[...] = lax.fori_loop(1, n, add, small_all[0])
    to_pair = remote(
        small_out, small_pair, spair_send.at[0], spair_recv.at[0], partner, me
    )

    @pl.when(not_attn)
    def _():
        to_pair.start()
        to_pair.wait_send()

    @pl.when(is_attn)
    def _():
        to_pair.wait_recv()
        small_out[5:7] = small_pair[3:5]

    @pl.loop(0, lines)
    def _(i):
        root = root_of(i)

        @pl.when(place < root)
        def _():
            up_copy(i).wait_send()

        @pl.when(place > root)
        def _():
            down_copy(i).wait_send()

        @pl.when((place <= root) & (place > 0))
        def _():
            left_copy(i, total_rows(i)).wait_send()

        @pl.when((place >= root) & (place < places - 1))
        def _():
            right_copy(i, total_rows(i)).wait_send()

        pair_copy(i, total_rows(i)).wait_send()

        @pl.when(place == root)
        def _():
            own_copy(i).wait()

    @pl.loop(0, lines + d_chunks)
    def _(i):
        @pl.when(i < sib_count)
        def _():
            sib_copy(i, 0).wait_send()

    @pl.when(not_attn)
    def _():
        @pl.loop(0, d_chunks)
        def _(e):
            x_copy(e).wait_send()

    @pl.loop(0, n)
    def _(d):
        @pl.when(d != me)
        def _():
            small_copy(d).wait_send()

    @pl.when(section == 0)
    def _():
        ig_own.wait()
        for s in range(1, SECTIONS):
            ig_copy(s).wait_send()

    @pl.when(section != 0)
    def _():
        ig_copy(0).wait_recv()

    remote(
        total_hbm.at[1 - core],
        total_hbm.at[1 - core],
        pair_send.at[0],
        pair_recv.at[0],
        section,
        sibling,
    ).wait_recv()


def reduction(grads, small, gcol, chunk=96, lag=1):
    width = grads.shape[1]
    half_w = 2 * width
    half_d = width
    n = lax.axis_size("dp")
    w_chunks, d_chunks = half_w // chunk, half_d // chunk
    lines = w_chunks + d_chunks
    cfg = (n, chunk, w_chunks, d_chunks, lag, d_chunks // 2)
    vmem = pl.BlockSpec(memory_space=pltpu.VMEM)
    anywhere = pl.BlockSpec(memory_space=pl.ANY)
    dma = pltpu.SemaphoreType.DMA
    every = lines + d_chunks
    return pl.pallas_call(
        functools.partial(reduce_kernel, cfg),
        out_shape=(
            jax.ShapeDtypeStruct((2, half_w + half_d, width), BF16),
            jax.ShapeDtypeStruct((8, width), F32),
            jax.ShapeDtypeStruct(gcol.shape[1:], BF16),
        ),
        in_specs=[anywhere, vmem, anywhere],
        out_specs=(anywhere, vmem, vmem),
        scratch_shapes=[
            pltpu.VMEM((every * chunk, width), BF16),
            pltpu.VMEM((every * chunk, width), BF16),
            pltpu.VMEM((lines * chunk, width), BF16),
            pltpu.VMEM((lines * chunk, width), BF16),
            pltpu.VMEM((chunk, width), F32),
            pltpu.VMEM((n, 8, width), F32),
            pltpu.VMEM((8, width), F32),
            dma((3,)),
            dma((every,)),
            dma((every,)),
            dma((lines,)),
            dma((lines,)),
            dma((lines,)),
            dma((lines,)),
            dma((lines,)),
            dma((lines,)),
            dma((lines,)),
            dma((lines,)),
            dma((1,)),
            dma((lines,)),
            dma((d_chunks,)),
            dma((d_chunks,)),
            dma((n,)),
            dma((1,)),
            dma((1,)),
            dma((1,)),
            dma((SECTIONS,)),
            dma((1,)),
            pltpu.SemaphoreType.REGULAR,
        ],
        compiler_params=pltpu.CompilerParams(
            collective_id=1, has_side_effects=True, vmem_limit_bytes=40 * 1024 * 1024
        ),
        name="reduction",
    )(grads, small, gcol)


def finish_kernel(
    total_ref,
    small_ref,
    ig_ref,
    out_ref,
    output,
    input_grad,
    gain,
    shift,
    weight,
    bias,
    down,
    hidden,
):
    block, row = pl.program_id(0), pl.program_id(1)

    @pl.when((block == 0) & (row == 0))
    def _():
        output[...] = out_ref[...]
        input_grad[...] = ig_ref[...].astype(F32)
        gain[...] = small_ref[0:1]
        shift[...] = small_ref[1:2]
        bias[...] = small_ref[2:3]
        hidden[...] = small_ref[5:7]

    is_down = block % 3 == 2

    @pl.when(jnp.logical_not(is_down))
    def _():
        weight[...] = total_ref[0].astype(F32)

    @pl.when(is_down)
    def _():
        down[...] = total_ref[0].astype(F32)


def finish(total, small, input_grad, output):
    width = total.shape[-1]
    steps = 2
    span = width // steps

    def whole(array):
        return pl.BlockSpec(array.shape, lambda b, r, k=array.ndim: (0,) * k)

    def weight_at(b, r):
        half, inner = b // 3, b % 3
        return jnp.where(inner == 2, steps - 1, r), 2 * half + jnp.minimum(inner, 1)

    def down_at(b, r):
        half, inner = b // 3, b % 3
        earlier = jnp.where(half == 0, 0, steps - 1)
        return jnp.where(inner == 2, steps * half + r, earlier), 0

    row = jax.ShapeDtypeStruct((1, width), F32)
    pair = jax.ShapeDtypeStruct((2, width), F32)
    wide_grad = jax.ShapeDtypeStruct(input_grad.shape, F32)
    return pl.pallas_call(
        finish_kernel,
        grid=(6, steps),
        out_shape=(
            output,
            wide_grad,
            row,
            row,
            jax.ShapeDtypeStruct((width, SECTIONS * width), F32),
            row,
            jax.ShapeDtypeStruct((2 * width, width), F32),
            pair,
        ),
        in_specs=[
            pl.BlockSpec((1, span, width), lambda b, r: (b, r, 0)),
            whole(small),
            whole(input_grad),
            whole(output),
        ],
        out_specs=(
            whole(output),
            whole(wide_grad),
            whole(row),
            whole(row),
            pl.BlockSpec((span, width), weight_at),
            whole(row),
            pl.BlockSpec((span, width), down_at),
            whole(pair),
        ),
        compiler_params=pltpu.CompilerParams(vmem_limit_bytes=32 * 1024 * 1024),
        name="finish",
    )(total.reshape(6, width, width), small, input_grad, output)


def on_device(
    tokens,
    cotangent,
    norm_gain,
    norm_shift,
    in_weight,
    out_bias,
    down_weight,
    hidden_bias,
    frame_device,
    tube_device,
    clip_kind,
):
    micro, rows, width = tokens.shape
    output, gcol, grads, small = pipeline(
        tokens,
        cotangent,
        norm_gain,
        norm_shift,
        in_weight[0],
        out_bias,
        down_weight,
        hidden_bias,
        frame_device,
        tube_device,
        clip_kind,
    )
    total, small_total, input_grad = reduction(grads, small, gcol)
    output, input_grad, gain, shift, weight, bias, down, hidden = finish(
        total, small_total, input_grad, output
    )
    quarter = width // SECTIONS
    return (
        output.reshape(micro, rows, quarter),
        input_grad.reshape(micro, rows, quarter),
        gain,
        shift,
        weight[None],
        bias,
        down,
        hidden.reshape(-1),
    )


def solution(mesh):
    return jax.shard_map(
        on_device,
        mesh=mesh,
        in_specs=(
            P(None, "dp", None),
            P(None, "dp", None),
            P("section", None),
            P("section", None),
            P("section", None, None),
            P("section", None),
            P("section", None),
            P("section"),
            P(),
            P(),
            P(),
        ),
        out_specs=(
            P(None, "dp", "section"),
            P(None, "dp", "section"),
            P("section", None),
            P("section", None),
            P("section", None, None),
            P("section", None),
            P("section", None),
            P("section"),
        ),
        check_vma=False,
    )
```

```python
import functools

import jax
import jax.numpy as jnp
from jax import lax
from jax.experimental import pallas as pl
from jax.experimental.pallas import tpu as pltpu
from jax.sharding import PartitionSpec as P

HEAD_DIM = 64
WINDOW = 256
BLOCK = 16
SECTIONS = 4
EPS = 1e-06
NEGATIVE = -1e30
MESH = pl.DeviceIdType.MESH
F32 = jnp.float32
BF16 = jnp.bfloat16


def mm(left, right):
    return lax.dot_general(left, right, (((1,), (0,)), ((), ())), preferred_element_type=F32)


def mm_nt(left, right):
    return lax.dot_general(left, right, (((1,), (1,)), ((), ())), preferred_element_type=F32)


def mm_tn(left, right):
    return lax.dot_general(left, right, (((0,), (0,)), ((), ())), preferred_element_type=F32)


def remote(src, dst, send_sem, recv_sem, section, dp):
    return pltpu.make_async_remote_copy(
        src_ref=src,
        dst_ref=dst,
        send_sem=send_sem,
        recv_sem=recv_sem,
        device_id=(section, dp),
        device_id_type=MESH,
    )


def normalise(hidden):
    average = jnp.mean(hidden, axis=-1, keepdims=True)
    centred = hidden - average
    inverse = lax.rsqrt(jnp.mean(centred * centred, axis=-1, keepdims=True) + EPS)
    return centred * inverse, inverse


def gelu_and_slope(u):
    cdf = 0.5 + 0.5 * lax.erf(u * 0.7071067811865476)
    bell = jnp.exp(-0.5 * u * u)
    return u * cdf, cdf + (0.3989422804014327 * u) * bell


def main_kernel(
    cfg,
    tok_hbm,
    cot_hbm,
    gain_ref,
    shift_ref,
    w_hbm,
    bias_ref,
    down_hbm,
    hb_ref,
    ftab,
    ttab,
    kind,
    out_ref,
    ig_ref,
    total_hbm,
    small_out,
    weights,
    keep_a,
    keep_b,
    hin,
    gin,
    leave,
    nrm,
    work,
    gcol,
    xsend,
    xrecv0,
    xrecv1,
    blocks,
    bias_early,
    bias_late,
    mask_add,
    spots,
    sources,
    guest,
    theirs,
    from_low,
    from_high,
    acc,
    small,
    small_all,
    small_pair,
    load_sem,
    w_send,
    w_recv,
    hb_send,
    hb_recv,
    h_send,
    h_recv,
    g_send,
    g_recv,
    x_send,
    x_recv,
    o_send,
    o_recv,
    ig_send,
    ig_recv,
    sib_send,
    sib_recv,
    up_send,
    low_recv,
    down_send,
    high_recv,
    left_send,
    right_send,
    total_recv,
    pair_send,
    pair_recv,
    local_sem,
    early_send,
    early_recv,
    guest_send,
    guest_recv,
    small_send,
    small_recv,
    spair_send,
    spair_recv,
):
    n, across, repeat, slots, chunks, width, wide, depth, chunk, lag, pieces = cfg
    section = lax.axis_index("section")
    me = lax.axis_index("dp")
    core = lax.rem(me, 2)
    place = lax.div(me, 2)
    places = n // 2
    sibling = me + 1 - 2 * core
    odd_place = lax.rem(place, 2)
    across_z = me + 2 - 4 * odd_place
    odd = lax.rem(section, 2)
    is_attn = odd == 0
    not_attn = odd == 1
    partner = section + 1 - 2 * odd
    is_first, is_last = lax.div(3 - section, 3), lax.div(section, 3)
    xrecv = (xrecv0, xrecv1)
    half = wide // 2
    quarter = width // SECTIONS

    def load_columns(j):
        columns = pl.ds(j * width, width)
        return pltpu.make_async_copy(w_hbm.at[:, columns], weights.at[j], load_sem.at[j])

    def load_rows(j):
        rows = pl.ds(j * width, width)
        return pltpu.make_async_copy(down_hbm.at[rows], weights.at[6 + j], load_sem.at[6 + j])

    load_t = pltpu.make_async_copy(tok_hbm, hin, load_sem.at[5])
    load_c = pltpu.make_async_copy(cot_hbm, gin, load_sem.at[5])

    @pl.when(section == 0)
    def _():
        load_t.start()

    for j in range(4):
        load_columns(j).start()

    @pl.when(section == 3)
    def _():
        load_c.start()

    @pl.when(not_attn)
    def _():
        load_rows(0).start()
        load_rows(1).start()

    barrier = pltpu.get_barrier_semaphore()

    def greet(s, d):
        pl.semaphore_signal(barrier, inc=1, device_id=(s, d), device_id_type=MESH)

    @pl.loop(0, n)
    def _(d):
        @pl.when(d != me)
        def _():
            greet(section, d)

        @pl.when((section == 1) | (section == 2))
        def _():
            greet(3 - section, d)

    greet(partner, me)
    greet(3 - partner, me)

    @pl.when((section == 0) | (section == 3))
    def _():
        greet(3 - section, me)

    def meet():
        edge = is_first + is_last
        pl.semaphore_wait(barrier, n + 1 + edge + (1 - edge) * n)

    bias_late[...] = hb_ref[...].astype(F32)
    send_bias = remote(bias_late, bias_early, hb_send.at[0], hb_recv.at[0], partner, me)
    span = half // 4
    step_rows = span // pieces

    def parts(z_side, which_core, k):
        first = which_core * span + k * step_rows
        in_block = pl.ds(pl.multiple_of(first, step_rows), step_rows)
        in_all = pl.ds(pl.multiple_of(z_side * width + first, step_rows), step_rows)
        return down_hbm.at[in_all], weights.at[4 + z_side, in_block]

    def down_first(k):
        source, here = parts(odd_place, core, k)
        return remote(source, here, w_send.at[0, k], w_recv.at[0, k], partner, me)

    def down_along(k):
        here = parts(odd_place, core, k)[1]
        return remote(here, here, w_send.at[1, k], w_recv.at[1, k], section, across_z)

    def down_pair(k):
        here = parts(odd_place, core, k)[1]
        return remote(here, here, w_send.at[2, k], w_recv.at[2, k], section, sibling)

    def down_last(k):
        here = parts(1 - odd_place, core, k)[1]
        return remote(here, here, w_send.at[3, k], w_recv.at[3, k], section, sibling)

    gain = gain_ref[...].astype(F32)
    shift = shift_ref[...].astype(F32)
    bias = bias_ref[...].astype(F32)
    small[...] = jnp.zeros_like(small)

    def role_of(table, micro, device):
        def step(r, found):
            return found + jnp.where(table[micro, r] == device, r, 0)

        return lax.fori_loop(0, n, step, 0)

    def make_tables(send_table, own_table):
        for m in range(2):

            @pl.loop(0, n)
            def _(d):
                spots[m, d] = lax.rem(role_of(send_table, m, d), across)

            family = lax.rem(lax.div(role_of(own_table, m, me), across), n // across)

            @pl.loop(0, across)
            def _(r):
                sources[m, r] = send_table[m, family * across + r]

    def send_blocks(c, rows, to_section, forward):
        blocks[...] = rows.reshape(blocks.shape)
        micro = lax.div(c, slots)
        slot = lax.rem(c, depth)

        @pl.when(c >= depth)
        def _():
            remote(
                xsend.at[slot], xsend.at[slot], x_send.at[c - depth], x_recv.at[0], to_section, me
            ).wait_send()

        @pl.loop(0, n)
        def _(d):
            spot = spots[micro, d]
            for g in range(repeat):
                block = g * across + spot if forward else spot * repeat + g
                xsend[slot, d, g] = blocks[block]

        for m in range(2):

            @pl.when(micro == m)
            def _():
                @pl.loop(0, n)
                def _(d):
                    remote(
                        xsend.at[slot, d],
                        xrecv[m].at[lax.rem(c, slots), me],
                        x_send.at[c],
                        x_recv.at[m],
                        to_section,
                        d,
                    ).start()

    def gather_blocks(c, target, from_section, forward):
        for m in range(2):

            @pl.when(c == m * slots)
            def _():
                remote(xrecv[m], xrecv[m], x_send.at[0], x_recv.at[m], from_section, me).wait_recv()
                @pl.loop(0, slots)
                def _(s):
                    group, inner = lax.div(s, repeat), lax.rem(s, repeat)

                    @pl.loop(0, across)
                    def _(r):
                        source = sources[m, r]
                        for f in range(repeat):
                            block = r * repeat + f if forward else f * across + r
                            rows = pl.ds(pl.multiple_of(block * BLOCK, BLOCK), BLOCK)
                            target[m * slots + s, rows] = xrecv[m][
                                group * repeat + f, source, inner
                            ]

    def norm_back(c, dn, gb):
        nh, inverse = normalise(hin[c].astype(F32))
        weighted = dn * gain
        first = jnp.mean(weighted, axis=-1, keepdims=True)
        second = jnp.mean(weighted * nh, axis=-1, keepdims=True)
        grad = gb.astype(F32) + inverse * (weighted - first - nh * second)
        small[0:1] += jnp.sum(dn * nh, axis=0, keepdims=True)
        small[1:2] += jnp.sum(dn, axis=0, keepdims=True)
        small[2:3] += jnp.sum(gb.astype(F32), axis=0, keepdims=True)
        return grad

    def ig_copy(s, c):
        return remote(gcol.at[s - 1, c], ig_ref.at[c], ig_send.at[s, c], ig_recv.at[0], s, me)

    @pl.when(is_attn)
    def _():
        @pl.when(section == 2)
        def _():
            make_tables(ftab, ttab)

        lane = lax.broadcasted_iota(jnp.int32, (1, 2 * HEAD_DIM), 1)
        first_head = jnp.where(lane < HEAD_DIM, 1.0, 0.0)
        pick = [first_head.astype(BF16), (1.0 - first_head).astype(BF16)]
        scale = HEAD_DIM ** (-0.5)
        pick_scaled = [
            (first_head * scale).astype(BF16),
            ((1.0 - first_head) * scale).astype(BF16),
        ]
        key_window = lax.broadcasted_iota(jnp.int32, (WINDOW, WINDOW), 0) % 16 // 4
        query_window = lax.broadcasted_iota(jnp.int32, (WINDOW, WINDOW), 1) % 16 // 4
        barred = jnp.where(key_window == query_window, 0.0, NEGATIVE)
        for m in range(2):
            mask_add[m] = barred * kind[m].astype(F32)

        def start_down():
            meet()

            @pl.loop(0, pieces)
            def _(k):
                down_first(k).start()

            send_bias.start()

        @pl.when(section == 2)
        def _():
            start_down()

        def forward(c):
            @pl.when(section == 2)
            def _():
                gather_blocks(c, hin, 1, True)

            @pl.when((section == 0) & (c == 0))
            def _():
                load_t.wait()

            micro = lax.div(c, slots)
            hidden = hin[c].astype(F32)
            nh, _ = normalise(hidden)
            normed = (nh * gain + shift).astype(BF16)
            nrm[c] = normed
            for j in range(3):
                columns = pl.ds(j * width, width)

                @pl.when(c == 0)
                def _():
                    load_columns(j).wait()

                keep_b[c, :, columns] = mm(normed, weights[j]).astype(BF16)

            @pl.when(c == 0)
            def _():
                load_columns(3).wait()

                @pl.when(section == 0)
                def _():
                    start_down()


            places_at = [g * 2 * HEAD_DIM for g in range(width // (2 * HEAD_DIM))]
            scores = []
            for offset in places_at:
                q = keep_b[c, :, pl.ds(offset, 2 * HEAD_DIM)]
                k = keep_b[c, :, pl.ds(width + offset, 2 * HEAD_DIM)]
                for one in range(2):
                    scores.append(mm_nt(k, q * pick_scaled[one]))
            probs = []
            for z in scores:
                z = z + mask_add[micro]
                e = jnp.exp(z - jnp.max(z, axis=0, keepdims=True))
                p = e * (1.0 / jnp.sum(e, axis=0, keepdims=True))
                probs.append(p.astype(BF16))
            for g, offset in enumerate(places_at):
                v = keep_b[c, :, pl.ds(2 * width + offset, 2 * HEAD_DIM)]
                o = None
                for one in range(2):
                    pb = probs[2 * g + one]
                    spot = (2 * g + one) * WINDOW
                    keep_a[c, :, pl.ds(spot, WINDOW)] = pb
                    term = mm_tn(pb, v * pick[one])
                    o = term if o is None else o + term
                keep_b[c, :, pl.ds(3 * width + offset, 2 * HEAD_DIM)] = o.astype(BF16)

            branch = mm(keep_b[c, :, pl.ds(3 * width, width)], weights[3])
            leave[c] = (hin[c].astype(F32) + branch + bias).astype(BF16)
            remote(
                leave.at[c], hin.at[c], h_send.at[c], h_recv.at[c], section + 1, me
            ).start()

        def backward(c):
            remote(gin.at[c], gin.at[c], g_send.at[c], g_recv.at[c], section + 1, me).wait_recv()
            remote(
                leave.at[c], hin.at[c], h_send.at[c], h_recv.at[c], section + 1, me
            ).wait_send()
            gb = gin[c]
            work[...] = mm_nt(gb, weights[3]).astype(BF16)

            places_at = [g * 2 * HEAD_DIM for g in range(width // (2 * HEAD_DIM))]
            grads = []
            for offset in places_at:
                v = keep_b[c, :, pl.ds(2 * width + offset, 2 * HEAD_DIM)]
                go = work[:, pl.ds(offset, 2 * HEAD_DIM)]
                for one in range(2):
                    grads.append(mm_nt(v, go * pick[one]))
            for g, offset in enumerate(places_at):
                q_at = pl.ds(offset, 2 * HEAD_DIM)
                k_at = pl.ds(width + offset, 2 * HEAD_DIM)
                v_at = pl.ds(2 * width + offset, 2 * HEAD_DIM)
                q, k, go = keep_b[c, :, q_at], keep_b[c, :, k_at], work[:, q_at]
                dq = dk = dv = None
                for one in range(2):
                    spot = (2 * g + one) * WINDOW
                    pb = keep_a[c, :, pl.ds(spot, WINDOW)]
                    p = pb.astype(F32)
                    pdp = p * grads[2 * g + one]
                    ds = (pdp - p * jnp.sum(pdp, axis=0, keepdims=True)).astype(BF16)
                    tv = mm(pb, go * pick[one])
                    tk = mm(ds, q * pick_scaled[one])
                    tq = mm_tn(ds, k * pick_scaled[one])
                    dv = tv if dv is None else dv + tv
                    dk = tk if dk is None else dk + tk
                    dq = tq if dq is None else dq + tq
                keep_b[c, :, q_at] = dq.astype(BF16)
                keep_b[c, :, k_at] = dk.astype(BF16)
                keep_b[c, :, v_at] = dv.astype(BF16)

            dn = sum(mm_nt(keep_b[c, :, pl.ds(j * width, width)], weights[j]) for j in range(3))
            leaving = norm_back(c, dn, gb).astype(BF16)

            @pl.when(section == 2)
            def _():
                send_blocks(c, leaving, 1, False)

            @pl.when(section == 0)
            def _():
                for s in range(1, SECTIONS):
                    gcol[s - 1, c] = leaving[:, s * quarter : (s + 1) * quarter]
                ig_ref[c] = leaving[:, 0:quarter]
                for s in range(1, SECTIONS):
                    ig_copy(s, c).start()

        @pl.loop(0, 2 * chunks)
        def _(step):
            c = lax.rem(step, chunks)

            @pl.when(step < chunks)
            def _():
                forward(c)

            @pl.when(step >= chunks)
            def _():
                backward(c)

    @pl.when(not_attn)
    def _():
        meet()

        @pl.when(section == 1)
        def _():
            make_tables(ttab, ftab)

        for j in range(4):
            load_columns(j).wait()

        load_rows(0).wait()
        load_rows(1).wait()

        @pl.loop(0, pieces)
        def _(k):
            down_first(k).wait_recv()
            down_along(k).start()
            down_pair(k).start()

        @pl.loop(0, pieces)
        def _(k):
            down_along(k).wait_recv()
            down_last(k).start()

        send_bias.wait_recv()

        @pl.when(section == 3)
        def _():
            load_c.wait()

        def forward(c):
            remote(hin.at[c], hin.at[c], h_send.at[c], h_recv.at[c], section - 1, me).wait_recv()
            hidden = hin[c].astype(F32)
            nh, _ = normalise(hidden)
            normed = (nh * gain + shift).astype(BF16)
            nrm[c] = normed
            for j in range(4):
                columns = pl.ds(j * width, width)
                u = mm(normed, weights[j])
                u = u + (bias_early, bias_late)[j // 2][:, pl.ds((j % 2) * width, width)]
                active, slope = gelu_and_slope(u)
                keep_a[c, :, columns] = active.astype(BF16)
                keep_b[c, :, columns] = slope.astype(BF16)

            @pl.when(c == 0)
            def _():
                @pl.loop(0, pieces)
                def _(k):
                    down_pair(k).wait_recv()
                    down_last(k).wait_recv()

            branch = mm(keep_a[c], weights[pl.ds(4, 4)].reshape(wide, width))
            leaving = (hin[c].astype(F32) + branch + bias).astype(BF16)

            @pl.when(section == 1)
            def _():
                send_blocks(c, leaving, 2, True)

            @pl.when(section == 3)
            def _():
                for s in range(SECTIONS - 1):
                    gcol[s, c] = leaving[:, s * quarter : (s + 1) * quarter]
                out_ref[c] = leaving[:, (SECTIONS - 1) * quarter :]
                for s in range(SECTIONS - 1):
                    remote(
                        gcol.at[s, c], out_ref.at[c], o_send.at[s, c], o_recv.at[0], s, me
                    ).start()

        def backward(c):
            @pl.when(section == 1)
            def _():
                gather_blocks(c, gin, 2, False)

            gb = gin[c]
            for j in range(4):
                columns = pl.ds(j * width, width)
                da = mm_nt(gb, weights[4 + j])
                du = da * keep_b[c, :, columns].astype(F32)
                keep_b[c, :, columns] = du.astype(BF16)
                small[3 + j : 4 + j] += jnp.sum(du, axis=0, keepdims=True)
            dn = sum(mm_nt(keep_b[c, :, pl.ds(j * width, width)], weights[j]) for j in range(4))
            leave[c] = norm_back(c, dn, gb).astype(BF16)
            remote(
                leave.at[c], gin.at[c], g_send.at[c], g_recv.at[c], section - 1, me
            ).start()
        @pl.loop(0, 2 * chunks)
        def _(step):
            last = lax.div(section, 2)
            c = last * lax.div(step, 2) + (1 - last) * lax.rem(step, chunks)
            back = last * lax.rem(step, 2) + (1 - last) * lax.div(step, chunks)

            @pl.when(back == 0)
            def _():
                forward(c)

            @pl.when(back == 1)
            def _():
                backward(c)

    @pl.when(not_attn)
    def _():
        @pl.loop(0, pieces)
        def _(k):
            down_along(k).wait_send()
            down_pair(k).wait_send()
            down_last(k).wait_send()

    side = width // 2
    per_block = side // chunk
    w_chunks, d_chunks = 4 * per_block, 2 * per_block
    rows_all = chunks * WINDOW

    def grad_rows(block, first, count):
        return weights.at[block, pl.ds(pl.multiple_of(first, count), count)]

    def half_rows(block):
        return pl.ds(pl.multiple_of(block * side, side), side)

    def block_of(turn):
        last = turn + 2 * lax.div(turn, 4) - 4 * lax.div(turn, 6)
        first = turn + 3 * lax.div(turn + 7, 8) - 5 * lax.div(turn + 5, 8) + 2 * lax.div(turn, 6)
        second = odd - is_last
        return second * first + (1 - second) * last

    def sib_copy(block, source):
        return remote(
            source, theirs.at[half_rows(block)], sib_send.at[block], sib_recv.at[block], section, sibling
        )

    def outer(left, left_at, right, right_at, block):
        right_value = right[:, :, right_at].reshape(rows_all, width)

        @pl.loop(0, width // WINDOW)
        def _(k):
            columns = pl.ds(pl.multiple_of(left_at + k * WINDOW, WINDOW), WINDOW)
            left_value = left[:, :, columns].reshape(rows_all, WINDOW)
            rows = pl.ds(pl.multiple_of(k * WINDOW, WINDOW), WINDOW)
            weights[block, rows] = mm_tn(left_value, right_value).astype(BF16)

    def grad_block(turn):
        block = block_of(turn)

        @pl.when((block < 4) & (not_attn | (block < 3)))
        def _():
            columns = pl.ds(pl.multiple_of(block * width, width), width)
            outer(nrm, 0, keep_b, columns, block)

        @pl.when((block == 3) & is_attn)
        def _():
            outer(keep_b, 3 * width, gin, pl.ds(0, width), block)

        @pl.when(block >= 4)
        def _():
            outer(keep_a, (block - 4) * width, gin, pl.ds(0, width), block)

        sib_copy(block, grad_rows(block, (1 - core) * side, side)).start()

    def early_copy(block, source):
        send, recv = early_send.at[block - 4], early_recv.at[block - 4]
        return (
            remote(source, grad_rows(block, core * side, side), send, recv, 2, me),
            remote(source, guest.at[half_rows(block - 4)], send, recv, 3, me),
        )

    def pair_sum(turn):
        block = block_of(turn)
        sib_copy(block, theirs.at[half_rows(block)]).wait_recv()

        here = grad_rows(block, core * side, side)
        value = here[...].astype(F32) + theirs[half_rows(block)].astype(F32)
        here[...] = value.astype(BF16)

        @pl.when((block == 4) | (block == 5))
        def _():
            to_two, to_three = early_copy(block, here)

            @pl.when(section == 3)
            def _():
                to_two.start()

            @pl.when(section == 1)
            def _():
                to_three.start()

    small_all[me] = small[...]

    def small_copy(d):
        return remote(small, small_all.at[me], small_send.at[d], small_recv.at[0], section, d)

    @pl.loop(0, n)
    def _(d):
        @pl.when(d != me)
        def _():
            small_copy(d).start()

    own_lines = w_chunks + d_chunks
    lines = own_lines + d_chunks * (is_last - is_first)

    def line_rows(i):
        return pl.ds(pl.multiple_of(i * chunk, chunk), chunk)

    def with_chunk(i, use):
        slot = lax.div(i, per_block)
        first = core * side + lax.rem(i, per_block) * chunk

        @pl.when(i < own_lines)
        def _():
            block = slot + 2 * odd * lax.div(slot, 4)
            use(grad_rows(block, first, chunk))

        @pl.when(i >= own_lines)
        def _():
            use(guest.at[pl.ds(pl.multiple_of((i - own_lines) * chunk, chunk), chunk)])

    def total_rows(i):
        first = core * side + lax.rem(i, per_block) * chunk
        return total_hbm.at[lax.div(i, per_block), pl.ds(pl.multiple_of(first, chunk), chunk)]

    def low_rows(i):
        return from_low.at[line_rows(i)]

    def high_rows(i):
        return from_high.at[line_rows(i)]

    def up_copy(i, source):
        return remote(source, low_rows(i), up_send.at[i], low_recv.at[i], section, me + 2)

    def down_copy(i, source):
        return remote(source, high_rows(i), down_send.at[i], high_recv.at[i], section, me - 2)

    def left_copy(i, source, target):
        return remote(source, target, left_send.at[i], total_recv.at[i], section, me - 2)

    def right_copy(i, source, target):
        return remote(source, target, right_send.at[i], total_recv.at[i], section, me + 2)

    def pair_copy(i, source):
        return remote(source, total_rows(i), pair_send.at[i], pair_recv.at[0], section, sibling)

    def own_copy(i, source):
        return pltpu.make_async_copy(source, total_rows(i), local_sem.at[i])

    def guest_copy(k, source):
        return remote(
            source, total_rows(w_chunks + k), guest_send.at[k], guest_recv.at[k], 0, me
        )

    def reduce_stage(i, root):
        def run(here):
            acc[...] = here[...].astype(F32)

            @pl.when((place <= root) & (place > 0))
            def _():
                up_copy(i, here).wait_recv()
                acc[...] += from_low[line_rows(i)].astype(F32)

            @pl.when((place >= root) & (place < places - 1))
            def _():
                down_copy(i, here).wait_recv()
                acc[...] += from_high[line_rows(i)].astype(F32)

            here[...] = acc[...].astype(BF16)

            @pl.when(place < root)
            def _():
                up_copy(i, here).start()

            @pl.when(place > root)
            def _():
                down_copy(i, here).start()

            @pl.when((place == root) & (i < own_lines))
            def _():
                @pl.when(place > 0)
                def _():
                    left_copy(i, here, total_rows(i)).start()

                @pl.when(place < places - 1)
                def _():
                    right_copy(i, here, total_rows(i)).start()

                pair_copy(i, here).start()
                own_copy(i, here).start()

            @pl.when((place == root) & (i >= own_lines))
            def _():
                @pl.when(place > 0)
                def _():
                    left_copy(i, here, high_rows(i)).start()

                @pl.when(place < places - 1)
                def _():
                    right_copy(i, here, low_rows(i)).start()

                guest_copy(i - own_lines, here).start()

        with_chunk(i, run)

    def pass_on(i, root, left_at, right_at, finish):
        @pl.when(place < root)
        def _():
            left_copy(i, left_at, left_at).wait_recv()

            @pl.when(place > 0)
            def _():
                left_copy(i, left_at, left_at).start()

            finish(left_at)

        @pl.when(place > root)
        def _():
            right_copy(i, right_at, right_at).wait_recv()

            @pl.when(place < places - 1)
            def _():
                right_copy(i, right_at, right_at).start()

            finish(right_at)

    def spread_stage(i, root):
        @pl.when(i < own_lines)
        def _():
            at = total_rows(i)
            pass_on(i, root, at, at, lambda ref: pair_copy(i, ref).start())

        @pl.when(i >= own_lines)
        def _():
            pass_on(
                i,
                root,
                high_rows(i),
                low_rows(i),
                lambda ref: guest_copy(i - own_lines, ref).start(),
            )

    height = places // 2
    pairs = lax.div(lines, 2)
    turns = 4 + 4 * odd

    @pl.loop(0, 1 + pairs + 2 * height * lag)
    def _(step):
        for at in range(2):
            turn = 2 * step - 1 + at

            @pl.when((turn >= 0) & (turn < turns))
            def _():
                grad_block(turn)

        for at in range(2):
            turn = 2 * step - 3 + at

            @pl.when((turn >= 0) & (turn < turns))
            def _():
                pair_sum(turn)

        for at in range(2):
            half_block = half_rows(at)
            arrived = early_copy(4 + at, theirs.at[half_block])[0]

            @pl.when((section == 2) & (step == 1 + (4 + at) * per_block // 2))
            def _():
                arrived.wait_recv()

            @pl.when((section == 3) & (step == 1 + (6 + at) * per_block // 2))
            def _():
                arrived.wait_recv()

        for stream in range(2):
            root = height - 1 + stream
            now = step - 1 - lag * (height - jnp.abs(place - root))

            @pl.when((now >= 0) & (now < pairs))
            def _():
                reduce_stage(2 * now + stream, root)

        for stream in range(2):
            root = height - 1 + stream
            past = step - 1 - lag * (height + jnp.abs(place - root))

            @pl.when((past >= 0) & (past < pairs))
            def _():
                spread_stage(2 * past + stream, root)

    @pl.when(section == 0)
    def _():
        @pl.loop(0, d_chunks)
        def _(k):
            here = total_rows(w_chunks + k)
            guest_copy(k, here).wait_recv()
            pair_copy(w_chunks + k, here).start()

    remote(
        small_all.at[pl.ds(0, n - 1)],
        small_all.at[pl.ds(0, n - 1)],
        small_send.at[0],
        small_recv.at[0],
        section,
        sibling,
    ).wait_recv()

    def add(d, so_far):
        return so_far + small_all[d]

    small_out[...] = lax.fori_loop(1, n, add, small_all[0])
    to_pair = remote(small_out, small_pair, spair_send.at[0], spair_recv.at[0], partner, me)

    @pl.when(not_attn)
    def _():
        to_pair.start()
        to_pair.wait_send()

    @pl.when(is_attn)
    def _():
        to_pair.wait_recv()
        small_out[5:7] = small_pair[3:5]

    @pl.loop(0, lines)
    def _(i):
        some = low_rows(i)

        for stream in range(2):
            root = height - 1 + stream

            @pl.when(lax.rem(i, 2) == stream)
            def _():
                @pl.when(place < root)
                def _():
                    up_copy(i, some).wait_send()

                @pl.when(place > root)
                def _():
                    down_copy(i, some).wait_send()

                @pl.when((place <= root) & (place > 0))
                def _():
                    left_copy(i, some, some).wait_send()

                @pl.when((place >= root) & (place < places - 1))
                def _():
                    right_copy(i, some, some).wait_send()

                @pl.when((place == root) & (i < own_lines))
                def _():
                    own_copy(i, some).wait()

        @pl.when(i < own_lines)
        def _():
            pair_copy(i, some).wait_send()

        @pl.when(i >= own_lines)
        def _():
            guest_copy(i - own_lines, some).wait_send()

    @pl.when(section == 0)
    def _():
        @pl.loop(w_chunks, own_lines)
        def _(i):
            pair_copy(i, low_rows(i)).wait_send()

    @pl.loop(0, turns)
    def _(turn):
        block = block_of(turn)
        sib_copy(block, theirs.at[half_rows(block)]).wait_send()

    @pl.loop(0, n)
    def _(d):
        @pl.when(d != me)
        def _():
            small_copy(d).wait_send()

    @pl.when(is_attn)
    def _():
        @pl.loop(0, pieces)
        def _(k):
            down_first(k).wait_send()

        send_bias.wait_send()

    @pl.when(not_attn)
    def _():
        for at in range(2):
            early_copy(4 + at, theirs.at[half_rows(at)])[0].wait_send()

        @pl.loop(0, chunks)
        def _(c):
            remote(
                leave.at[c], gin.at[c], g_send.at[c], g_recv.at[c], section - 1, me
            ).wait_send()

    @pl.when((section == 1) | (section == 2))
    def _():
        @pl.loop(chunks - depth, chunks)
        def _(c):
            slot = lax.rem(c, depth)
            remote(
                xsend.at[slot], xsend.at[slot], x_send.at[c], x_recv.at[0], 3 - section, me
            ).wait_send()

    @pl.when(section == 3)
    def _():
        @pl.loop(0, chunks)
        def _(c):
            for s in range(SECTIONS - 1):
                remote(
                    gcol.at[s, c], out_ref.at[c], o_send.at[s, c], o_recv.at[0], s, me
                ).wait_send()

    @pl.when(section != 3)
    def _():
        remote(out_ref, out_ref, o_send.at[0, 0], o_recv.at[0], 3, me).wait_recv()

    @pl.when(section == 0)
    def _():
        @pl.loop(0, chunks)
        def _(c):
            for s in range(1, SECTIONS):
                ig_copy(s, c).wait_send()

    @pl.when(section != 0)
    def _():
        remote(ig_ref, ig_ref, ig_send.at[0, 0], ig_recv.at[0], 0, me).wait_recv()

    remote(
        total_hbm.at[pl.ds(0, 3)],
        total_hbm.at[pl.ds(0, 3)],
        pair_send.at[0],
        pair_recv.at[0],
        section,
        sibling,
    ).wait_recv()


def pipeline(
    tokens, cotangent, gain, shift, weight, bias, down, hidden_bias, ftab, ttab, kind, chunk=96, lag=1
):
    micro, rows, width = tokens.shape
    wide = weight.shape[1]
    n = lax.axis_size("dp")
    across = min(n, 16)
    repeat = 16 // across
    slots = rows // WINDOW
    chunks = micro * slots
    quarter = width // SECTIONS
    depth = chunks if n <= 8 else 1
    pieces = 4
    cfg = (n, across, repeat, slots, chunks, width, wide, depth, chunk, lag, pieces)
    vmem = pl.BlockSpec(memory_space=pltpu.VMEM)
    smem = pl.BlockSpec(memory_space=pltpu.SMEM)
    anywhere = pl.BlockSpec(memory_space=pl.ANY)
    dma = pltpu.SemaphoreType.DMA
    chunked = (chunks, WINDOW, width)
    side = width // 2
    lines = 8 * side // chunk
    per_chunk = [dma((lines,)) for _ in range(8)]
    return pl.pallas_call(
        functools.partial(main_kernel, cfg),
        out_shape=(
            jax.ShapeDtypeStruct((chunks, WINDOW, quarter), BF16),
            jax.ShapeDtypeStruct((chunks, WINDOW, quarter), BF16),
            jax.ShapeDtypeStruct((6, width, width), BF16),
            jax.ShapeDtypeStruct((8, width), F32),
        ),
        in_specs=[anywhere, anywhere, vmem, vmem, anywhere, vmem, anywhere, vmem, smem, smem, smem],
        out_specs=(vmem, vmem, anywhere, vmem),
        scratch_shapes=[
            pltpu.VMEM((8, width, width), BF16),
            pltpu.VMEM((chunks, WINDOW, wide), BF16),
            pltpu.VMEM((chunks, WINDOW, wide), BF16),
            pltpu.VMEM(chunked, BF16),
            pltpu.VMEM(chunked, BF16),
            pltpu.VMEM(chunked, BF16),
            pltpu.VMEM(chunked, BF16),
            pltpu.VMEM((WINDOW, width), BF16),
            pltpu.VMEM((SECTIONS - 1, chunks, WINDOW, quarter), BF16),
            pltpu.VMEM((depth, n, repeat, BLOCK, width), BF16),
            pltpu.VMEM((slots, n, repeat, BLOCK, width), BF16),
            pltpu.VMEM((slots, n, repeat, BLOCK, width), BF16),
            pltpu.VMEM((WINDOW // BLOCK, BLOCK, width), BF16),
            pltpu.VMEM((1, wide // 2), F32),
            pltpu.VMEM((1, wide // 2), F32),
            pltpu.VMEM((2, WINDOW, WINDOW), F32),
            pltpu.SMEM((2, n), jnp.int32),
            pltpu.SMEM((2, across), jnp.int32),
            pltpu.VMEM((2 * side, width), BF16),
            pltpu.VMEM((8 * side, width), BF16),
            pltpu.VMEM((lines * chunk, width), BF16),
            pltpu.VMEM((lines * chunk, width), BF16),
            pltpu.VMEM((chunk, width), F32),
            pltpu.VMEM((8, width), F32),
            pltpu.VMEM((n, 8, width), F32),
            pltpu.VMEM((8, width), F32),
            dma((8,)),
            dma((4, pieces)),
            dma((4, pieces)),
            dma((1,)),
            dma((1,)),
            dma((chunks,)),
            dma((chunks,)),
            dma((chunks,)),
            dma((chunks,)),
            dma((chunks,)),
            dma((micro,)),
            dma((SECTIONS - 1, chunks)),
            dma((1,)),
            dma((SECTIONS, chunks)),
            dma((1,)),
            dma((8,)),
            dma((8,)),
            *per_chunk,
            dma((1,)),
            dma((lines,)),
            dma((2,)),
            dma((2,)),
            dma((lines // 4,)),
            dma((lines // 4,)),
            dma((n,)),
            dma((1,)),
            dma((1,)),
            dma((1,)),
        ],
        compiler_params=pltpu.CompilerParams(
            collective_id=0, has_side_effects=True, vmem_limit_bytes=63 * 1024 * 1024
        ),
        name="pipeline",
    )(
        tokens.reshape(chunked),
        cotangent.reshape(chunked),
        gain,
        shift,
        weight,
        bias,
        down,
        hidden_bias.reshape(1, -1),
        ftab,
        ttab,
        kind,
    )


def finish_kernel(
    total_ref,
    small_ref,
    ig_ref,
    out_ref,
    output,
    input_grad,
    gain,
    shift,
    weight,
    bias,
    down,
    hidden,
):
    block, row = pl.program_id(0), pl.program_id(1)

    @pl.when((block == 0) & (row == 0))
    def _():
        output[...] = out_ref[...]
        input_grad[...] = ig_ref[...].astype(F32)
        gain[...] = small_ref[0:1]
        shift[...] = small_ref[1:2]
        bias[...] = small_ref[2:3]
        hidden[...] = small_ref[5:7]

    is_down = block >= 4

    @pl.when(jnp.logical_not(is_down))
    def _():
        weight[...] = total_ref[0].astype(F32)

    @pl.when(is_down)
    def _():
        down[...] = total_ref[0].astype(F32)


def finish(total, small, input_grad, output):
    width = total.shape[-1]
    steps = 2
    span = width // steps

    def whole(array):
        return pl.BlockSpec(array.shape, lambda b, r, k=array.ndim: (0,) * k)

    def weight_at(b, r):
        return jnp.where(b < 4, r, steps - 1), jnp.minimum(b, 3)

    def down_at(b, r):
        return jnp.where(b < 4, 0, (b - 4) * steps + r), 0

    row = jax.ShapeDtypeStruct((1, width), F32)
    pair = jax.ShapeDtypeStruct((2, width), F32)
    wide_grad = jax.ShapeDtypeStruct(input_grad.shape, F32)
    return pl.pallas_call(
        finish_kernel,
        grid=(6, steps),
        out_shape=(
            output,
            wide_grad,
            row,
            row,
            jax.ShapeDtypeStruct((width, SECTIONS * width), F32),
            row,
            jax.ShapeDtypeStruct((2 * width, width), F32),
            pair,
        ),
        in_specs=[
            pl.BlockSpec((1, span, width), lambda b, r: (b, r, 0)),
            whole(small),
            whole(input_grad),
            whole(output),
        ],
        out_specs=(
            whole(output),
            whole(wide_grad),
            whole(row),
            whole(row),
            pl.BlockSpec((span, width), weight_at),
            whole(row),
            pl.BlockSpec((span, width), down_at),
            whole(pair),
        ),
        compiler_params=pltpu.CompilerParams(vmem_limit_bytes=32 * 1024 * 1024),
        name="finish",
    )(total, small, input_grad, output)


def on_device(
    tokens,
    cotangent,
    norm_gain,
    norm_shift,
    in_weight,
    out_bias,
    down_weight,
    hidden_bias,
    frame_device,
    tube_device,
    clip_kind,
):
    micro, rows, width = tokens.shape
    output, input_grad, total, small_total = pipeline(
        tokens,
        cotangent,
        norm_gain,
        norm_shift,
        in_weight[0],
        out_bias,
        down_weight,
        hidden_bias,
        frame_device,
        tube_device,
        clip_kind,
    )
    output, input_grad, gain, shift, weight, bias, down, hidden = finish(
        total, small_total, input_grad, output
    )
    quarter = width // SECTIONS
    return (
        output.reshape(micro, rows, quarter),
        input_grad.reshape(micro, rows, quarter),
        gain,
        shift,
        weight[None],
        bias,
        down,
        hidden.reshape(-1),
    )


def solution(mesh):
    return jax.shard_map(
        on_device,
        mesh=mesh,
        in_specs=(
            P(None, "dp", None),
            P(None, "dp", None),
            P("section", None),
            P("section", None),
            P("section", None, None),
            P("section", None),
            P("section", None),
            P("section"),
            P(),
            P(),
            P(),
        ),
        out_specs=(
            P(None, "dp", "section"),
            P(None, "dp", "section"),
            P("section", None),
            P("section", None),
            P("section", None, None),
            P("section", None),
            P("section", None),
            P("section"),
        ),
        check_vma=False,
    )
```

```python
import functools

import jax
import jax.numpy as jnp
from jax import lax
from jax.experimental import pallas as pl
from jax.experimental.pallas import tpu as pltpu
from jax.sharding import PartitionSpec as P

HEAD_DIM = 64
WINDOW = 256
BLOCK = 16
SECTIONS = 4
EPS = 1e-06
NEGATIVE = -1e30
MESH = pl.DeviceIdType.MESH
F32 = jnp.float32
BF16 = jnp.bfloat16


def mm(left, right):
    return lax.dot_general(left, right, (((1,), (0,)), ((), ())), preferred_element_type=F32)


def mm_nt(left, right):
    return lax.dot_general(left, right, (((1,), (1,)), ((), ())), preferred_element_type=F32)


def mm_tn(left, right):
    return lax.dot_general(left, right, (((0,), (0,)), ((), ())), preferred_element_type=F32)


def remote(src, dst, send_sem, recv_sem, section, dp):
    return pltpu.make_async_remote_copy(
        src_ref=src,
        dst_ref=dst,
        send_sem=send_sem,
        recv_sem=recv_sem,
        device_id=(section, dp),
        device_id_type=MESH,
    )


def normalise(hidden):
    average = jnp.mean(hidden, axis=-1, keepdims=True)
    centred = hidden - average
    inverse = lax.rsqrt(jnp.mean(centred * centred, axis=-1, keepdims=True) + EPS)
    return centred * inverse, inverse


def gelu_and_slope(u):
    cdf = 0.5 + 0.5 * lax.erf(u * 0.7071067811865476)
    bell = jnp.exp(-0.5 * u * u)
    return u * cdf, cdf + (0.3989422804014327 * u) * bell


def main_kernel(
    cfg,
    tok_hbm,
    cot_hbm,
    gain_ref,
    shift_ref,
    w_hbm,
    bias_ref,
    down_hbm,
    hb_ref,
    ftab,
    ttab,
    kind,
    out_ref,
    ig_ref,
    total_hbm,
    small_out,
    weights,
    keep_a,
    keep_b,
    hin,
    gin,
    leave,
    nrm,
    work,
    gcol,
    xsend,
    xrecv0,
    xrecv1,
    xrecv2,
    xrecv3,
    blocks,
    bias_early,
    bias_late,
    mask_add,
    spots,
    sources,
    guest,
    theirs,
    from_low,
    from_high,
    acc,
    small,
    small_all,
    small_pair,
    load_sem,
    w_send,
    w_recv,
    hb_send,
    hb_recv,
    h_send,
    h_recv,
    g_send,
    g_recv,
    x_send,
    x_recv,
    o_send,
    o_recv,
    ig_send,
    ig_recv,
    sib_send,
    sib_recv,
    up_send,
    low_recv,
    down_send,
    high_recv,
    left_send,
    right_send,
    total_recv,
    pair_send,
    pair_recv,
    local_sem,
    early_send,
    early_recv,
    guest_send,
    guest_recv,
    small_send,
    small_recv,
    spair_send,
    spair_recv,
):
    n, across, repeat, slots, chunks, width, wide, depth, chunk, lag, pieces = cfg
    section = lax.axis_index("section")
    me = lax.axis_index("dp")
    core = lax.rem(me, 2)
    place = lax.div(me, 2)
    places = n // 2
    sibling = me + 1 - 2 * core
    odd_place = lax.rem(place, 2)
    across_z = me + 2 - 4 * odd_place
    odd = lax.rem(section, 2)
    is_attn = odd == 0
    not_attn = odd == 1
    partner = section + 1 - 2 * odd
    is_first, is_last = lax.div(3 - section, 3), lax.div(section, 3)
    xrecv = (xrecv0, xrecv1, xrecv2, xrecv3)
    share = WINDOW // repeat
    half = wide // 2
    quarter = width // SECTIONS

    def load_columns(j):
        columns = pl.ds(j * width, width)
        return pltpu.make_async_copy(w_hbm.at[:, columns], weights.at[j], load_sem.at[j])

    def load_rows(j):
        rows = pl.ds(j * width, width)
        return pltpu.make_async_copy(down_hbm.at[rows], weights.at[6 + j], load_sem.at[6 + j])

    load_t = pltpu.make_async_copy(tok_hbm, hin, load_sem.at[5])
    load_c = pltpu.make_async_copy(cot_hbm, gin, load_sem.at[5])

    @pl.when(section == 0)
    def _():
        load_t.start()

    for j in range(4):
        load_columns(j).start()

    @pl.when(section == 3)
    def _():
        load_c.start()

    @pl.when(not_attn)
    def _():
        load_rows(0).start()
        load_rows(1).start()

    barrier = pltpu.get_barrier_semaphore()

    def greet(s, d):
        pl.semaphore_signal(barrier, inc=1, device_id=(s, d), device_id_type=MESH)

    @pl.loop(0, n)
    def _(d):
        @pl.when(d != me)
        def _():
            greet(section, d)

        @pl.when((section == 1) | (section == 2))
        def _():
            greet(3 - section, d)

    greet(partner, me)
    greet(3 - partner, me)

    @pl.when((section == 0) | (section == 3))
    def _():
        greet(3 - section, me)

    def meet():
        edge = is_first + is_last
        pl.semaphore_wait(barrier, n + 1 + edge + (1 - edge) * n)

    bias_late[...] = hb_ref[...].astype(F32).reshape(bias_late.shape)
    send_bias = remote(bias_late, bias_early, hb_send.at[0], hb_recv.at[0], partner, me)
    span = half // 4
    step_rows = span // pieces

    def parts(z_side, which_core, k):
        first = which_core * span + k * step_rows
        in_block = pl.ds(pl.multiple_of(first, step_rows), step_rows)
        in_all = pl.ds(pl.multiple_of(z_side * width + first, step_rows), step_rows)
        return down_hbm.at[in_all], weights.at[4 + z_side, in_block]

    def down_first(k):
        source, here = parts(odd_place, core, k)
        return remote(source, here, w_send.at[0, k], w_recv.at[0, k], partner, me)

    def down_along(k):
        here = parts(odd_place, core, k)[1]
        return remote(here, here, w_send.at[1, k], w_recv.at[1, k], section, across_z)

    def down_pair(k):
        here = parts(odd_place, core, k)[1]
        return remote(here, here, w_send.at[2, k], w_recv.at[2, k], section, sibling)

    def down_last(k):
        here = parts(1 - odd_place, core, k)[1]
        return remote(here, here, w_send.at[3, k], w_recv.at[3, k], section, sibling)

    gain = gain_ref[...].astype(F32)
    shift = shift_ref[...].astype(F32)
    bias = bias_ref[...].astype(F32)
    small[...] = jnp.zeros_like(small)

    def role_of(table, micro, device):
        def step(r, found):
            return found + jnp.where(table[micro, r] == device, r, 0)

        return lax.fori_loop(0, n, step, 0)

    def make_tables(send_table, own_table):
        for m in range(2):

            @pl.loop(0, n)
            def _(d):
                spots[m, d] = lax.rem(role_of(send_table, m, d), across)

            family = lax.rem(lax.div(role_of(own_table, m, me), across), n // across)

            @pl.loop(0, across)
            def _(r):
                sources[m, r] = send_table[m, family * across + r]

    def slot_of(unit, f):
        return lax.div(unit, repeat) * repeat + f

    def share_rows(k):
        return pl.ds(pl.multiple_of(k * share, share), share)

    def unit_copy(k):
        unit, f = lax.div(k, repeat), lax.rem(k, repeat)
        return remote(
            leave.at[slot_of(unit, f), share_rows(lax.rem(unit, repeat))],
            hin.at[unit, share_rows(f)],
            h_send.at[k],
            h_recv.at[unit],
            1,
            me,
        )

    def unit_back(unit, f):
        return remote(
            leave.at[unit, share_rows(f)],
            gin.at[slot_of(unit, f), share_rows(lax.rem(unit, repeat))],
            g_send.at[unit, f],
            g_recv.at[slot_of(unit, f)],
            0,
            me,
        )

    def slot_copy(c):
        return remote(leave.at[c], hin.at[c], h_send.at[c], h_recv.at[c], 3, me)

    def slot_back(c):
        return remote(leave.at[c], gin.at[c], g_send.at[c, 0], g_recv.at[c], 2, me)

    def send_blocks(c, rows, to_section, forward):
        blocks[...] = rows.reshape(blocks.shape)
        micro = lax.div(c, slots)
        slot = lax.rem(c, depth)

        @pl.when(c >= depth)
        def _():
            remote(
                xsend.at[slot], xsend.at[slot], x_send.at[c - depth], x_recv.at[0], to_section, me
            ).wait_send()

        @pl.loop(0, n)
        def _(d):
            spot = spots[micro, d]
            for g in range(repeat):
                block = g * across + spot if forward else spot * repeat + g
                xsend[slot, d, g] = blocks[block]

        for i in range(chunks):

            @pl.when(c == i)
            def _():
                @pl.loop(0, n)
                def _(d):
                    remote(
                        xsend.at[slot, d],
                        xrecv[i].at[me],
                        x_send.at[c],
                        x_recv.at[i],
                        to_section,
                        d,
                    ).start()

    def gather_blocks(c, target, from_section, forward):
        for i in range(chunks):

            @pl.when(c == i)
            def _():
                remote(xrecv[i], xrecv[i], x_send.at[0], x_recv.at[i], from_section, me).wait_recv()

                @pl.loop(0, across)
                def _(r):
                    source = sources[i // slots, r]
                    for f in range(repeat):
                        block = r * repeat + f if forward else f * across + r
                        rows = pl.ds(pl.multiple_of(block * BLOCK, BLOCK), BLOCK)
                        target[i, rows] = xrecv[i][source, f]

    def norm_back(c, dn, gb):
        nh, inverse = normalise(hin[c].astype(F32))
        weighted = dn * gain
        first = jnp.mean(weighted, axis=-1, keepdims=True)
        second = jnp.mean(weighted * nh, axis=-1, keepdims=True)
        grad = gb.astype(F32) + inverse * (weighted - first - nh * second)
        small[0:1] += jnp.sum(dn * nh, axis=0, keepdims=True)
        small[1:2] += jnp.sum(dn, axis=0, keepdims=True)
        small[2:3] += jnp.sum(gb.astype(F32), axis=0, keepdims=True)
        return grad

    def ig_copy(s, c):
        return remote(gcol.at[s - 1, c], ig_ref.at[c], ig_send.at[s, c], ig_recv.at[0], s, me)

    @pl.when(is_attn)
    def _():
        lane = lax.broadcasted_iota(jnp.int32, (1, 2 * HEAD_DIM), 1)
        first_head = jnp.where(lane < HEAD_DIM, 1.0, 0.0)
        pick = [first_head.astype(BF16), (1.0 - first_head).astype(BF16)]
        scale = HEAD_DIM ** (-0.5)
        pick_scaled = [
            (first_head * scale).astype(BF16),
            ((1.0 - first_head) * scale).astype(BF16),
        ]
        key_window = lax.broadcasted_iota(jnp.int32, (WINDOW, WINDOW), 0) % 16 // 4
        query_window = lax.broadcasted_iota(jnp.int32, (WINDOW, WINDOW), 1) % 16 // 4
        barred = jnp.where(key_window == query_window, 0.0, NEGATIVE)
        for m in range(2):
            mask_add[m] = barred * kind[m].astype(F32)

        meet()

        @pl.loop(0, pieces)
        def _(k):
            down_first(k).start()

        send_bias.start()

        @pl.when(section == 2)
        def _():
            make_tables(ftab, ttab)

        def forward(c):
            @pl.when(section == 2)
            def _():
                gather_blocks(c, hin, 1, True)

            @pl.when((section == 0) & (c == 0))
            def _():
                load_t.wait()

            micro = lax.div(c, slots)
            hidden = hin[c].astype(F32)
            nh, _ = normalise(hidden)
            normed = (nh * gain + shift).astype(BF16)
            nrm[c] = normed
            for j in range(3):
                columns = pl.ds(j * width, width)

                @pl.when(c == 0)
                def _():
                    load_columns(j).wait()

                keep_b[c, :, columns] = mm(normed, weights[j]).astype(BF16)

            @pl.when(c == 0)
            def _():
                load_columns(3).wait()


            places_at = [g * 2 * HEAD_DIM for g in range(width // (2 * HEAD_DIM))]
            scores = []
            for offset in places_at:
                q = keep_b[c, :, pl.ds(offset, 2 * HEAD_DIM)]
                k = keep_b[c, :, pl.ds(width + offset, 2 * HEAD_DIM)]
                for one in range(2):
                    scores.append(mm_nt(k, q * pick_scaled[one]))
            probs = []
            for z in scores:
                z = z + mask_add[micro]
                e = jnp.exp(z - jnp.max(z, axis=0, keepdims=True))
                p = e * (1.0 / jnp.sum(e, axis=0, keepdims=True))
                probs.append(p.astype(BF16))
            for g, offset in enumerate(places_at):
                v = keep_b[c, :, pl.ds(2 * width + offset, 2 * HEAD_DIM)]
                o = None
                for one in range(2):
                    pb = probs[2 * g + one]
                    spot = (2 * g + one) * WINDOW
                    keep_a[c, :, pl.ds(spot, WINDOW)] = pb
                    term = mm_tn(pb, v * pick[one])
                    o = term if o is None else o + term
                keep_b[c, :, pl.ds(3 * width + offset, 2 * HEAD_DIM)] = o.astype(BF16)

            branch = mm(keep_b[c, :, pl.ds(3 * width, width)], weights[3])
            leave[c] = (hin[c].astype(F32) + branch + bias).astype(BF16)

            @pl.when(section == 2)
            def _():
                slot_copy(c).start()

            @pl.when(section == 0)
            def _():
                unit_copy(c).start()

            @pl.when((section == 0) & (c == chunks - 1))
            def _():
                @pl.loop(chunks, chunks * repeat)
                def _(k):
                    unit_copy(k - 2).wait_send()
                    unit_copy(k).start()

        def backward(c):
            slot_back(c).wait_recv()
            gb = gin[c]
            work[...] = mm_nt(gb, weights[3]).astype(BF16)

            places_at = [g * 2 * HEAD_DIM for g in range(width // (2 * HEAD_DIM))]
            grads = []
            for offset in places_at:
                v = keep_b[c, :, pl.ds(2 * width + offset, 2 * HEAD_DIM)]
                go = work[:, pl.ds(offset, 2 * HEAD_DIM)]
                for one in range(2):
                    grads.append(mm_nt(v, go * pick[one]))
            for g, offset in enumerate(places_at):
                q_at = pl.ds(offset, 2 * HEAD_DIM)
                k_at = pl.ds(width + offset, 2 * HEAD_DIM)
                v_at = pl.ds(2 * width + offset, 2 * HEAD_DIM)
                q, k, go = keep_b[c, :, q_at], keep_b[c, :, k_at], work[:, q_at]
                dq = dk = dv = None
                for one in range(2):
                    spot = (2 * g + one) * WINDOW
                    pb = keep_a[c, :, pl.ds(spot, WINDOW)]
                    p = pb.astype(F32)
                    pdp = p * grads[2 * g + one]
                    ds = (pdp - p * jnp.sum(pdp, axis=0, keepdims=True)).astype(BF16)
                    tv = mm(pb, go * pick[one])
                    tk = mm(ds, q * pick_scaled[one])
                    tq = mm_tn(ds, k * pick_scaled[one])
                    dv = tv if dv is None else dv + tv
                    dk = tk if dk is None else dk + tk
                    dq = tq if dq is None else dq + tq
                keep_b[c, :, q_at] = dq.astype(BF16)
                keep_b[c, :, k_at] = dk.astype(BF16)
                keep_b[c, :, v_at] = dv.astype(BF16)

            dn = sum(mm_nt(keep_b[c, :, pl.ds(j * width, width)], weights[j]) for j in range(3))
            leaving = norm_back(c, dn, gb).astype(BF16)

            @pl.when(section == 2)
            def _():
                send_blocks(c, leaving, 1, False)

            @pl.when(section == 0)
            def _():
                for s in range(1, SECTIONS):
                    gcol[s - 1, c] = leaving[:, s * quarter : (s + 1) * quarter]
                ig_ref[c] = leaving[:, 0:quarter]
                for s in range(1, SECTIONS):
                    ig_copy(s, c).start()

        @pl.loop(0, 2 * chunks)
        def _(step):
            c = lax.rem(step, chunks)

            @pl.when(step < chunks)
            def _():
                forward(c)

            @pl.when(step >= chunks)
            def _():
                backward(c)

    @pl.when(not_attn)
    def _():
        meet()

        @pl.when(section == 1)
        def _():
            make_tables(ttab, ftab)

        for j in range(4):
            load_columns(j).wait()

        load_rows(0).wait()
        load_rows(1).wait()

        @pl.loop(0, pieces)
        def _(k):
            down_first(k).wait_recv()
            down_along(k).start()
            down_pair(k).start()

        @pl.loop(0, pieces)
        def _(k):
            down_along(k).wait_recv()
            down_last(k).start()

        send_bias.wait_recv()

        @pl.when(section == 3)
        def _():
            load_c.wait()

        def forward(c):
            slot_copy(c).wait_recv()
            hidden = hin[c].astype(F32)
            nh, _ = normalise(hidden)
            normed = (nh * gain + shift).astype(BF16)
            nrm[c] = normed
            for j in range(4):
                columns = pl.ds(j * width, width)
                u = mm(normed, weights[j])
                u = u + (bias_early, bias_late)[j // 2][:, pl.ds((j % 2) * width, width)]
                active, slope = gelu_and_slope(u)
                keep_a[c, :, columns] = active.astype(BF16)
                keep_b[c, :, columns] = slope.astype(BF16)

            @pl.when(c == 0)
            def _():
                @pl.loop(0, pieces)
                def _(k):
                    down_pair(k).wait_recv()
                    down_last(k).wait_recv()

            branch = mm(keep_a[c], weights[pl.ds(4, 4)].reshape(wide, width))
            leaving = (hin[c].astype(F32) + branch + bias).astype(BF16)

            @pl.when(section == 1)
            def _():
                send_blocks(c, leaving, 2, True)

            @pl.when(section == 3)
            def _():
                for s in range(SECTIONS - 1):
                    gcol[s, c] = leaving[:, s * quarter : (s + 1) * quarter]
                out_ref[c] = leaving[:, (SECTIONS - 1) * quarter :]
                for s in range(SECTIONS - 1):
                    remote(
                        gcol.at[s, c], out_ref.at[c], o_send.at[s, c], o_recv.at[0], s, me
                    ).start()

        def backward(c):
            @pl.when(section == 1)
            def _():
                gather_blocks(c, gin, 2, False)

            gb = gin[c]
            for j in range(4):
                columns = pl.ds(j * width, width)
                da = mm_nt(gb, weights[4 + j])
                du = da * keep_b[c, :, columns].astype(F32)
                keep_b[c, :, columns] = du.astype(BF16)
                small[3 + j : 4 + j] += jnp.sum(du, axis=0, keepdims=True)
            dn = sum(mm_nt(keep_b[c, :, pl.ds(j * width, width)], weights[j]) for j in range(4))
            leave[c] = norm_back(c, dn, gb).astype(BF16)

            @pl.when(section == 3)
            def _():
                slot_back(c).start()

            @pl.when(section == 1)
            def _():
                for f in range(repeat):
                    unit_back(c, f).start()
        @pl.loop(0, 2 * chunks)
        def _(step):
            last = lax.div(section, 2)
            c = last * lax.div(step, 2) + (1 - last) * lax.rem(step, chunks)
            back = last * lax.rem(step, 2) + (1 - last) * lax.div(step, chunks)

            @pl.when(back == 0)
            def _():
                forward(c)

            @pl.when(back == 1)
            def _():
                backward(c)

    @pl.when(not_attn)
    def _():
        @pl.loop(0, pieces)
        def _(k):
            down_along(k).wait_send()
            down_pair(k).wait_send()
            down_last(k).wait_send()

    side = width // 2
    per_block = side // chunk
    w_chunks, d_chunks = 4 * per_block, 2 * per_block
    rows_all = chunks * WINDOW

    def grad_rows(block, first, count):
        return weights.at[block, pl.ds(pl.multiple_of(first, count), count)]

    def half_rows(block):
        return pl.ds(pl.multiple_of(block * side, side), side)

    def block_of(turn):
        last = turn + 2 * lax.div(turn, 4) - 4 * lax.div(turn, 6)
        first = turn + 3 * lax.div(turn + 7, 8) - 5 * lax.div(turn + 5, 8) + 2 * lax.div(turn, 6)
        second = odd - is_last
        return second * first + (1 - second) * last

    def sib_copy(block, source):
        return remote(
            source, theirs.at[half_rows(block)], sib_send.at[block], sib_recv.at[block], section, sibling
        )

    def outer(left, left_at, right, right_at, block):
        right_value = right[:, :, right_at].reshape(rows_all, width)

        @pl.loop(0, width // WINDOW)
        def _(k):
            columns = pl.ds(pl.multiple_of(left_at + k * WINDOW, WINDOW), WINDOW)
            left_value = left[:, :, columns].reshape(rows_all, WINDOW)
            rows = pl.ds(pl.multiple_of(k * WINDOW, WINDOW), WINDOW)
            weights[block, rows] = mm_tn(left_value, right_value).astype(BF16)

    def grad_block(turn):
        block = block_of(turn)

        @pl.when((block < 4) & (not_attn | (block < 3)))
        def _():
            columns = pl.ds(pl.multiple_of(block * width, width), width)
            outer(nrm, 0, keep_b, columns, block)

        @pl.when((block == 3) & is_attn)
        def _():
            outer(keep_b, 3 * width, gin, pl.ds(0, width), block)

        @pl.when(block >= 4)
        def _():
            outer(keep_a, (block - 4) * width, gin, pl.ds(0, width), block)

        sib_copy(block, grad_rows(block, (1 - core) * side, side)).start()

    def early_copy(block, source):
        send, recv = early_send.at[block - 4], early_recv.at[block - 4]
        return (
            remote(source, grad_rows(block, core * side, side), send, recv, 2, me),
            remote(source, guest.at[half_rows(block - 4)], send, recv, 3, me),
        )

    def pair_sum(turn):
        block = block_of(turn)
        sib_copy(block, theirs.at[half_rows(block)]).wait_recv()

        here = grad_rows(block, core * side, side)
        value = here[...].astype(F32) + theirs[half_rows(block)].astype(F32)
        here[...] = value.astype(BF16)

        @pl.when((block == 4) | (block == 5))
        def _():
            to_two, to_three = early_copy(block, here)

            @pl.when(section == 3)
            def _():
                to_two.start()

            @pl.when(section == 1)
            def _():
                to_three.start()

    small_all[me] = small[...]

    def small_copy(d):
        return remote(small, small_all.at[me], small_send.at[d], small_recv.at[0], section, d)

    @pl.loop(0, n)
    def _(d):
        @pl.when(d != me)
        def _():
            small_copy(d).start()

    own_lines = w_chunks + d_chunks
    lines = own_lines + d_chunks * (is_last - is_first)

    def line_rows(i):
        return pl.ds(pl.multiple_of(i * chunk, chunk), chunk)

    def with_chunk(i, use):
        slot = lax.div(i, per_block)
        first = core * side + lax.rem(i, per_block) * chunk

        @pl.when(i < own_lines)
        def _():
            block = slot + 2 * odd * lax.div(slot, 4)
            use(grad_rows(block, first, chunk))

        @pl.when(i >= own_lines)
        def _():
            use(guest.at[pl.ds(pl.multiple_of((i - own_lines) * chunk, chunk), chunk)])

    def total_rows(i):
        first = core * side + lax.rem(i, per_block) * chunk
        return total_hbm.at[lax.div(i, per_block), pl.ds(pl.multiple_of(first, chunk), chunk)]

    def low_rows(i):
        return from_low.at[line_rows(i)]

    def high_rows(i):
        return from_high.at[line_rows(i)]

    def up_copy(i, source):
        return remote(source, low_rows(i), up_send.at[i], low_recv.at[i], section, me + 2)

    def down_copy(i, source):
        return remote(source, high_rows(i), down_send.at[i], high_recv.at[i], section, me - 2)

    def left_copy(i, source, target):
        return remote(source, target, left_send.at[i], total_recv.at[i], section, me - 2)

    def right_copy(i, source, target):
        return remote(source, target, right_send.at[i], total_recv.at[i], section, me + 2)

    def pair_copy(i, source):
        return remote(source, total_rows(i), pair_send.at[i], pair_recv.at[0], section, sibling)

    def own_copy(i, source):
        return pltpu.make_async_copy(source, total_rows(i), local_sem.at[i])

    def guest_copy(k, source):
        return remote(
            source, total_rows(w_chunks + k), guest_send.at[k], guest_recv.at[k], 0, me
        )

    def reduce_stage(i, root):
        def run(here):
            acc[...] = here[...].astype(F32)

            @pl.when((place <= root) & (place > 0))
            def _():
                up_copy(i, here).wait_recv()
                acc[...] += from_low[line_rows(i)].astype(F32)

            @pl.when((place >= root) & (place < places - 1))
            def _():
                down_copy(i, here).wait_recv()
                acc[...] += from_high[line_rows(i)].astype(F32)

            here[...] = acc[...].astype(BF16)

            @pl.when(place < root)
            def _():
                up_copy(i, here).start()

            @pl.when(place > root)
            def _():
                down_copy(i, here).start()

            @pl.when((place == root) & (i < own_lines))
            def _():
                @pl.when(place > 0)
                def _():
                    left_copy(i, here, total_rows(i)).start()

                @pl.when(place < places - 1)
                def _():
                    right_copy(i, here, total_rows(i)).start()

                pair_copy(i, here).start()
                own_copy(i, here).start()

            @pl.when((place == root) & (i >= own_lines))
            def _():
                @pl.when(place > 0)
                def _():
                    left_copy(i, here, high_rows(i)).start()

                @pl.when(place < places - 1)
                def _():
                    right_copy(i, here, low_rows(i)).start()

                guest_copy(i - own_lines, here).start()

        with_chunk(i, run)

    def pass_on(i, root, left_at, right_at, finish):
        @pl.when(place < root)
        def _():
            left_copy(i, left_at, left_at).wait_recv()

            @pl.when(place > 0)
            def _():
                left_copy(i, left_at, left_at).start()

            finish(left_at)

        @pl.when(place > root)
        def _():
            right_copy(i, right_at, right_at).wait_recv()

            @pl.when(place < places - 1)
            def _():
                right_copy(i, right_at, right_at).start()

            finish(right_at)

    def spread_stage(i, root):
        @pl.when(i < own_lines)
        def _():
            at = total_rows(i)
            pass_on(i, root, at, at, lambda ref: pair_copy(i, ref).start())

        @pl.when(i >= own_lines)
        def _():
            pass_on(
                i,
                root,
                high_rows(i),
                low_rows(i),
                lambda ref: guest_copy(i - own_lines, ref).start(),
            )

    height = places // 2
    pairs = lax.div(lines, 2)
    turns = 4 + 4 * odd

    @pl.loop(0, 1 + pairs + 2 * height * lag)
    def _(step):
        for at in range(2):
            turn = 2 * step - 1 + at

            @pl.when((turn >= 0) & (turn < turns))
            def _():
                grad_block(turn)

        for at in range(2):
            turn = 2 * step - 3 + at

            @pl.when((turn >= 0) & (turn < turns))
            def _():
                pair_sum(turn)

        for at in range(2):
            half_block = half_rows(at)
            arrived = early_copy(4 + at, theirs.at[half_block])[0]

            @pl.when((section == 2) & (step == 1 + (4 + at) * per_block // 2))
            def _():
                arrived.wait_recv()

            @pl.when((section == 3) & (step == 1 + (6 + at) * per_block // 2))
            def _():
                arrived.wait_recv()

        for stream in range(2):
            root = height - 1 + stream
            now = step - 1 - lag * (height - jnp.abs(place - root))

            @pl.when((now >= 0) & (now < pairs))
            def _():
                reduce_stage(2 * now + stream, root)

        for stream in range(2):
            root = height - 1 + stream
            past = step - 1 - lag * (height + jnp.abs(place - root))

            @pl.when((past >= 0) & (past < pairs))
            def _():
                spread_stage(2 * past + stream, root)

    @pl.when(section == 0)
    def _():
        @pl.loop(0, d_chunks)
        def _(k):
            here = total_rows(w_chunks + k)
            guest_copy(k, here).wait_recv()
            pair_copy(w_chunks + k, here).start()

    remote(
        small_all.at[pl.ds(0, n - 1)],
        small_all.at[pl.ds(0, n - 1)],
        small_send.at[0],
        small_recv.at[0],
        section,
        sibling,
    ).wait_recv()

    def add(d, so_far):
        return so_far + small_all[d]

    small_out[...] = lax.fori_loop(1, n, add, small_all[0])
    to_pair = remote(small_out, small_pair, spair_send.at[0], spair_recv.at[0], partner, me)

    @pl.when(not_attn)
    def _():
        to_pair.start()
        to_pair.wait_send()

    @pl.when(is_attn)
    def _():
        to_pair.wait_recv()
        small_out[5:7] = small_pair[3:5]

    @pl.loop(0, lines)
    def _(i):
        some = low_rows(i)

        for stream in range(2):
            root = height - 1 + stream

            @pl.when(lax.rem(i, 2) == stream)
            def _():
                @pl.when(place < root)
                def _():
                    up_copy(i, some).wait_send()

                @pl.when(place > root)
                def _():
                    down_copy(i, some).wait_send()

                @pl.when((place <= root) & (place > 0))
                def _():
                    left_copy(i, some, some).wait_send()

                @pl.when((place >= root) & (place < places - 1))
                def _():
                    right_copy(i, some, some).wait_send()

                @pl.when((place == root) & (i < own_lines))
                def _():
                    own_copy(i, some).wait()

        @pl.when(i < own_lines)
        def _():
            pair_copy(i, some).wait_send()

        @pl.when(i >= own_lines)
        def _():
            guest_copy(i - own_lines, some).wait_send()

    @pl.when(section == 0)
    def _():
        @pl.loop(w_chunks, own_lines)
        def _(i):
            pair_copy(i, low_rows(i)).wait_send()

    @pl.loop(0, turns)
    def _(turn):
        block = block_of(turn)
        sib_copy(block, theirs.at[half_rows(block)]).wait_send()

    @pl.loop(0, n)
    def _(d):
        @pl.when(d != me)
        def _():
            small_copy(d).wait_send()

    @pl.when(is_attn)
    def _():
        @pl.loop(0, pieces)
        def _(k):
            down_first(k).wait_send()

        send_bias.wait_send()

        @pl.when(section == 0)
        def _():
            @pl.loop(0, chunks - 2)
            def _(k):
                unit_copy(k).wait_send()

            @pl.loop(chunks * repeat - 2, chunks * repeat)
            def _(k):
                unit_copy(k).wait_send()

        @pl.when(section == 2)
        def _():
            @pl.loop(0, chunks)
            def _(c):
                slot_copy(c).wait_send()

    @pl.when(not_attn)
    def _():
        for at in range(2):
            early_copy(4 + at, theirs.at[half_rows(at)])[0].wait_send()

        @pl.when(section == 3)
        def _():
            @pl.loop(0, chunks)
            def _(c):
                slot_back(c).wait_send()

        @pl.when(section == 1)
        def _():
            @pl.loop(0, chunks)
            def _(c):
                for f in range(repeat):
                    unit_back(c, f).wait_send()

    @pl.when((section == 1) | (section == 2))
    def _():
        @pl.loop(chunks - depth, chunks)
        def _(c):
            slot = lax.rem(c, depth)
            remote(
                xsend.at[slot], xsend.at[slot], x_send.at[c], x_recv.at[0], 3 - section, me
            ).wait_send()

    @pl.when(section == 3)
    def _():
        @pl.loop(0, chunks)
        def _(c):
            for s in range(SECTIONS - 1):
                remote(
                    gcol.at[s, c], out_ref.at[c], o_send.at[s, c], o_recv.at[0], s, me
                ).wait_send()

    @pl.when(section != 3)
    def _():
        remote(out_ref, out_ref, o_send.at[0, 0], o_recv.at[0], 3, me).wait_recv()

    @pl.when(section == 0)
    def _():
        @pl.loop(0, chunks)
        def _(c):
            for s in range(1, SECTIONS):
                ig_copy(s, c).wait_send()

    @pl.when(section != 0)
    def _():
        remote(ig_ref, ig_ref, ig_send.at[0, 0], ig_recv.at[0], 0, me).wait_recv()

    remote(
        total_hbm.at[pl.ds(0, 3)],
        total_hbm.at[pl.ds(0, 3)],
        pair_send.at[0],
        pair_recv.at[0],
        section,
        sibling,
    ).wait_recv()


def pipeline(
    tokens, cotangent, gain, shift, weight, bias, down, hidden_bias, ftab, ttab, kind, chunk=96, lag=1
):
    micro, rows, width = tokens.shape
    wide = weight.shape[1]
    n = lax.axis_size("dp")
    across = min(n, 16)
    repeat = 16 // across
    slots = rows // WINDOW
    chunks = micro * slots
    quarter = width // SECTIONS
    depth = chunks if n <= 8 else 1
    pieces = 4
    cfg = (n, across, repeat, slots, chunks, width, wide, depth, chunk, lag, pieces)
    vmem = pl.BlockSpec(memory_space=pltpu.VMEM)
    smem = pl.BlockSpec(memory_space=pltpu.SMEM)
    anywhere = pl.BlockSpec(memory_space=pl.ANY)
    dma = pltpu.SemaphoreType.DMA
    chunked = (chunks, WINDOW, width)
    side = width // 2
    lines = 8 * side // chunk
    per_chunk = [dma((lines,)) for _ in range(8)]
    return pl.pallas_call(
        functools.partial(main_kernel, cfg),
        out_shape=(
            jax.ShapeDtypeStruct((chunks, WINDOW, quarter), BF16),
            jax.ShapeDtypeStruct((chunks, WINDOW, quarter), BF16),
            jax.ShapeDtypeStruct((6, width, width), BF16),
            jax.ShapeDtypeStruct((8, width), F32),
        ),
        in_specs=[anywhere, anywhere, vmem, vmem, anywhere, vmem, anywhere, vmem, smem, smem, smem],
        out_specs=(vmem, vmem, anywhere, vmem),
        scratch_shapes=[
            pltpu.VMEM((8, width, width), BF16),
            pltpu.VMEM((chunks, WINDOW, wide), BF16),
            pltpu.VMEM((chunks, WINDOW, wide), BF16),
            pltpu.VMEM(chunked, BF16),
            pltpu.VMEM(chunked, BF16),
            pltpu.VMEM(chunked, BF16),
            pltpu.VMEM(chunked, BF16),
            pltpu.VMEM((WINDOW, width), BF16),
            pltpu.VMEM((SECTIONS - 1, chunks, WINDOW, quarter), BF16),
            pltpu.VMEM((depth, n, repeat, BLOCK, width), BF16),
            *[pltpu.VMEM((n, repeat, BLOCK, width), BF16) for _ in range(4)],
            pltpu.VMEM((WINDOW // BLOCK, BLOCK, width), BF16),
            pltpu.VMEM((1, wide // 2), F32),
            pltpu.VMEM((1, wide // 2), F32),
            pltpu.VMEM((2, WINDOW, WINDOW), F32),
            pltpu.SMEM((2, n), jnp.int32),
            pltpu.SMEM((2, across), jnp.int32),
            pltpu.VMEM((2 * side, width), BF16),
            pltpu.VMEM((8 * side, width), BF16),
            pltpu.VMEM((lines * chunk, width), BF16),
            pltpu.VMEM((lines * chunk, width), BF16),
            pltpu.VMEM((chunk, width), F32),
            pltpu.VMEM((8, width), F32),
            pltpu.VMEM((n, 8, width), F32),
            pltpu.VMEM((8, width), F32),
            dma((8,)),
            dma((4, pieces)),
            dma((4, pieces)),
            dma((1,)),
            dma((1,)),
            dma((chunks * repeat,)),
            dma((chunks,)),
            dma((chunks, repeat)),
            dma((chunks,)),
            dma((chunks,)),
            dma((chunks,)),
            dma((SECTIONS - 1, chunks)),
            dma((1,)),
            dma((SECTIONS, chunks)),
            dma((1,)),
            dma((8,)),
            dma((8,)),
            *per_chunk,
            dma((1,)),
            dma((lines,)),
            dma((2,)),
            dma((2,)),
            dma((lines // 4,)),
            dma((lines // 4,)),
            dma((n,)),
            dma((1,)),
            dma((1,)),
            dma((1,)),
        ],
        compiler_params=pltpu.CompilerParams(
            collective_id=0, has_side_effects=True, vmem_limit_bytes=63 * 1024 * 1024
        ),
        name="pipeline",
    )(
        tokens.reshape(chunked),
        cotangent.reshape(chunked),
        gain,
        shift,
        weight,
        bias,
        down,
        hidden_bias,
        ftab,
        ttab,
        kind,
    )


def finish_kernel(
    total_hbm,
    small_ref,
    ig_ref,
    out_ref,
    output,
    input_grad,
    gain,
    shift,
    weight_hbm,
    bias,
    down_hbm,
    hidden,
    short,
    full,
    in_sem,
    out_sem,
):
    width = total_hbm.shape[2]
    steps = short.shape[1]
    span = width // steps
    order = [(b, r) for b in range(6) for r in range(steps)]

    def read(b, r):
        rows = pl.ds(r * span, span)
        return pltpu.make_async_copy(total_hbm.at[b, rows], short.at[b, r], in_sem.at[b, r])

    def write(b, r):
        if b < 4:
            target = weight_hbm.at[pl.ds(r * span, span), pl.ds(b * width, width)]
        else:
            target = down_hbm.at[pl.ds((b - 4) * width + r * span, span)]
        return pltpu.make_async_copy(full.at[b, r], target, out_sem.at[b, r])

    for b, r in order:
        read(b, r).start()
    for b, r in order:
        read(b, r).wait()
        full[b, r] = short[b, r].astype(F32)
        write(b, r).start()
    slots = output.shape[2] // WINDOW
    for c in range(out_ref.shape[0]):
        at = pl.ds(c % slots * WINDOW, WINDOW)
        output[c // slots, :, at] = out_ref[c].T
        input_grad[c // slots, :, at] = ig_ref[c].astype(F32).T
    gain[...] = small_ref[0:1]
    shift[...] = small_ref[1:2]
    bias[...] = small_ref[2:3]
    for k in range(2):
        hidden[pl.ds(k * width, width)] = small_ref[5 + k]
    for b, r in order:
        write(b, r).wait()


def finish(total, small, input_grad, output, micro):
    width = total.shape[-1]
    steps = 2
    turned = (micro, output.shape[2], output.size // micro // output.shape[2])
    row = jax.ShapeDtypeStruct((1, width), F32)
    vmem = pl.BlockSpec(memory_space=pltpu.VMEM)
    anywhere = pl.BlockSpec(memory_space=pl.ANY)
    return pl.pallas_call(
        finish_kernel,
        out_shape=(
            jax.ShapeDtypeStruct(turned, BF16),
            jax.ShapeDtypeStruct(turned, F32),
            row,
            row,
            jax.ShapeDtypeStruct((width, SECTIONS * width), F32),
            row,
            jax.ShapeDtypeStruct((2 * width, width), F32),
            jax.ShapeDtypeStruct((2 * width,), F32),
        ),
        in_specs=[anywhere, vmem, vmem, vmem],
        out_specs=(vmem, vmem, vmem, vmem, anywhere, vmem, anywhere, vmem),
        scratch_shapes=[
            pltpu.VMEM((6, steps, width // steps, width), BF16),
            pltpu.VMEM((6, steps, width // steps, width), F32),
            pltpu.SemaphoreType.DMA((6, steps)),
            pltpu.SemaphoreType.DMA((6, steps)),
        ],
        compiler_params=pltpu.CompilerParams(vmem_limit_bytes=60 * 1024 * 1024),
        name="finish",
    )(total, small, input_grad, output)


def on_device(
    tokens,
    cotangent,
    norm_gain,
    norm_shift,
    in_weight,
    out_bias,
    down_weight,
    hidden_bias,
    frame_device,
    tube_device,
    clip_kind,
):
    micro, rows, width = tokens.shape
    output, input_grad, total, small_total = pipeline(
        tokens,
        cotangent,
        norm_gain,
        norm_shift,
        in_weight[0],
        out_bias,
        down_weight,
        hidden_bias,
        frame_device,
        tube_device,
        clip_kind,
    )
    output, input_grad, gain, shift, weight, bias, down, hidden = finish(
        total, small_total, input_grad, output, micro
    )
    return (
        output.transpose(0, 2, 1),
        input_grad.transpose(0, 2, 1),
        gain,
        shift,
        weight[None],
        bias,
        down,
        hidden,
    )


def solution(mesh):
    return jax.shard_map(
        on_device,
        mesh=mesh,
        in_specs=(
            P(None, "dp", None),
            P(None, "dp", None),
            P("section", None),
            P("section", None),
            P("section", None, None),
            P("section", None),
            P("section", None),
            P("section"),
            P(),
            P(),
            P(),
        ),
        out_specs=(
            P(None, "dp", "section"),
            P(None, "dp", "section"),
            P("section", None),
            P("section", None),
            P("section", None, None),
            P("section", None),
            P("section", None),
            P("section"),
        ),
        check_vma=False,
    )
```

```python
import functools

import jax
import jax.numpy as jnp
from jax import lax
from jax.experimental import pallas as pl
from jax.experimental.pallas import tpu as pltpu
from jax.sharding import PartitionSpec as P

HEAD_DIM = 64
WINDOW = 256
BLOCK = 16
SECTIONS = 4
EPS = 1e-06
NEGATIVE = -1e30
MESH = pl.DeviceIdType.MESH
F32 = jnp.float32
BF16 = jnp.bfloat16


def mm(left, right):
    return lax.dot_general(left, right, (((1,), (0,)), ((), ())), preferred_element_type=F32)


def mm_nt(left, right):
    return lax.dot_general(left, right, (((1,), (1,)), ((), ())), preferred_element_type=F32)


def mm_tn(left, right):
    return lax.dot_general(left, right, (((0,), (0,)), ((), ())), preferred_element_type=F32)


def remote(src, dst, send_sem, recv_sem, section, dp):
    return pltpu.make_async_remote_copy(
        src_ref=src,
        dst_ref=dst,
        send_sem=send_sem,
        recv_sem=recv_sem,
        device_id=(section, dp),
        device_id_type=MESH,
    )


def normalise(hidden):
    average = jnp.mean(hidden, axis=-1, keepdims=True)
    centred = hidden - average
    inverse = lax.rsqrt(jnp.mean(centred * centred, axis=-1, keepdims=True) + EPS)
    return centred * inverse, inverse


def gelu_and_slope(u):
    cdf = 0.5 + 0.5 * lax.erf(u * 0.7071067811865476)
    bell = jnp.exp(-0.5 * u * u)
    return u * cdf, cdf + (0.3989422804014327 * u) * bell


def main_kernel(
    cfg,
    tok_hbm,
    cot_hbm,
    gain_ref,
    shift_ref,
    w_hbm,
    bias_ref,
    down_hbm,
    hb_ref,
    ftab,
    ttab,
    kind,
    out_ref,
    ig_ref,
    total_hbm,
    small_out,
    weights,
    keep_a,
    keep_b,
    hin,
    gin,
    leave,
    nrm,
    work,
    gcol,
    xsend,
    xrecv0,
    xrecv1,
    xrecv2,
    xrecv3,
    blocks,
    bias_early,
    bias_late,
    mask_add,
    spots,
    sources,
    guest,
    theirs,
    from_low,
    from_high,
    acc,
    small,
    small_all,
    small_pair,
    load_sem,
    w_send,
    w_recv,
    r_send,
    r_recv,
    hb_send,
    hb_recv,
    h_send,
    h_recv,
    g_send,
    g_recv,
    x_send,
    x_recv,
    o_send,
    o_recv,
    ig_send,
    ig_recv,
    sib_send,
    sib_recv,
    up_send,
    low_recv,
    down_send,
    high_recv,
    left_send,
    right_send,
    total_recv,
    pair_send,
    pair_recv,
    local_sem,
    early_send,
    early_recv,
    guest_send,
    guest_recv,
    small_send,
    small_recv,
    spair_send,
    spair_recv,
):
    n, across, repeat, slots, chunks, width, wide, depth, chunk, lag, pieces, direct = cfg
    section = lax.axis_index("section")
    me = lax.axis_index("dp")
    core = lax.rem(me, 2)
    place = lax.div(me, 2)
    places = n // 2
    sibling = me + 1 - 2 * core
    odd_place = lax.rem(place, 2)
    across_z = me + 2 - 4 * odd_place
    odd = lax.rem(section, 2)
    is_attn = odd == 0
    not_attn = odd == 1
    partner = section + 1 - 2 * odd
    is_first, is_last = lax.div(3 - section, 3), lax.div(section, 3)
    xrecv = (xrecv0, xrecv1, xrecv2, xrecv3)
    share = WINDOW // repeat
    half = wide // 2
    quarter = width // SECTIONS

    def load_columns(j):
        columns = pl.ds(j * width, width)
        return pltpu.make_async_copy(w_hbm.at[:, columns], weights.at[j], load_sem.at[j])

    def load_rows(j):
        rows = pl.ds(j * width, width)
        return pltpu.make_async_copy(down_hbm.at[rows], weights.at[6 + j], load_sem.at[6 + j])

    load_t = pltpu.make_async_copy(tok_hbm, hin, load_sem.at[5])
    load_c = pltpu.make_async_copy(cot_hbm, gin, load_sem.at[5])

    @pl.when(section == 0)
    def _():
        load_t.start()

    for j in range(4):
        load_columns(j).start()

    @pl.when(section == 3)
    def _():
        load_c.start()

    @pl.when(not_attn)
    def _():
        load_rows(0).start()
        load_rows(1).start()

    barrier = pltpu.get_barrier_semaphore()

    def greet(s, d):
        pl.semaphore_signal(barrier, inc=1, device_id=(s, d), device_id_type=MESH)

    @pl.loop(0, n)
    def _(d):
        @pl.when(d != me)
        def _():
            greet(section, d)

        @pl.when((section == 1) | (section == 2))
        def _():
            greet(3 - section, d)

    greet(partner, me)
    greet(3 - partner, me)

    @pl.when((section == 0) | (section == 3))
    def _():
        greet(3 - section, me)

    def meet():
        edge = is_first + is_last
        pl.semaphore_wait(barrier, n + 1 + edge + (1 - edge) * n)

    bias_late[...] = hb_ref[...].astype(F32).reshape(bias_late.shape)
    send_bias = remote(bias_late, bias_early, hb_send.at[0], hb_recv.at[0], partner, me)
    span = half // 4
    step_rows = span // pieces

    def parts(z_side, which_core, k):
        first = which_core * span + k * step_rows
        in_block = pl.ds(pl.multiple_of(first, step_rows), step_rows)
        in_all = pl.ds(pl.multiple_of(z_side * width + first, step_rows), step_rows)
        return down_hbm.at[in_all], weights.at[4 + z_side, in_block]

    def down_first(k):
        source, here = parts(odd_place, core, k)
        return remote(source, here, w_send.at[0, k], w_recv.at[0, k], partner, me)

    def guest_rows(k):
        return guest.at[pl.ds(pl.multiple_of(k * step_rows, step_rows), step_rows)]

    def down_round_0(k):
        source, here = parts(odd_place, core, k)
        return remote(source, here, w_send.at[0, k], r_recv.at[k], 2, me)

    def down_round_2(k):
        here = parts(odd_place, core, k)[1]
        return remote(here, guest_rows(k), r_send.at[k], r_recv.at[k], 3, me)

    def down_round_3(k):
        here = parts(odd_place, core, k)[1]
        return remote(guest_rows(k), here, r_send.at[k], w_recv.at[0, k], 1, me)

    def down_along(k):
        here = parts(odd_place, core, k)[1]
        return remote(here, here, w_send.at[1, k], w_recv.at[1, k], section, across_z)

    def down_pair(k):
        here = parts(odd_place, core, k)[1]
        return remote(here, here, w_send.at[2, k], w_recv.at[2, k], section, sibling)

    def down_last(k):
        here = parts(1 - odd_place, core, k)[1]
        return remote(here, here, w_send.at[3, k], w_recv.at[3, k], section, sibling)

    gain = gain_ref[...].astype(F32)
    shift = shift_ref[...].astype(F32)
    bias = bias_ref[...].astype(F32)
    small[...] = jnp.zeros_like(small)

    def role_of(table, micro, device):
        def step(r, found):
            return found + jnp.where(table[micro, r] == device, r, 0)

        return lax.fori_loop(0, n, step, 0)

    def make_tables(send_table, own_table):
        for m in range(2):

            @pl.loop(0, n)
            def _(d):
                spots[m, d] = lax.rem(role_of(send_table, m, d), across)

            family = lax.rem(lax.div(role_of(own_table, m, me), across), n // across)

            @pl.loop(0, across)
            def _(r):
                sources[m, r] = send_table[m, family * across + r]

    def slot_of(unit, f):
        return lax.div(unit, repeat) * repeat + f

    def share_rows(k):
        return pl.ds(pl.multiple_of(k * share, share), share)

    def unit_copy(k):
        unit, f = lax.div(k, repeat), lax.rem(k, repeat)
        return remote(
            leave.at[slot_of(unit, f), share_rows(lax.rem(unit, repeat))],
            hin.at[unit, share_rows(f)],
            h_send.at[k],
            h_recv.at[k],
            1,
            me,
        )

    def unit_back(unit, f):
        return remote(
            leave.at[unit, share_rows(f)],
            gin.at[slot_of(unit, f), share_rows(lax.rem(unit, repeat))],
            g_send.at[unit, f],
            g_recv.at[slot_of(unit, f)],
            0,
            me,
        )

    def slot_copy(c):
        return remote(leave.at[c], hin.at[c], h_send.at[c], h_recv.at[c], 3, me)

    def slot_back(c):
        return remote(leave.at[c], gin.at[c], g_send.at[c, 0], g_recv.at[c], 2, me)

    def wait_depth(c, to_section):
        @pl.when(c >= depth)
        def _():
            some = xsend.at[lax.rem(c, depth)]
            remote(some, some, x_send.at[c - depth], x_recv.at[0], to_section, me).wait_send()

    def send_share(unit, f, rows):
        micro, slot = lax.div(unit, slots), lax.rem(unit, depth)
        blocks[pl.ds(0, across)] = rows.reshape(across, BLOCK, width)

        @pl.when(f == 0)
        def _():
            wait_depth(unit, 2)

        @pl.loop(0, n)
        def _(d):
            xsend[slot, d, f] = blocks[spots[micro, d]]

        for i in range(chunks):

            @pl.when(unit == i)
            def _():
                @pl.loop(0, n)
                def _(d):
                    remote(
                        xsend.at[slot, d, f],
                        xrecv[i].at[me, f],
                        x_send.at[i],
                        x_recv.at[i],
                        2,
                        d,
                    ).start()

    def send_slot(c, rows):
        micro, slot = lax.div(c, slots), lax.rem(c, depth)
        blocks[...] = rows.reshape(blocks.shape)
        wait_depth(c, 1)

        @pl.loop(0, n)
        def _(d):
            spot = spots[micro, d]
            for f in range(repeat):
                xsend[slot, d, f] = blocks[spot * repeat + f]

        for i in range(chunks):

            @pl.when(c == i)
            def _():
                @pl.loop(0, n)
                def _(d):
                    remote(
                        xsend.at[slot, d],
                        xrecv[i].at[me],
                        x_send.at[i],
                        x_recv.at[i],
                        1,
                        d,
                    ).start()

    def gather_blocks(c, target, from_section, forward):
        for i in range(chunks):

            @pl.when(c == i)
            def _():
                remote(xrecv[i], xrecv[i], x_send.at[0], x_recv.at[i], from_section, me).wait_recv()

                @pl.loop(0, across)
                def _(r):
                    source = sources[i // slots, r]
                    for f in range(repeat):
                        block = r * repeat + f if forward else f * across + r
                        rows = pl.ds(pl.multiple_of(block * BLOCK, BLOCK), BLOCK)
                        target[i, rows] = xrecv[i][source, f]

    def norm_back(c, dn, gb):
        nh, inverse = normalise(hin[c].astype(F32))
        weighted = dn * gain
        first = jnp.mean(weighted, axis=-1, keepdims=True)
        second = jnp.mean(weighted * nh, axis=-1, keepdims=True)
        grad = gb.astype(F32) + inverse * (weighted - first - nh * second)
        small[0:1] += jnp.sum(dn * nh, axis=0, keepdims=True)
        small[1:2] += jnp.sum(dn, axis=0, keepdims=True)
        small[2:3] += jnp.sum(gb.astype(F32), axis=0, keepdims=True)
        return grad

    def ig_copy(s, c):
        return remote(gcol.at[s - 1, c], ig_ref.at[c], ig_send.at[s, c], ig_recv.at[0], s, me)

    @pl.when(is_attn)
    def _():
        lane = lax.broadcasted_iota(jnp.int32, (1, 2 * HEAD_DIM), 1)
        first_head = jnp.where(lane < HEAD_DIM, 1.0, 0.0)
        pick = [first_head.astype(BF16), (1.0 - first_head).astype(BF16)]
        scale = HEAD_DIM ** (-0.5)
        pick_scaled = [
            (first_head * scale).astype(BF16),
            ((1.0 - first_head) * scale).astype(BF16),
        ]
        key_window = lax.broadcasted_iota(jnp.int32, (WINDOW, WINDOW), 0) % 16 // 4
        query_window = lax.broadcasted_iota(jnp.int32, (WINDOW, WINDOW), 1) % 16 // 4
        barred = jnp.where(key_window == query_window, 0.0, NEGATIVE)
        for m in range(2):
            mask_add[m] = barred * kind[m].astype(F32)

        meet()

        @pl.when(section == 0)
        def _():
            @pl.loop(direct, pieces)
            def _(k):
                down_round_0(k).start()

            @pl.loop(0, direct)
            def _(k):
                down_first(k).start()

        send_bias.start()

        @pl.when(section == 2)
        def _():
            @pl.loop(direct, pieces)
            def _(k):
                down_round_0(k).wait_recv()
                down_round_2(k).start()

            @pl.loop(direct, pieces)
            def _(k):
                down_round_2(k).wait_send()

            @pl.loop(0, pieces)
            def _(k):
                down_first(k).start()

            make_tables(ftab, ttab)

        def forward(c):
            @pl.when(section == 2)
            def _():
                gather_blocks(c, hin, 1, True)

            @pl.when((section == 0) & (c == 0))
            def _():
                load_t.wait()

            micro = lax.div(c, slots)
            hidden = hin[c].astype(F32)
            nh, _ = normalise(hidden)
            normed = (nh * gain + shift).astype(BF16)
            nrm[c] = normed
            for j in range(3):
                columns = pl.ds(j * width, width)

                @pl.when(c == 0)
                def _():
                    load_columns(j).wait()

                keep_b[c, :, columns] = mm(normed, weights[j]).astype(BF16)

            @pl.when(c == 0)
            def _():
                load_columns(3).wait()


            places_at = [g * 2 * HEAD_DIM for g in range(width // (2 * HEAD_DIM))]
            scores = []
            for offset in places_at:
                q = keep_b[c, :, pl.ds(offset, 2 * HEAD_DIM)]
                k = keep_b[c, :, pl.ds(width + offset, 2 * HEAD_DIM)]
                for one in range(2):
                    scores.append(mm_nt(k, q * pick_scaled[one]))
            probs = []
            for z in scores:
                z = z + mask_add[micro]
                e = jnp.exp(z - jnp.max(z, axis=0, keepdims=True))
                p = e * (1.0 / jnp.sum(e, axis=0, keepdims=True))
                probs.append(p.astype(BF16))
            for g, offset in enumerate(places_at):
                v = keep_b[c, :, pl.ds(2 * width + offset, 2 * HEAD_DIM)]
                o = None
                for one in range(2):
                    pb = probs[2 * g + one]
                    spot = (2 * g + one) * WINDOW
                    keep_a[c, :, pl.ds(spot, WINDOW)] = pb
                    term = mm_tn(pb, v * pick[one])
                    o = term if o is None else o + term
                keep_b[c, :, pl.ds(3 * width + offset, 2 * HEAD_DIM)] = o.astype(BF16)

            branch = mm(keep_b[c, :, pl.ds(3 * width, width)], weights[3])
            leave[c] = (hin[c].astype(F32) + branch + bias).astype(BF16)

            @pl.when(section == 2)
            def _():
                slot_copy(c).start()

            @pl.when((section == 0) & (c == 0))
            def _():
                @pl.loop(0, direct)
                def _(k):
                    down_first(k).wait_send()

            @pl.when(section == 0)
            def _():
                unit_copy(c).start()

            @pl.when((section == 0) & (c == chunks - 1))
            def _():
                @pl.loop(chunks, chunks * repeat)
                def _(k):
                    unit_copy(k - 2).wait_send()
                    unit_copy(k).start()

        def backward(c):
            slot_back(c).wait_recv()
            gb = gin[c]
            work[...] = mm_nt(gb, weights[3]).astype(BF16)

            places_at = [g * 2 * HEAD_DIM for g in range(width // (2 * HEAD_DIM))]
            grads = []
            for offset in places_at:
                v = keep_b[c, :, pl.ds(2 * width + offset, 2 * HEAD_DIM)]
                go = work[:, pl.ds(offset, 2 * HEAD_DIM)]
                for one in range(2):
                    grads.append(mm_nt(v, go * pick[one]))
            for g, offset in enumerate(places_at):
                q_at = pl.ds(offset, 2 * HEAD_DIM)
                k_at = pl.ds(width + offset, 2 * HEAD_DIM)
                v_at = pl.ds(2 * width + offset, 2 * HEAD_DIM)
                q, k, go = keep_b[c, :, q_at], keep_b[c, :, k_at], work[:, q_at]
                dq = dk = dv = None
                for one in range(2):
                    spot = (2 * g + one) * WINDOW
                    pb = keep_a[c, :, pl.ds(spot, WINDOW)]
                    p = pb.astype(F32)
                    pdp = p * grads[2 * g + one]
                    ds = (pdp - p * jnp.sum(pdp, axis=0, keepdims=True)).astype(BF16)
                    tv = mm(pb, go * pick[one])
                    tk = mm(ds, q * pick_scaled[one])
                    tq = mm_tn(ds, k * pick_scaled[one])
                    dv = tv if dv is None else dv + tv
                    dk = tk if dk is None else dk + tk
                    dq = tq if dq is None else dq + tq
                keep_b[c, :, q_at] = dq.astype(BF16)
                keep_b[c, :, k_at] = dk.astype(BF16)
                keep_b[c, :, v_at] = dv.astype(BF16)

            dn = sum(mm_nt(keep_b[c, :, pl.ds(j * width, width)], weights[j]) for j in range(3))
            leaving = norm_back(c, dn, gb).astype(BF16)

            @pl.when(section == 2)
            def _():
                send_slot(c, leaving)

            @pl.when(section == 0)
            def _():
                for s in range(1, SECTIONS):
                    gcol[s - 1, c] = leaving[:, s * quarter : (s + 1) * quarter]
                ig_ref[c] = leaving[:, 0:quarter]
                for s in range(1, SECTIONS):
                    ig_copy(s, c).start()

        @pl.loop(0, 2 * chunks)
        def _(step):
            c = lax.rem(step, chunks)

            @pl.when(step < chunks)
            def _():
                forward(c)

            @pl.when(step >= chunks)
            def _():
                backward(c)

    @pl.when(not_attn)
    def _():
        meet()

        @pl.when(section == 1)
        def _():
            make_tables(ttab, ftab)

        for j in range(4):
            load_columns(j).wait()

        load_rows(0).wait()
        load_rows(1).wait()

        @pl.when(section == 3)
        def _():
            @pl.loop(direct, pieces)
            def _(k):
                down_round_2(k).wait_recv()
                down_round_3(k).start()

            @pl.loop(direct, pieces)
            def _(k):
                down_round_3(k).wait_send()

        @pl.loop(0, pieces)
        def _(k):
            down_first(k).wait_recv()
            down_along(k).start()
            down_pair(k).start()

        send_bias.wait_recv()

        @pl.when(section == 3)
        def _():
            load_c.wait()

        def forward(c, at, first):
            hidden = hin[c, at].astype(F32)
            nh, _ = normalise(hidden)
            normed = (nh * gain + shift).astype(BF16)
            nrm[c, at] = normed
            for j in range(4):
                columns = pl.ds(j * width, width)
                u = mm(normed, weights[j])
                u = u + (bias_early, bias_late)[j // 2][:, pl.ds((j % 2) * width, width)]
                active, slope = gelu_and_slope(u)
                keep_a[c, at, columns] = active.astype(BF16)
                keep_b[c, at, columns] = slope.astype(BF16)

            @pl.when(first)
            def _():
                @pl.loop(0, pieces)
                def _(k):
                    down_along(k).wait_recv()
                    down_last(k).start()

                @pl.loop(0, pieces)
                def _(k):
                    down_pair(k).wait_recv()
                    down_last(k).wait_recv()

            branch = mm(keep_a[c, at], weights[pl.ds(4, 4)].reshape(wide, width))
            return (hin[c, at].astype(F32) + branch + bias).astype(BF16)

        def forward_share(k):
            unit, f = lax.div(k, repeat), lax.rem(k, repeat)
            unit_copy(k).wait_recv()
            leaving = forward(unit, share_rows(f), k == 0)
            send_share(unit, f, leaving)

        def forward_slot(c):
            slot_copy(c).wait_recv()
            leaving = forward(c, pl.ds(0, WINDOW), c == 0)
            for s in range(SECTIONS - 1):
                gcol[s, c] = leaving[:, s * quarter : (s + 1) * quarter]
            out_ref[c] = leaving[:, (SECTIONS - 1) * quarter :]
            for s in range(SECTIONS - 1):
                remote(
                    gcol.at[s, c], out_ref.at[c], o_send.at[s, c], o_recv.at[0], s, me
                ).start()

        def backward(c):
            @pl.when(section == 1)
            def _():
                gather_blocks(c, gin, 2, False)

            gb = gin[c]
            for j in range(4):
                columns = pl.ds(j * width, width)
                da = mm_nt(gb, weights[4 + j])
                du = da * keep_b[c, :, columns].astype(F32)
                keep_b[c, :, columns] = du.astype(BF16)
                small[3 + j : 4 + j] += jnp.sum(du, axis=0, keepdims=True)
            dn = sum(mm_nt(keep_b[c, :, pl.ds(j * width, width)], weights[j]) for j in range(4))
            leave[c] = norm_back(c, dn, gb).astype(BF16)

            @pl.when(section == 3)
            def _():
                slot_back(c).start()

            @pl.when(section == 1)
            def _():
                unit_back(c, 0).start()

            @pl.when((section == 1) & (c < chunks - 1))
            def _():
                for f in range(1, repeat):
                    unit_back(c, f).start()
        @pl.when(section == 1)
        def _():
            pl.loop(0, chunks * repeat)(forward_share)

        @pl.loop(0, chunks)
        def _(c):
            @pl.when(section == 3)
            def _():
                forward_slot(c)

            backward(c)

    @pl.when(not_attn)
    def _():
        @pl.loop(0, pieces)
        def _(k):
            down_along(k).wait_send()
            down_pair(k).wait_send()
            down_last(k).wait_send()

    side = width // 2
    per_block = side // chunk
    w_chunks, d_chunks = 4 * per_block, 2 * per_block
    rows_all = chunks * WINDOW

    def grad_rows(block, first, count):
        return weights.at[block, pl.ds(pl.multiple_of(first, count), count)]

    def half_rows(block):
        return pl.ds(pl.multiple_of(block * side, side), side)

    def block_of(turn):
        last = turn + 2 * lax.div(turn, 4) - 4 * lax.div(turn, 6)
        first = turn + 3 * lax.div(turn + 7, 8) - 5 * lax.div(turn + 5, 8) + 2 * lax.div(turn, 6)
        second = odd - is_last
        return second * first + (1 - second) * last

    def sib_copy(block, source):
        return remote(
            source, theirs.at[half_rows(block)], sib_send.at[block], sib_recv.at[block], section, sibling
        )

    def outer(left, left_at, right, right_at, block):
        right_value = right[:, :, right_at].reshape(rows_all, width)

        @pl.loop(0, width // WINDOW)
        def _(k):
            columns = pl.ds(pl.multiple_of(left_at + k * WINDOW, WINDOW), WINDOW)
            left_value = left[:, :, columns].reshape(rows_all, WINDOW)
            rows = pl.ds(pl.multiple_of(k * WINDOW, WINDOW), WINDOW)
            weights[block, rows] = mm_tn(left_value, right_value).astype(BF16)

    def grad_block(turn):
        block = block_of(turn)

        @pl.when((block < 4) & (not_attn | (block < 3)))
        def _():
            columns = pl.ds(pl.multiple_of(block * width, width), width)
            outer(nrm, 0, keep_b, columns, block)

        @pl.when((block == 3) & is_attn)
        def _():
            outer(keep_b, 3 * width, gin, pl.ds(0, width), block)

        @pl.when(block >= 4)
        def _():
            outer(keep_a, (block - 4) * width, gin, pl.ds(0, width), block)

        sib_copy(block, grad_rows(block, (1 - core) * side, side)).start()

    def early_copy(at, source):
        return (
            remote(
                source,
                grad_rows(4 + at, core * side, side),
                early_send.at[at],
                early_recv.at[at],
                2,
                me,
            ),
            remote(source, guest.at[half_rows(at)], early_send.at[at], early_recv.at[at], 3, me),
        )

    def pair_sum(turn):
        block = block_of(turn)
        sib_copy(block, theirs.at[half_rows(block)]).wait_recv()

        here = grad_rows(block, core * side, side)
        value = here[...].astype(F32) + theirs[half_rows(block)].astype(F32)
        here[...] = value.astype(BF16)

        @pl.when((section == 3) & ((block == 4) | (block == 5)))
        def _():
            early_copy(block - 4, here)[0].start()

        @pl.when((section == 1) & ((block == 4) | (block == 5)))
        def _():
            early_copy(block - 4, here)[1].start()

        @pl.when((section == 1) & (block == 7))
        def _():
            early_copy(2, here)[1].start()

    small_all[me] = small[...]

    def small_copy(d):
        return remote(small, small_all.at[me], small_send.at[d], small_recv.at[0], section, d)

    @pl.loop(0, n)
    def _(d):
        @pl.when(d != me)
        def _():
            small_copy(d).start()

    own_lines = w_chunks + d_chunks
    is_second = odd - is_last
    lines = own_lines + d_chunks * (is_last - is_first) + per_block * (is_last - is_second)

    def line_rows(i):
        return pl.ds(pl.multiple_of(i * chunk, chunk), chunk)

    def with_chunk(i, use):
        slot = lax.div(i, per_block)
        first = core * side + lax.rem(i, per_block) * chunk

        @pl.when(i < own_lines)
        def _():
            block = slot + 2 * odd * lax.div(slot, 4)
            use(grad_rows(block, first, chunk))

        @pl.when(i >= own_lines)
        def _():
            use(guest.at[pl.ds(pl.multiple_of((i - own_lines) * chunk, chunk), chunk)])

    def total_rows(i):
        first = core * side + lax.rem(i, per_block) * chunk
        return total_hbm.at[lax.div(i, per_block), pl.ds(pl.multiple_of(first, chunk), chunk)]

    def low_rows(i):
        return from_low.at[line_rows(i)]

    def high_rows(i):
        return from_high.at[line_rows(i)]

    def up_copy(i, source):
        return remote(source, low_rows(i), up_send.at[i], low_recv.at[i], section, me + 2)

    def down_copy(i, source):
        return remote(source, high_rows(i), down_send.at[i], high_recv.at[i], section, me - 2)

    def left_copy(i, source, target):
        return remote(source, target, left_send.at[i], total_recv.at[i], section, me - 2)

    def right_copy(i, source, target):
        return remote(source, target, right_send.at[i], total_recv.at[i], section, me + 2)

    def pair_copy(i, source):
        return remote(source, total_rows(i), pair_send.at[i], pair_recv.at[0], section, sibling)

    def own_copy(i, source):
        return pltpu.make_async_copy(source, total_rows(i), local_sem.at[i])

    def guest_copy(k, source):
        owner = lax.div(k, d_chunks)
        home = total_rows(w_chunks + k - per_block * owner)
        return remote(source, home, guest_send.at[k], guest_recv.at[k], owner, me)

    def reduce_stage(i, root):
        def run(here):
            acc[...] = here[...].astype(F32)

            @pl.when((place <= root) & (place > 0))
            def _():
                up_copy(i, here).wait_recv()
                acc[...] += from_low[line_rows(i)].astype(F32)

            @pl.when((place >= root) & (place < places - 1))
            def _():
                down_copy(i, here).wait_recv()
                acc[...] += from_high[line_rows(i)].astype(F32)

            here[...] = acc[...].astype(BF16)

            @pl.when(place < root)
            def _():
                up_copy(i, here).start()

            @pl.when(place > root)
            def _():
                down_copy(i, here).start()

            @pl.when((place == root) & (i < own_lines))
            def _():
                @pl.when(place > 0)
                def _():
                    left_copy(i, here, total_rows(i)).start()

                @pl.when(place < places - 1)
                def _():
                    right_copy(i, here, total_rows(i)).start()

                pair_copy(i, here).start()
                own_copy(i, here).start()

            @pl.when((place == root) & (i >= own_lines))
            def _():
                @pl.when(place > 0)
                def _():
                    left_copy(i, here, high_rows(i)).start()

                @pl.when(place < places - 1)
                def _():
                    right_copy(i, here, low_rows(i)).start()

                guest_copy(i - own_lines, here).start()

        with_chunk(i, run)

    def pass_on(i, root, left_at, right_at, finish):
        @pl.when(place < root)
        def _():
            left_copy(i, left_at, left_at).wait_recv()

            @pl.when(place > 0)
            def _():
                left_copy(i, left_at, left_at).start()

            finish(left_at)

        @pl.when(place > root)
        def _():
            right_copy(i, right_at, right_at).wait_recv()

            @pl.when(place < places - 1)
            def _():
                right_copy(i, right_at, right_at).start()

            finish(right_at)

    def spread_stage(i, root):
        @pl.when(i < own_lines)
        def _():
            at = total_rows(i)
            pass_on(i, root, at, at, lambda ref: pair_copy(i, ref).start())

        @pl.when(i >= own_lines)
        def _():
            pass_on(
                i,
                root,
                high_rows(i),
                low_rows(i),
                lambda ref: guest_copy(i - own_lines, ref).start(),
            )

    to_pair = remote(small_out, small_pair, spair_send.at[0], spair_recv.at[0], partner, me)

    def sum_small():
        remote(
            small_all.at[pl.ds(0, n - 1)],
            small_all.at[pl.ds(0, n - 1)],
            small_send.at[0],
            small_recv.at[0],
            section,
            sibling,
        ).wait_recv()

        def add(d, so_far):
            return so_far + small_all[d]

        small_out[...] = lax.fori_loop(1, n, add, small_all[0])

        @pl.when(not_attn)
        def _():
            to_pair.start()

    height = places // 2
    pairs = lax.div(lines, 2)
    turns = 4 + 4 * odd

    @pl.loop(0, 1 + pairs + 2 * height * lag)
    def _(step):
        for at in range(2):
            turn = 2 * step - 1 + at

            @pl.when((turn >= 0) & (turn < turns))
            def _():
                grad_block(turn)

        if repeat > 1:

            @pl.when((section == 1) & (step == 0))
            def _():
                unit_back(chunks - 1, 0).wait_send()
                for f in range(1, repeat):
                    unit_back(chunks - 1, f).start()

        @pl.when(step == 6)
        def _():
            sum_small()

        for at in range(2):
            turn = 2 * step - 3 + at

            @pl.when((turn >= 0) & (turn < turns))
            def _():
                pair_sum(turn)

        for at in range(3):
            arrived = early_copy(min(at, 1), theirs.at[half_rows(at)])[0]
            if at == 2:
                arrived = early_copy(at, theirs.at[half_rows(at)])[1]
            else:

                @pl.when((section == 2) & (step == 1 + (4 + at) * per_block // 2))
                def _():
                    arrived.wait_recv()

            @pl.when((section == 3) & (step == 1 + (6 + at) * per_block // 2))
            def _():
                arrived.wait_recv()

        for stream in range(2):
            root = height - 1 + stream
            now = step - 1 - lag * (height - jnp.abs(place - root))

            @pl.when((now >= 0) & (now < pairs))
            def _():
                reduce_stage(2 * now + stream, root)

        for stream in range(2):
            root = height - 1 + stream
            past = step - 1 - lag * (height + jnp.abs(place - root))

            @pl.when((past >= 0) & (past < pairs))
            def _():
                spread_stage(2 * past + stream, root)

    @pl.when(section < 2)
    def _():
        @pl.loop(lines, own_lines)
        def _(i):
            here = total_rows(i)
            guest_copy(i - w_chunks + per_block * odd, here).wait_recv()
            pair_copy(i, here).start()

    @pl.when(not_attn)
    def _():
        to_pair.wait_send()

    @pl.when(is_attn)
    def _():
        to_pair.wait_recv()
        small_out[5:7] = small_pair[3:5]

    @pl.loop(0, lines)
    def _(i):
        some = low_rows(i)

        for stream in range(2):
            root = height - 1 + stream

            @pl.when(lax.rem(i, 2) == stream)
            def _():
                @pl.when(place < root)
                def _():
                    up_copy(i, some).wait_send()

                @pl.when(place > root)
                def _():
                    down_copy(i, some).wait_send()

                @pl.when((place <= root) & (place > 0))
                def _():
                    left_copy(i, some, some).wait_send()

                @pl.when((place >= root) & (place < places - 1))
                def _():
                    right_copy(i, some, some).wait_send()

                @pl.when((place == root) & (i < own_lines))
                def _():
                    own_copy(i, some).wait()

        @pl.when(i < own_lines)
        def _():
            pair_copy(i, some).wait_send()

        @pl.when(i >= own_lines)
        def _():
            guest_copy(i - own_lines, some).wait_send()

    @pl.when(section < 2)
    def _():
        @pl.loop(lines, own_lines)
        def _(i):
            pair_copy(i, low_rows(i)).wait_send()

    @pl.loop(0, turns)
    def _(turn):
        block = block_of(turn)
        sib_copy(block, theirs.at[half_rows(block)]).wait_send()

    @pl.loop(0, n)
    def _(d):
        @pl.when(d != me)
        def _():
            small_copy(d).wait_send()

    @pl.when(is_attn)
    def _():
        @pl.loop(direct * is_first, pieces)
        def _(k):
            down_first(k).wait_send()

        send_bias.wait_send()

        @pl.when(section == 0)
        def _():
            @pl.loop(0, chunks - 2)
            def _(k):
                unit_copy(k).wait_send()

            @pl.loop(chunks * repeat - 2, chunks * repeat)
            def _(k):
                unit_copy(k).wait_send()

        @pl.when(section == 2)
        def _():
            @pl.loop(0, chunks)
            def _(c):
                slot_copy(c).wait_send()

    @pl.when(not_attn)
    def _():
        for at in range(2):
            early_copy(at, theirs.at[half_rows(at)])[0].wait_send()

        @pl.when(section == 1)
        def _():
            early_copy(2, theirs.at[half_rows(2)])[1].wait_send()

        @pl.when(section == 3)
        def _():
            @pl.loop(0, chunks)
            def _(c):
                slot_back(c).wait_send()

        @pl.when(section == 1)
        def _():
            @pl.loop(0, chunks - 1)
            def _(c):
                for f in range(repeat):
                    unit_back(c, f).wait_send()

            for f in range(min(1, repeat - 1), repeat):
                unit_back(chunks - 1, f).wait_send()

    @pl.when((section == 1) | (section == 2))
    def _():
        @pl.loop(chunks - depth, chunks)
        def _(c):
            slot = lax.rem(c, depth)
            remote(
                xsend.at[slot], xsend.at[slot], x_send.at[c], x_recv.at[0], 3 - section, me
            ).wait_send()

    @pl.when(section == 3)
    def _():
        @pl.loop(0, chunks)
        def _(c):
            for s in range(SECTIONS - 1):
                remote(
                    gcol.at[s, c], out_ref.at[c], o_send.at[s, c], o_recv.at[0], s, me
                ).wait_send()

    @pl.when(section != 3)
    def _():
        remote(out_ref, out_ref, o_send.at[0, 0], o_recv.at[0], 3, me).wait_recv()

    @pl.when(section == 0)
    def _():
        @pl.loop(0, chunks)
        def _(c):
            for s in range(1, SECTIONS):
                ig_copy(s, c).wait_send()

    @pl.when(section != 0)
    def _():
        remote(ig_ref, ig_ref, ig_send.at[0, 0], ig_recv.at[0], 0, me).wait_recv()

    remote(
        total_hbm.at[pl.ds(0, 3)],
        total_hbm.at[pl.ds(0, 3)],
        pair_send.at[0],
        pair_recv.at[0],
        section,
        sibling,
    ).wait_recv()


def pipeline(
    tokens, cotangent, gain, shift, weight, bias, down, hidden_bias, ftab, ttab, kind, chunk=96, lag=1
):
    micro, rows, width = tokens.shape
    wide = weight.shape[1]
    n = lax.axis_size("dp")
    across = min(n, 16)
    repeat = 16 // across
    slots = rows // WINDOW
    chunks = micro * slots
    quarter = width // SECTIONS
    depth = chunks if n <= 8 else 1
    pieces, direct = 8, 6
    cfg = (n, across, repeat, slots, chunks, width, wide, depth, chunk, lag, pieces, direct)
    vmem = pl.BlockSpec(memory_space=pltpu.VMEM)
    smem = pl.BlockSpec(memory_space=pltpu.SMEM)
    anywhere = pl.BlockSpec(memory_space=pl.ANY)
    dma = pltpu.SemaphoreType.DMA
    chunked = (chunks, WINDOW, width)
    side = width // 2
    lines = 9 * side // chunk
    per_chunk = [dma((lines,)) for _ in range(8)]
    return pl.pallas_call(
        functools.partial(main_kernel, cfg),
        out_shape=(
            jax.ShapeDtypeStruct((chunks, WINDOW, quarter), BF16),
            jax.ShapeDtypeStruct((chunks, WINDOW, quarter), BF16),
            jax.ShapeDtypeStruct((6, width, width), BF16),
            jax.ShapeDtypeStruct((8, width), F32),
        ),
        in_specs=[anywhere, anywhere, vmem, vmem, anywhere, vmem, anywhere, vmem, smem, smem, smem],
        out_specs=(vmem, vmem, anywhere, vmem),
        scratch_shapes=[
            pltpu.VMEM((8, width, width), BF16),
            pltpu.VMEM((chunks, WINDOW, wide), BF16),
            pltpu.VMEM((chunks, WINDOW, wide), BF16),
            pltpu.VMEM(chunked, BF16),
            pltpu.VMEM(chunked, BF16),
            pltpu.VMEM(chunked, BF16),
            pltpu.VMEM(chunked, BF16),
            pltpu.VMEM((WINDOW, width), BF16),
            pltpu.VMEM((SECTIONS - 1, chunks, WINDOW, quarter), BF16),
            pltpu.VMEM((depth, n, repeat, BLOCK, width), BF16),
            *[pltpu.VMEM((n, repeat, BLOCK, width), BF16) for _ in range(4)],
            pltpu.VMEM((WINDOW // BLOCK, BLOCK, width), BF16),
            pltpu.VMEM((1, wide // 2), F32),
            pltpu.VMEM((1, wide // 2), F32),
            pltpu.VMEM((2, WINDOW, WINDOW), F32),
            pltpu.SMEM((2, n), jnp.int32),
            pltpu.SMEM((2, across), jnp.int32),
            pltpu.VMEM((3 * side, width), BF16),
            pltpu.VMEM((8 * side, width), BF16),
            pltpu.VMEM((lines * chunk, width), BF16),
            pltpu.VMEM((lines * chunk, width), BF16),
            pltpu.VMEM((chunk, width), F32),
            pltpu.VMEM((8, width), F32),
            pltpu.VMEM((n, 8, width), F32),
            pltpu.VMEM((8, width), F32),
            dma((8,)),
            dma((4, pieces)),
            dma((4, pieces)),
            dma((pieces,)),
            dma((pieces,)),
            dma((1,)),
            dma((1,)),
            dma((chunks * repeat,)),
            dma((chunks * repeat,)),
            dma((chunks, repeat)),
            dma((chunks,)),
            dma((chunks,)),
            dma((chunks,)),
            dma((SECTIONS - 1, chunks)),
            dma((1,)),
            dma((SECTIONS, chunks)),
            dma((1,)),
            dma((8,)),
            dma((8,)),
            *per_chunk,
            dma((1,)),
            dma((lines,)),
            dma((3,)),
            dma((3,)),
            dma((lines // 3,)),
            dma((lines // 3,)),
            dma((n,)),
            dma((1,)),
            dma((1,)),
            dma((1,)),
        ],
        compiler_params=pltpu.CompilerParams(
            collective_id=0, has_side_effects=True, vmem_limit_bytes=63 * 1024 * 1024
        ),
        name="pipeline",
    )(
        tokens.reshape(chunked),
        cotangent.reshape(chunked),
        gain,
        shift,
        weight,
        bias,
        down,
        hidden_bias,
        ftab,
        ttab,
        kind,
    )


def finish_kernel(
    total_hbm,
    small_ref,
    ig_ref,
    out_ref,
    output,
    input_grad,
    gain,
    shift,
    weight_hbm,
    bias,
    down_hbm,
    hidden,
    short,
    full,
    in_sem,
    out_sem,
):
    width = total_hbm.shape[2]
    steps = short.shape[1]
    span = width // steps
    order = [(b, r) for b in range(6) for r in range(steps)]

    def read(b, r):
        rows = pl.ds(r * span, span)
        return pltpu.make_async_copy(total_hbm.at[b, rows], short.at[b, r], in_sem.at[b, r])

    def write(b, r):
        if b < 4:
            target = weight_hbm.at[pl.ds(r * span, span), pl.ds(b * width, width)]
        else:
            target = down_hbm.at[pl.ds((b - 4) * width + r * span, span)]
        return pltpu.make_async_copy(full.at[b, r], target, out_sem.at[b, r])

    for b, r in order:
        read(b, r).start()
    for b, r in order:
        read(b, r).wait()
        full[b, r] = short[b, r].astype(F32)
        write(b, r).start()
    slots = output.shape[2] // WINDOW
    for c in range(out_ref.shape[0]):
        at = pl.ds(c % slots * WINDOW, WINDOW)
        output[c // slots, :, at] = out_ref[c].T
        input_grad[c // slots, :, at] = ig_ref[c].astype(F32).T
    gain[...] = small_ref[0:1]
    shift[...] = small_ref[1:2]
    bias[...] = small_ref[2:3]
    for k in range(2):
        hidden[pl.ds(k * width, width)] = small_ref[5 + k]
    for b, r in order:
        write(b, r).wait()


def finish(total, small, input_grad, output, micro):
    width = total.shape[-1]
    steps = 2
    turned = (micro, output.shape[2], output.size // micro // output.shape[2])
    row = jax.ShapeDtypeStruct((1, width), F32)
    vmem = pl.BlockSpec(memory_space=pltpu.VMEM)
    anywhere = pl.BlockSpec(memory_space=pl.ANY)
    return pl.pallas_call(
        finish_kernel,
        out_shape=(
            jax.ShapeDtypeStruct(turned, BF16),
            jax.ShapeDtypeStruct(turned, F32),
            row,
            row,
            jax.ShapeDtypeStruct((width, SECTIONS * width), F32),
            row,
            jax.ShapeDtypeStruct((2 * width, width), F32),
            jax.ShapeDtypeStruct((2 * width,), F32),
        ),
        in_specs=[anywhere, vmem, vmem, vmem],
        out_specs=(vmem, vmem, vmem, vmem, anywhere, vmem, anywhere, vmem),
        scratch_shapes=[
            pltpu.VMEM((6, steps, width // steps, width), BF16),
            pltpu.VMEM((6, steps, width // steps, width), F32),
            pltpu.SemaphoreType.DMA((6, steps)),
            pltpu.SemaphoreType.DMA((6, steps)),
        ],
        compiler_params=pltpu.CompilerParams(vmem_limit_bytes=60 * 1024 * 1024),
        name="finish",
    )(total, small, input_grad, output)


def on_device(
    tokens,
    cotangent,
    norm_gain,
    norm_shift,
    in_weight,
    out_bias,
    down_weight,
    hidden_bias,
    frame_device,
    tube_device,
    clip_kind,
):
    micro, rows, width = tokens.shape
    output, input_grad, total, small_total = pipeline(
        tokens,
        cotangent,
        norm_gain,
        norm_shift,
        in_weight[0],
        out_bias,
        down_weight,
        hidden_bias,
        frame_device,
        tube_device,
        clip_kind,
    )
    output, input_grad, gain, shift, weight, bias, down, hidden = finish(
        total, small_total, input_grad, output, micro
    )
    return (
        output.transpose(0, 2, 1),
        input_grad.transpose(0, 2, 1),
        gain,
        shift,
        weight[None],
        bias,
        down,
        hidden,
    )


def solution(mesh):
    return jax.shard_map(
        on_device,
        mesh=mesh,
        in_specs=(
            P(None, "dp", None),
            P(None, "dp", None),
            P("section", None),
            P("section", None),
            P("section", None, None),
            P("section", None),
            P("section", None),
            P("section"),
            P(),
            P(),
            P(),
        ),
        out_specs=(
            P(None, "dp", "section"),
            P(None, "dp", "section"),
            P("section", None),
            P("section", None),
            P("section", None, None),
            P("section", None),
            P("section", None),
            P("section"),
        ),
        check_vma=False,
    )
```

```python
import functools

import jax
import jax.numpy as jnp
from jax import lax
from jax.experimental import pallas as pl
from jax.experimental.pallas import tpu as pltpu
from jax.sharding import PartitionSpec as P

HEAD_DIM = 64
WINDOW = 256
BLOCK = 16
SECTIONS = 4
EPS = 1e-06
NEGATIVE = -1e30
MESH = pl.DeviceIdType.MESH
F32 = jnp.float32
BF16 = jnp.bfloat16


def mm(left, right):
    return lax.dot_general(left, right, (((1,), (0,)), ((), ())), preferred_element_type=F32)


def mm_nt(left, right):
    return lax.dot_general(left, right, (((1,), (1,)), ((), ())), preferred_element_type=F32)


def mm_tn(left, right):
    return lax.dot_general(left, right, (((0,), (0,)), ((), ())), preferred_element_type=F32)


def remote(src, dst, send_sem, recv_sem, section, dp):
    return pltpu.make_async_remote_copy(
        src_ref=src,
        dst_ref=dst,
        send_sem=send_sem,
        recv_sem=recv_sem,
        device_id=(section, dp),
        device_id_type=MESH,
    )


def normalise(hidden):
    average = jnp.mean(hidden, axis=-1, keepdims=True)
    centred = hidden - average
    inverse = lax.rsqrt(jnp.mean(centred * centred, axis=-1, keepdims=True) + EPS)
    return centred * inverse, inverse


def gelu_and_slope(u):
    cdf = 0.5 + 0.5 * lax.erf(u * 0.7071067811865476)
    bell = jnp.exp(-0.5 * u * u)
    return u * cdf, cdf + (0.3989422804014327 * u) * bell


def main_kernel(
    cfg,
    tok_hbm,
    cot_hbm,
    gain_ref,
    shift_ref,
    w_hbm,
    bias_ref,
    down_hbm,
    hb_ref,
    ftab,
    ttab,
    kind,
    out_ref,
    ig_ref,
    total_hbm,
    small_out,
    weights,
    keep_a,
    keep_b,
    hin,
    gin,
    leave,
    nrm,
    work,
    gcol,
    xsend,
    xrecv0,
    xrecv1,
    xrecv2,
    xrecv3,
    blocks,
    bias_early,
    bias_late,
    mask_add,
    spots,
    sources,
    guest,
    theirs,
    from_low,
    from_high,
    acc,
    small,
    small_all,
    small_pair,
    load_sem,
    w_send,
    w_recv,
    r_send,
    r_recv,
    hb_send,
    hb_recv,
    h_send,
    h_recv,
    g_send,
    g_recv,
    x_send,
    x_recv,
    o_send,
    o_recv,
    ig_send,
    ig_recv,
    sib_send,
    sib_recv,
    up_send,
    low_recv,
    down_send,
    high_recv,
    left_send,
    right_send,
    total_recv,
    pair_send,
    pair_recv,
    local_sem,
    early_send,
    early_recv,
    guest_send,
    guest_recv,
    small_send,
    small_recv,
    spair_send,
    spair_recv,
):
    n, across, repeat, slots, chunks, width, wide, depth, chunk, lag, pieces, direct = cfg
    section = lax.axis_index("section")
    me = lax.axis_index("dp")
    core = lax.rem(me, 2)
    place = lax.div(me, 2)
    places = n // 2
    sibling = me + 1 - 2 * core
    odd_place = lax.rem(place, 2)
    across_z = me + 2 - 4 * odd_place
    odd = lax.rem(section, 2)
    is_attn = odd == 0
    not_attn = odd == 1
    partner = section + 1 - 2 * odd
    is_first, is_last = lax.div(3 - section, 3), lax.div(section, 3)
    xrecv = (xrecv0, xrecv1, xrecv2, xrecv3)
    share = WINDOW // repeat
    few = n <= 8
    half = wide // 2
    quarter = width // SECTIONS

    barrier = pltpu.get_barrier_semaphore()

    def greet(s, d):
        pl.semaphore_signal(barrier, inc=1, device_id=(s, d), device_id_type=MESH)

    greet(partner, me)
    greet(3 - partner, me)

    @pl.when((section == 0) | (section == 3))
    def _():
        greet(3 - section, me)

    @pl.loop(0, n, unroll=few)
    def _(d):
        @pl.when(d != me)
        def _():
            greet(section, d)

        @pl.when((section == 1) | (section == 2))
        def _():
            greet(3 - section, d)

    def load_columns(j):
        columns = pl.ds(j * width, width)
        return pltpu.make_async_copy(w_hbm.at[:, columns], weights.at[j], load_sem.at[j])

    def load_rows(j):
        rows = pl.ds(j * width, width)
        return pltpu.make_async_copy(down_hbm.at[rows], weights.at[6 + j], load_sem.at[6 + j])

    load_t = pltpu.make_async_copy(tok_hbm, hin, load_sem.at[5])
    load_c = pltpu.make_async_copy(cot_hbm, gin, load_sem.at[5])

    @pl.when(section == 0)
    def _():
        load_t.start()

    for j in range(4):
        load_columns(j).start()

    @pl.when(section == 3)
    def _():
        load_c.start()

    @pl.when(not_attn)
    def _():
        load_rows(0).start()
        load_rows(1).start()

    def meet():
        edge = is_first + is_last
        pl.semaphore_wait(barrier, n + 1 + edge + (1 - edge) * n)

    bias_late[...] = hb_ref[...].astype(F32).reshape(bias_late.shape)
    send_bias = remote(bias_late, bias_early, hb_send.at[0], hb_recv.at[0], partner, me)
    span = half // 4
    step_rows = span // pieces

    def parts(z_side, which_core, k):
        first = which_core * span + k * step_rows
        in_block = pl.ds(pl.multiple_of(first, step_rows), step_rows)
        in_all = pl.ds(pl.multiple_of(z_side * width + first, step_rows), step_rows)
        return down_hbm.at[in_all], weights.at[4 + z_side, in_block]

    def down_first(k):
        source, here = parts(odd_place, core, k)
        return remote(source, here, w_send.at[0, k], w_recv.at[0, k], partner, me)

    def guest_rows(k):
        return guest.at[pl.ds(pl.multiple_of(k * step_rows, step_rows), step_rows)]

    def down_round_0(k):
        source, here = parts(odd_place, core, k)
        return remote(source, here, w_send.at[0, k], r_recv.at[k], 2, me)

    def down_round_2(k):
        here = parts(odd_place, core, k)[1]
        return remote(here, guest_rows(k), r_send.at[k], r_recv.at[k], 3, me)

    def down_round_3(k):
        here = parts(odd_place, core, k)[1]
        return remote(guest_rows(k), here, r_send.at[k], w_recv.at[0, k], 1, me)

    def down_along(k):
        here = parts(odd_place, core, k)[1]
        return remote(here, here, w_send.at[1, k], w_recv.at[1, k], section, across_z)

    def down_pair(k):
        here = parts(odd_place, core, k)[1]
        return remote(here, here, w_send.at[2, k], w_recv.at[2, k], section, sibling)

    def down_last(k):
        here = parts(1 - odd_place, core, k)[1]
        return remote(here, here, w_send.at[3, k], w_recv.at[3, k], section, sibling)

    gain = gain_ref[...].astype(F32)
    shift = shift_ref[...].astype(F32)
    bias = bias_ref[...].astype(F32)
    small[...] = jnp.zeros_like(small)

    def role_of(table, micro, device):
        def step(r, found):
            return found + jnp.where(table[micro, r] == device, r, 0)

        return lax.fori_loop(0, n, step, 0)

    def make_tables(send_table, own_table):
        for m in range(2):

            @pl.loop(0, n)
            def _(d):
                spots[m, d] = lax.rem(role_of(send_table, m, d), across)

            family = lax.rem(lax.div(role_of(own_table, m, me), across), n // across)

            @pl.loop(0, across)
            def _(r):
                sources[m, r] = send_table[m, family * across + r]

    def slot_of(unit, f):
        return lax.div(unit, repeat) * repeat + f

    def share_rows(k):
        return pl.ds(pl.multiple_of(k * share, share), share)

    def unit_copy(k):
        unit, f = lax.div(k, repeat), lax.rem(k, repeat)
        return remote(
            leave.at[slot_of(unit, f), share_rows(lax.rem(unit, repeat))],
            hin.at[unit, share_rows(f)],
            h_send.at[k],
            h_recv.at[k],
            1,
            me,
        )

    def unit_back(unit, f):
        return remote(
            leave.at[unit, share_rows(f)],
            gin.at[slot_of(unit, f), share_rows(lax.rem(unit, repeat))],
            g_send.at[unit, f],
            g_recv.at[slot_of(unit, f)],
            0,
            me,
        )

    def slot_copy(c):
        return remote(leave.at[c], hin.at[c], h_send.at[c], h_recv.at[c], 3, me)

    def slot_back(c):
        return remote(leave.at[c], gin.at[c], g_send.at[c, 0], g_recv.at[c], 2, me)

    def wait_depth(c, to_section):
        @pl.when(c >= depth)
        def _():
            some = xsend.at[lax.rem(c, depth)]
            remote(some, some, x_send.at[c - depth], x_recv.at[0], to_section, me).wait_send()

    def send_share(unit, f, rows):
        micro, slot = lax.div(unit, slots), lax.rem(unit, depth)
        blocks[pl.ds(0, across)] = rows.reshape(across, BLOCK, width)

        @pl.when(f == 0)
        def _():
            wait_depth(unit, 2)

        @pl.loop(0, n, unroll=few)
        def _(d):
            xsend[slot, d, f] = blocks[spots[micro, d]]

        for i in range(chunks):

            @pl.when(unit == i)
            def _():
                @pl.loop(0, n, unroll=few)
                def _(d):
                    remote(
                        xsend.at[slot, d, f],
                        xrecv[i].at[me, f],
                        x_send.at[i],
                        x_recv.at[i],
                        2,
                        d,
                    ).start()

    def send_slot(c, rows):
        micro, slot = lax.div(c, slots), lax.rem(c, depth)
        blocks[...] = rows.reshape(blocks.shape)
        wait_depth(c, 1)

        @pl.loop(0, n, unroll=few)
        def _(d):
            spot = spots[micro, d]
            for f in range(repeat):
                xsend[slot, d, f] = blocks[spot * repeat + f]

        for i in range(chunks):

            @pl.when(c == i)
            def _():
                @pl.loop(0, n, unroll=few)
                def _(d):
                    remote(
                        xsend.at[slot, d],
                        xrecv[i].at[me],
                        x_send.at[i],
                        x_recv.at[i],
                        1,
                        d,
                    ).start()

    def gather_blocks(c, target, from_section, forward):
        for i in range(chunks):

            @pl.when(c == i)
            def _():
                remote(xrecv[i], xrecv[i], x_send.at[0], x_recv.at[i], from_section, me).wait_recv()

                @pl.loop(0, across, unroll=few)
                def _(r):
                    source = sources[i // slots, r]
                    for f in range(repeat):
                        block = r * repeat + f if forward else f * across + r
                        rows = pl.ds(pl.multiple_of(block * BLOCK, BLOCK), BLOCK)
                        target[i, rows] = xrecv[i][source, f]

    def norm_back(c, dn, gb):
        nh, inverse = normalise(hin[c].astype(F32))
        weighted = dn * gain
        first = jnp.mean(weighted, axis=-1, keepdims=True)
        second = jnp.mean(weighted * nh, axis=-1, keepdims=True)
        grad = gb.astype(F32) + inverse * (weighted - first - nh * second)
        small[0:1] += jnp.sum(dn * nh, axis=0, keepdims=True)
        small[1:2] += jnp.sum(dn, axis=0, keepdims=True)
        small[2:3] += jnp.sum(gb.astype(F32), axis=0, keepdims=True)
        return grad

    def ig_copy(s, c):
        return remote(gcol.at[s - 1, c], ig_ref.at[c], ig_send.at[s, c], ig_recv.at[0], s, me)

    @pl.when(is_attn)
    def _():
        lane = lax.broadcasted_iota(jnp.int32, (1, 2 * HEAD_DIM), 1)
        first_head = jnp.where(lane < HEAD_DIM, 1.0, 0.0)
        pick = [first_head.astype(BF16), (1.0 - first_head).astype(BF16)]
        scale = HEAD_DIM ** (-0.5)
        pick_scaled = [
            (first_head * scale).astype(BF16),
            ((1.0 - first_head) * scale).astype(BF16),
        ]
        key_window = lax.broadcasted_iota(jnp.int32, (WINDOW, WINDOW), 0) % 16 // 4
        query_window = lax.broadcasted_iota(jnp.int32, (WINDOW, WINDOW), 1) % 16 // 4
        barred = jnp.where(key_window == query_window, 0.0, NEGATIVE)
        for m in range(2):
            mask_add[m] = barred * kind[m].astype(F32)

        meet()

        @pl.when(section == 0)
        def _():
            @pl.loop(direct, pieces)
            def _(k):
                down_round_0(k).start()

            @pl.loop(0, direct)
            def _(k):
                down_first(k).start()

        send_bias.start()

        @pl.when(section == 2)
        def _():
            @pl.loop(direct, pieces)
            def _(k):
                down_round_0(k).wait_recv()
                down_round_2(k).start()

            @pl.loop(direct, pieces)
            def _(k):
                down_round_2(k).wait_send()

            @pl.loop(0, pieces)
            def _(k):
                down_first(k).start()

            make_tables(ftab, ttab)

        def forward(c):
            @pl.when(section == 2)
            def _():
                gather_blocks(c, hin, 1, True)

            @pl.when((section == 0) & (c == 0))
            def _():
                load_t.wait()

            micro = lax.div(c, slots)
            hidden = hin[c].astype(F32)
            nh, _ = normalise(hidden)
            normed = (nh * gain + shift).astype(BF16)
            nrm[c] = normed
            for j in range(3):
                columns = pl.ds(j * width, width)

                @pl.when(c == 0)
                def _():
                    load_columns(j).wait()

                keep_b[c, :, columns] = mm(normed, weights[j]).astype(BF16)

            @pl.when(c == 0)
            def _():
                load_columns(3).wait()


            places_at = [g * 2 * HEAD_DIM for g in range(width // (2 * HEAD_DIM))]
            scores = []
            for offset in places_at:
                q = keep_b[c, :, pl.ds(offset, 2 * HEAD_DIM)]
                k = keep_b[c, :, pl.ds(width + offset, 2 * HEAD_DIM)]
                for one in range(2):
                    scores.append(mm_nt(k, q * pick_scaled[one]))
            probs = []
            for z in scores:
                z = z + mask_add[micro]
                e = jnp.exp(z - jnp.max(z, axis=0, keepdims=True))
                p = e * (1.0 / jnp.sum(e, axis=0, keepdims=True))
                probs.append(p.astype(BF16))
            for g, offset in enumerate(places_at):
                v = keep_b[c, :, pl.ds(2 * width + offset, 2 * HEAD_DIM)]
                o = None
                for one in range(2):
                    pb = probs[2 * g + one]
                    spot = (2 * g + one) * WINDOW
                    keep_a[c, :, pl.ds(spot, WINDOW)] = pb
                    term = mm_tn(pb, v * pick[one])
                    o = term if o is None else o + term
                keep_b[c, :, pl.ds(3 * width + offset, 2 * HEAD_DIM)] = o.astype(BF16)

            branch = mm(keep_b[c, :, pl.ds(3 * width, width)], weights[3])
            leave[c] = (hin[c].astype(F32) + branch + bias).astype(BF16)

            @pl.when(section == 2)
            def _():
                slot_copy(c).start()

            @pl.when((section == 0) & (c == 0))
            def _():
                @pl.loop(0, direct)
                def _(k):
                    down_first(k).wait_send()

            @pl.when(section == 0)
            def _():
                unit_copy(c).start()

            @pl.when((section == 0) & (c == chunks - 1))
            def _():
                @pl.loop(chunks, chunks * repeat)
                def _(k):
                    unit_copy(k - 2).wait_send()
                    unit_copy(k).start()

        def backward(c):
            slot_back(c).wait_recv()
            gb = gin[c]
            work[...] = mm_nt(gb, weights[3]).astype(BF16)

            places_at = [g * 2 * HEAD_DIM for g in range(width // (2 * HEAD_DIM))]
            grads = []
            for offset in places_at:
                v = keep_b[c, :, pl.ds(2 * width + offset, 2 * HEAD_DIM)]
                go = work[:, pl.ds(offset, 2 * HEAD_DIM)]
                for one in range(2):
                    grads.append(mm_nt(v, go * pick[one]))
            for g, offset in enumerate(places_at):
                q_at = pl.ds(offset, 2 * HEAD_DIM)
                k_at = pl.ds(width + offset, 2 * HEAD_DIM)
                v_at = pl.ds(2 * width + offset, 2 * HEAD_DIM)
                q, k, go = keep_b[c, :, q_at], keep_b[c, :, k_at], work[:, q_at]
                dq = dk = dv = None
                for one in range(2):
                    spot = (2 * g + one) * WINDOW
                    pb = keep_a[c, :, pl.ds(spot, WINDOW)]
                    p = pb.astype(F32)
                    pdp = p * grads[2 * g + one]
                    ds = (pdp - p * jnp.sum(pdp, axis=0, keepdims=True)).astype(BF16)
                    tv = mm(pb, go * pick[one])
                    tk = mm(ds, q * pick_scaled[one])
                    tq = mm_tn(ds, k * pick_scaled[one])
                    dv = tv if dv is None else dv + tv
                    dk = tk if dk is None else dk + tk
                    dq = tq if dq is None else dq + tq
                keep_b[c, :, q_at] = dq.astype(BF16)
                keep_b[c, :, k_at] = dk.astype(BF16)
                keep_b[c, :, v_at] = dv.astype(BF16)

            dn = sum(mm_nt(keep_b[c, :, pl.ds(j * width, width)], weights[j]) for j in range(3))
            leaving = norm_back(c, dn, gb).astype(BF16)

            @pl.when(section == 2)
            def _():
                send_slot(c, leaving)

            @pl.when(section == 0)
            def _():
                for s in range(1, SECTIONS):
                    gcol[s - 1, c] = leaving[:, s * quarter : (s + 1) * quarter]
                ig_ref[c] = leaving[:, 0:quarter]
                for s in range(1, SECTIONS):
                    ig_copy(s, c).start()

        @pl.loop(0, 2 * chunks)
        def _(step):
            c = lax.rem(step, chunks)

            @pl.when(step < chunks)
            def _():
                forward(c)

            @pl.when(step >= chunks)
            def _():
                backward(c)

    @pl.when(not_attn)
    def _():
        meet()

        @pl.when(section == 1)
        def _():
            make_tables(ttab, ftab)

        for j in range(4):
            load_columns(j).wait()

        load_rows(0).wait()
        load_rows(1).wait()

        @pl.when(section == 3)
        def _():
            @pl.loop(direct, pieces)
            def _(k):
                down_round_2(k).wait_recv()
                down_round_3(k).start()

            @pl.loop(direct, pieces)
            def _(k):
                down_round_3(k).wait_send()

        @pl.loop(0, pieces)
        def _(k):
            down_first(k).wait_recv()
            down_along(k).start()
            down_pair(k).start()

        send_bias.wait_recv()

        @pl.when(section == 3)
        def _():
            load_c.wait()

        def forward(c, at, first):
            hidden = hin[c, at].astype(F32)
            nh, _ = normalise(hidden)
            normed = (nh * gain + shift).astype(BF16)
            nrm[c, at] = normed
            for j in range(4):
                columns = pl.ds(j * width, width)
                u = mm(normed, weights[j])
                u = u + (bias_early, bias_late)[j // 2][:, pl.ds((j % 2) * width, width)]
                active, slope = gelu_and_slope(u)
                keep_a[c, at, columns] = active.astype(BF16)
                keep_b[c, at, columns] = slope.astype(BF16)

            @pl.when(first)
            def _():
                @pl.loop(0, pieces)
                def _(k):
                    down_along(k).wait_recv()
                    down_last(k).start()

                @pl.loop(0, pieces)
                def _(k):
                    down_pair(k).wait_recv()
                    down_last(k).wait_recv()

            branch = mm(keep_a[c, at], weights[pl.ds(4, 4)].reshape(wide, width))
            return (hin[c, at].astype(F32) + branch + bias).astype(BF16)

        def forward_share(k):
            unit, f = lax.div(k, repeat), lax.rem(k, repeat)
            unit_copy(k).wait_recv()
            leaving = forward(unit, share_rows(f), k == 0)
            send_share(unit, f, leaving)

        def forward_slot(c):
            slot_copy(c).wait_recv()
            leaving = forward(c, pl.ds(0, WINDOW), c == 0)
            for s in range(SECTIONS - 1):
                gcol[s, c] = leaving[:, s * quarter : (s + 1) * quarter]
            out_ref[c] = leaving[:, (SECTIONS - 1) * quarter :]

        def backward(c):
            @pl.when(section == 1)
            def _():
                gather_blocks(c, gin, 2, False)

            gb = gin[c]
            for j in range(4):
                columns = pl.ds(j * width, width)
                da = mm_nt(gb, weights[4 + j])
                du = da * keep_b[c, :, columns].astype(F32)
                keep_b[c, :, columns] = du.astype(BF16)
                small[3 + j : 4 + j] += jnp.sum(du, axis=0, keepdims=True)
            dn = sum(mm_nt(keep_b[c, :, pl.ds(j * width, width)], weights[j]) for j in range(4))
            leave[c] = norm_back(c, dn, gb).astype(BF16)

            @pl.when(section == 3)
            def _():
                slot_back(c).start()

            @pl.when(section == 1)
            def _():
                unit_back(c, 0).start()

            @pl.when((section == 1) & (c < chunks - 1))
            def _():
                for f in range(1, repeat):
                    unit_back(c, f).start()
        @pl.when(section == 1)
        def _():
            pl.loop(0, chunks * repeat)(forward_share)

        @pl.loop(0, chunks)
        def _(c):
            @pl.when(section == 3)
            def _():
                forward_slot(c)

            backward(c)

    @pl.when(not_attn)
    def _():
        @pl.loop(0, pieces)
        def _(k):
            down_along(k).wait_send()
            down_pair(k).wait_send()
            down_last(k).wait_send()

    side = width // 2
    per_block = side // chunk
    w_chunks, d_chunks = 4 * per_block, 2 * per_block
    rows_all = chunks * WINDOW

    def grad_rows(block, first, count):
        return weights.at[block, pl.ds(pl.multiple_of(first, count), count)]

    def half_rows(block):
        return pl.ds(pl.multiple_of(block * side, side), side)

    def block_of(turn):
        last = turn + 2 * lax.div(turn, 4) - 4 * lax.div(turn, 6)
        first = turn + 3 * lax.div(turn + 7, 8) - 5 * lax.div(turn + 5, 8) + 2 * lax.div(turn, 6)
        second = odd - is_last
        return second * first + (1 - second) * last

    def sib_copy(block, source):
        return remote(
            source, theirs.at[half_rows(block)], sib_send.at[block], sib_recv.at[block], section, sibling
        )

    def outer(left, left_at, right, right_at, block):
        right_value = right[:, :, right_at].reshape(rows_all, width)

        @pl.loop(0, width // WINDOW)
        def _(k):
            columns = pl.ds(pl.multiple_of(left_at + k * WINDOW, WINDOW), WINDOW)
            left_value = left[:, :, columns].reshape(rows_all, WINDOW)
            rows = pl.ds(pl.multiple_of(k * WINDOW, WINDOW), WINDOW)
            weights[block, rows] = mm_tn(left_value, right_value).astype(BF16)

    def grad_block(turn):
        block = block_of(turn)

        @pl.when((block < 4) & (not_attn | (block < 3)))
        def _():
            columns = pl.ds(pl.multiple_of(block * width, width), width)
            outer(nrm, 0, keep_b, columns, block)

        @pl.when((block == 3) & is_attn)
        def _():
            outer(keep_b, 3 * width, gin, pl.ds(0, width), block)

        @pl.when(block >= 4)
        def _():
            outer(keep_a, (block - 4) * width, gin, pl.ds(0, width), block)

        sib_copy(block, grad_rows(block, (1 - core) * side, side)).start()

    def early_copy(at, source):
        return remote(
            source,
            grad_rows(4 + at, core * side, side),
            early_send.at[at],
            early_recv.at[at],
            2,
            me,
        )

    def guest_block(at, source):
        place_of = guest.at[half_rows(at % 2)]
        return remote(source, place_of, early_send.at[at], early_recv.at[at], 3 - at // 2, me)

    def pair_sum(turn):
        block = block_of(turn)
        sib_copy(block, theirs.at[half_rows(block)]).wait_recv()

        here = grad_rows(block, core * side, side)
        value = here[...].astype(F32) + theirs[half_rows(block)].astype(F32)
        here[...] = value.astype(BF16)

        @pl.when((section == 3) & ((block == 4) | (block == 5)))
        def _():
            early_copy(block - 4, here).start()

        for at, which in enumerate((4, 5, 7)):

            @pl.when((section == 1) & (block == which))
            def _():
                guest_block(at, here).start()

    small_all[me] = small[...]

    def small_copy(d):
        return remote(small, small_all.at[me], small_send.at[d], small_recv.at[0], section, d)

    @pl.loop(0, n)
    def _(d):
        @pl.when(d != me)
        def _():
            small_copy(d).start()

    own_lines = w_chunks + d_chunks
    is_second, is_third = odd - is_last, 1 - odd - is_first
    lines = own_lines + d_chunks * (is_last - is_first) + per_block * (is_third - is_second)
    guests = d_chunks * is_last + per_block * is_third
    ahead = own_lines - per_block

    def line_at(turn):
        late, last = lax.div(turn, ahead), lax.div(turn, ahead + guests)
        return turn + per_block * late - (per_block + guests) * last

    def line_rows(i):
        return pl.ds(pl.multiple_of(i * chunk, chunk), chunk)

    def with_chunk(i, use):
        slot = lax.div(i, per_block)
        first = core * side + lax.rem(i, per_block) * chunk

        @pl.when(i < own_lines)
        def _():
            block = slot + 2 * odd * lax.div(slot, 4)
            use(grad_rows(block, first, chunk))

        @pl.when(i >= own_lines)
        def _():
            use(guest.at[pl.ds(pl.multiple_of((i - own_lines) * chunk, chunk), chunk)])

    def total_rows(i):
        first = core * side + lax.rem(i, per_block) * chunk
        return total_hbm.at[lax.div(i, per_block), pl.ds(pl.multiple_of(first, chunk), chunk)]

    def low_rows(i):
        return from_low.at[line_rows(i)]

    def high_rows(i):
        return from_high.at[line_rows(i)]

    def up_copy(i, source):
        return remote(source, low_rows(i), up_send.at[i], low_recv.at[i], section, me + 2)

    def down_copy(i, source):
        return remote(source, high_rows(i), down_send.at[i], high_recv.at[i], section, me - 2)

    def left_copy(i, source, target):
        return remote(source, target, left_send.at[i], total_recv.at[i], section, me - 2)

    def right_copy(i, source, target):
        return remote(source, target, right_send.at[i], total_recv.at[i], section, me + 2)

    def pair_copy(i, source):
        return remote(source, total_rows(i), pair_send.at[i], pair_recv.at[0], section, sibling)

    def own_copy(i, source):
        return pltpu.make_async_copy(source, total_rows(i), local_sem.at[i])

    def guest_copy(k, source):
        owner = 1 - is_last
        home = total_rows(w_chunks + k + per_block * owner)
        return remote(source, home, guest_send.at[k], guest_recv.at[k], owner, me)

    def reduce_stage(i, root):
        def run(here):
            acc[...] = here[...].astype(F32)

            @pl.when((place <= root) & (place > 0))
            def _():
                up_copy(i, here).wait_recv()
                acc[...] += from_low[line_rows(i)].astype(F32)

            @pl.when((place >= root) & (place < places - 1))
            def _():
                down_copy(i, here).wait_recv()
                acc[...] += from_high[line_rows(i)].astype(F32)

            here[...] = acc[...].astype(BF16)

            @pl.when(place < root)
            def _():
                up_copy(i, here).start()

            @pl.when(place > root)
            def _():
                down_copy(i, here).start()

            @pl.when((place == root) & (i < own_lines))
            def _():
                @pl.when(place > 0)
                def _():
                    left_copy(i, here, total_rows(i)).start()

                @pl.when(place < places - 1)
                def _():
                    right_copy(i, here, total_rows(i)).start()

                pair_copy(i, here).start()
                own_copy(i, here).start()

            @pl.when((place == root) & (i >= own_lines))
            def _():
                @pl.when(place > 0)
                def _():
                    left_copy(i, here, high_rows(i)).start()

                @pl.when(place < places - 1)
                def _():
                    right_copy(i, here, low_rows(i)).start()

                guest_copy(i - own_lines, here).start()

        with_chunk(i, run)

    def pass_on(i, root, left_at, right_at, finish):
        @pl.when(place < root)
        def _():
            left_copy(i, left_at, left_at).wait_recv()

            @pl.when(place > 0)
            def _():
                left_copy(i, left_at, left_at).start()

            finish(left_at)

        @pl.when(place > root)
        def _():
            right_copy(i, right_at, right_at).wait_recv()

            @pl.when(place < places - 1)
            def _():
                right_copy(i, right_at, right_at).start()

            finish(right_at)

    def spread_stage(i, root):
        @pl.when(i < own_lines)
        def _():
            at = total_rows(i)
            pass_on(i, root, at, at, lambda ref: pair_copy(i, ref).start())

        @pl.when(i >= own_lines)
        def _():
            pass_on(
                i,
                root,
                high_rows(i),
                low_rows(i),
                lambda ref: guest_copy(i - own_lines, ref).start(),
            )

    to_pair = remote(small_out, small_pair, spair_send.at[0], spair_recv.at[0], partner, me)

    def sum_small():
        remote(
            small_all.at[pl.ds(0, n - 1)],
            small_all.at[pl.ds(0, n - 1)],
            small_send.at[0],
            small_recv.at[0],
            section,
            sibling,
        ).wait_recv()

        def add(d, so_far):
            return so_far + small_all[d]

        small_out[...] = lax.fori_loop(1, n, add, small_all[0])

        @pl.when(not_attn)
        def _():
            to_pair.start()

    height = places // 2
    pairs = lax.div(lines, 2)
    turns = 4 + 4 * odd

    @pl.loop(0, 1 + pairs + 2 * height * lag)
    def _(step):
        for at in range(2):
            turn = 2 * step - 1 + at

            @pl.when((turn >= 0) & (turn < turns))
            def _():
                grad_block(turn)

        if repeat > 1:

            @pl.when((section == 1) & (step == 0))
            def _():
                unit_back(chunks - 1, 0).wait_send()
                for f in range(1, repeat):
                    unit_back(chunks - 1, f).start()

        @pl.when(step == 6)
        def _():
            sum_small()

        @pl.when((section == 3) & (step == 8))
        def _():
            @pl.loop(0, chunks)
            def _(c):
                for s in range(SECTIONS - 1):
                    remote(
                        gcol.at[s, c], out_ref.at[c], o_send.at[s, c], o_recv.at[0], s, me
                    ).start()

        for at in range(2):
            turn = 2 * step - 3 + at

            @pl.when((turn >= 0) & (turn < turns))
            def _():
                pair_sum(turn)

        for at in range(2):

            @pl.when((section == 2) & (step == 1 + (4 + 2 * at) * per_block // 2))
            def _():
                early_copy(at, theirs.at[half_rows(at)]).wait_recv()

            @pl.when((section == 3) & (step == 1 + (5 + at) * per_block // 2))
            def _():
                guest_block(at, theirs.at[half_rows(at)]).wait_recv()

        @pl.when((section == 2) & (step == 1 + 5 * per_block // 2))
        def _():
            guest_block(2, theirs.at[half_rows(0)]).wait_recv()

        for stream in range(2):
            root = height - 1 + stream
            now = step - 1 - lag * (height - jnp.abs(place - root))

            @pl.when((now >= 0) & (now < pairs))
            def _():
                reduce_stage(line_at(2 * now + stream), root)

        for stream in range(2):
            root = height - 1 + stream
            past = step - 1 - lag * (height + jnp.abs(place - root))

            @pl.when((past >= 0) & (past < pairs))
            def _():
                spread_stage(line_at(2 * past + stream), root)

    @pl.when(section < 2)
    def _():
        @pl.loop(lines, own_lines)
        def _(i):
            here = total_rows(i)
            k = i - lines
            remote(here, here, guest_send.at[k], guest_recv.at[k], 3 - section, me).wait_recv()
            pair_copy(i, here).start()

    @pl.when(not_attn)
    def _():
        to_pair.wait_send()

    @pl.when(is_attn)
    def _():
        to_pair.wait_recv()
        small_out[5:7] = small_pair[3:5]

    @pl.loop(0, lines)
    def _(i):
        some = low_rows(i)

        for stream in range(2):
            root = height - 1 + stream

            @pl.when(lax.rem(i, 2) == stream)
            def _():
                @pl.when(place < root)
                def _():
                    up_copy(i, some).wait_send()

                @pl.when(place > root)
                def _():
                    down_copy(i, some).wait_send()

                @pl.when((place <= root) & (place > 0))
                def _():
                    left_copy(i, some, some).wait_send()

                @pl.when((place >= root) & (place < places - 1))
                def _():
                    right_copy(i, some, some).wait_send()

                @pl.when((place == root) & (i < own_lines))
                def _():
                    own_copy(i, some).wait()

        @pl.when(i < own_lines)
        def _():
            pair_copy(i, some).wait_send()

        @pl.when(i >= own_lines)
        def _():
            guest_copy(i - own_lines, some).wait_send()

    @pl.when(section < 2)
    def _():
        @pl.loop(lines, own_lines)
        def _(i):
            pair_copy(i, low_rows(i)).wait_send()

    @pl.loop(0, turns)
    def _(turn):
        block = block_of(turn)
        sib_copy(block, theirs.at[half_rows(block)]).wait_send()

    @pl.loop(0, n)
    def _(d):
        @pl.when(d != me)
        def _():
            small_copy(d).wait_send()

    @pl.when(is_attn)
    def _():
        @pl.loop(direct * is_first, pieces)
        def _(k):
            down_first(k).wait_send()

        send_bias.wait_send()

        @pl.when(section == 0)
        def _():
            @pl.loop(0, chunks - 2)
            def _(k):
                unit_copy(k).wait_send()

            @pl.loop(chunks * repeat - 2, chunks * repeat)
            def _(k):
                unit_copy(k).wait_send()

        @pl.when(section == 2)
        def _():
            @pl.loop(0, chunks)
            def _(c):
                slot_copy(c).wait_send()

    @pl.when(not_attn)
    def _():
        for at in range(2):
            early_copy(at, theirs.at[half_rows(at)]).wait_send()

        @pl.when(section == 1)
        def _():
            guest_block(2, theirs.at[half_rows(0)]).wait_send()

        @pl.when(section == 3)
        def _():
            @pl.loop(0, chunks)
            def _(c):
                slot_back(c).wait_send()

        @pl.when(section == 1)
        def _():
            @pl.loop(0, chunks - 1)
            def _(c):
                for f in range(repeat):
                    unit_back(c, f).wait_send()

            for f in range(min(1, repeat - 1), repeat):
                unit_back(chunks - 1, f).wait_send()

    @pl.when((section == 1) | (section == 2))
    def _():
        @pl.loop(chunks - depth, chunks)
        def _(c):
            slot = lax.rem(c, depth)
            remote(
                xsend.at[slot], xsend.at[slot], x_send.at[c], x_recv.at[0], 3 - section, me
            ).wait_send()

    @pl.when(section == 3)
    def _():
        @pl.loop(0, chunks)
        def _(c):
            for s in range(SECTIONS - 1):
                remote(
                    gcol.at[s, c], out_ref.at[c], o_send.at[s, c], o_recv.at[0], s, me
                ).wait_send()

    @pl.when(section != 3)
    def _():
        remote(out_ref, out_ref, o_send.at[0, 0], o_recv.at[0], 3, me).wait_recv()

    @pl.when(section == 0)
    def _():
        @pl.loop(0, chunks)
        def _(c):
            for s in range(1, SECTIONS):
                ig_copy(s, c).wait_send()

    @pl.when(section != 0)
    def _():
        remote(ig_ref, ig_ref, ig_send.at[0, 0], ig_recv.at[0], 0, me).wait_recv()

    remote(
        total_hbm.at[pl.ds(0, 3)],
        total_hbm.at[pl.ds(0, 3)],
        pair_send.at[0],
        pair_recv.at[0],
        section,
        sibling,
    ).wait_recv()


def pipeline(
    tokens, cotangent, gain, shift, weight, bias, down, hidden_bias, ftab, ttab, kind, chunk=96, lag=1
):
    micro, rows, width = tokens.shape
    wide = weight.shape[1]
    n = lax.axis_size("dp")
    across = min(n, 16)
    repeat = 16 // across
    slots = rows // WINDOW
    chunks = micro * slots
    quarter = width // SECTIONS
    depth = chunks if n <= 8 else 1
    pieces, direct = 4, 3
    cfg = (n, across, repeat, slots, chunks, width, wide, depth, chunk, lag, pieces, direct)
    vmem = pl.BlockSpec(memory_space=pltpu.VMEM)
    smem = pl.BlockSpec(memory_space=pltpu.SMEM)
    anywhere = pl.BlockSpec(memory_space=pl.ANY)
    dma = pltpu.SemaphoreType.DMA
    chunked = (chunks, WINDOW, width)
    side = width // 2
    lines = 8 * side // chunk
    per_chunk = [dma((lines,)) for _ in range(8)]
    return pl.pallas_call(
        functools.partial(main_kernel, cfg),
        out_shape=(
            jax.ShapeDtypeStruct((chunks, WINDOW, quarter), BF16),
            jax.ShapeDtypeStruct((chunks, WINDOW, quarter), BF16),
            jax.ShapeDtypeStruct((6, width, width), BF16),
            jax.ShapeDtypeStruct((8, width), F32),
        ),
        in_specs=[anywhere, anywhere, vmem, vmem, anywhere, vmem, anywhere, vmem, smem, smem, smem],
        out_specs=(vmem, vmem, anywhere, vmem),
        scratch_shapes=[
            pltpu.VMEM((8, width, width), BF16),
            pltpu.VMEM((chunks, WINDOW, wide), BF16),
            pltpu.VMEM((chunks, WINDOW, wide), BF16),
            pltpu.VMEM(chunked, BF16),
            pltpu.VMEM(chunked, BF16),
            pltpu.VMEM(chunked, BF16),
            pltpu.VMEM(chunked, BF16),
            pltpu.VMEM((WINDOW, width), BF16),
            pltpu.VMEM((SECTIONS - 1, chunks, WINDOW, quarter), BF16),
            pltpu.VMEM((depth, n, repeat, BLOCK, width), BF16),
            *[pltpu.VMEM((n, repeat, BLOCK, width), BF16) for _ in range(4)],
            pltpu.VMEM((WINDOW // BLOCK, BLOCK, width), BF16),
            pltpu.VMEM((1, wide // 2), F32),
            pltpu.VMEM((1, wide // 2), F32),
            pltpu.VMEM((2, WINDOW, WINDOW), F32),
            pltpu.SMEM((2, n), jnp.int32),
            pltpu.SMEM((2, across), jnp.int32),
            pltpu.VMEM((2 * side, width), BF16),
            pltpu.VMEM((8 * side, width), BF16),
            pltpu.VMEM((lines * chunk, width), BF16),
            pltpu.VMEM((lines * chunk, width), BF16),
            pltpu.VMEM((chunk, width), F32),
            pltpu.VMEM((8, width), F32),
            pltpu.VMEM((n, 8, width), F32),
            pltpu.VMEM((8, width), F32),
            dma((8,)),
            dma((4, pieces)),
            dma((4, pieces)),
            dma((pieces,)),
            dma((pieces,)),
            dma((1,)),
            dma((1,)),
            dma((chunks * repeat,)),
            dma((chunks * repeat,)),
            dma((chunks, repeat)),
            dma((chunks,)),
            dma((chunks,)),
            dma((chunks,)),
            dma((SECTIONS - 1, chunks)),
            dma((1,)),
            dma((SECTIONS, chunks)),
            dma((1,)),
            dma((8,)),
            dma((8,)),
            *per_chunk,
            dma((1,)),
            dma((lines,)),
            dma((3,)),
            dma((3,)),
            dma((lines // 4,)),
            dma((lines // 4,)),
            dma((n,)),
            dma((1,)),
            dma((1,)),
            dma((1,)),
        ],
        compiler_params=pltpu.CompilerParams(
            collective_id=0, has_side_effects=True, vmem_limit_bytes=63 * 1024 * 1024
        ),
        name="pipeline",
    )(
        tokens.reshape(chunked),
        cotangent.reshape(chunked),
        gain,
        shift,
        weight,
        bias,
        down,
        hidden_bias,
        ftab,
        ttab,
        kind,
    )


def finish_kernel(
    total_hbm,
    small_ref,
    ig_ref,
    out_ref,
    output,
    input_grad,
    gain,
    shift,
    weight_hbm,
    bias,
    down_hbm,
    hidden,
    short,
    full,
    in_sem,
    out_sem,
):
    width = total_hbm.shape[2]
    steps = short.shape[1]
    span = width // steps
    order = [(b, r) for b in range(6) for r in range(steps)]

    def read(b, r):
        rows = pl.ds(r * span, span)
        return pltpu.make_async_copy(total_hbm.at[b, rows], short.at[b, r], in_sem.at[b, r])

    def write(b, r):
        if b < 4:
            target = weight_hbm.at[pl.ds(r * span, span), pl.ds(b * width, width)]
        else:
            target = down_hbm.at[pl.ds((b - 4) * width + r * span, span)]
        return pltpu.make_async_copy(full.at[b, r], target, out_sem.at[b, r])

    for b, r in order:
        read(b, r).start()
    for b, r in order:
        read(b, r).wait()
        full[b, r] = short[b, r].astype(F32)
        write(b, r).start()
    slots = output.shape[2] // WINDOW
    for c in range(out_ref.shape[0]):
        at = pl.ds(c % slots * WINDOW, WINDOW)
        output[c // slots, :, at] = out_ref[c].T
        input_grad[c // slots, :, at] = ig_ref[c].astype(F32).T
    gain[...] = small_ref[0:1]
    shift[...] = small_ref[1:2]
    bias[...] = small_ref[2:3]
    for k in range(2):
        hidden[pl.ds(k * width, width)] = small_ref[5 + k]
    for b, r in order:
        write(b, r).wait()


def finish(total, small, input_grad, output, micro):
    width = total.shape[-1]
    steps = 2
    turned = (micro, output.shape[2], output.size // micro // output.shape[2])
    row = jax.ShapeDtypeStruct((1, width), F32)
    vmem = pl.BlockSpec(memory_space=pltpu.VMEM)
    anywhere = pl.BlockSpec(memory_space=pl.ANY)
    return pl.pallas_call(
        finish_kernel,
        out_shape=(
            jax.ShapeDtypeStruct(turned, BF16),
            jax.ShapeDtypeStruct(turned, F32),
            row,
            row,
            jax.ShapeDtypeStruct((width, SECTIONS * width), F32),
            row,
            jax.ShapeDtypeStruct((2 * width, width), F32),
            jax.ShapeDtypeStruct((2 * width,), F32),
        ),
        in_specs=[anywhere, vmem, vmem, vmem],
        out_specs=(vmem, vmem, vmem, vmem, anywhere, vmem, anywhere, vmem),
        scratch_shapes=[
            pltpu.VMEM((6, steps, width // steps, width), BF16),
            pltpu.VMEM((6, steps, width // steps, width), F32),
            pltpu.SemaphoreType.DMA((6, steps)),
            pltpu.SemaphoreType.DMA((6, steps)),
        ],
        compiler_params=pltpu.CompilerParams(vmem_limit_bytes=60 * 1024 * 1024),
        name="finish",
    )(total, small, input_grad, output)


def on_device(
    tokens,
    cotangent,
    norm_gain,
    norm_shift,
    in_weight,
    out_bias,
    down_weight,
    hidden_bias,
    frame_device,
    tube_device,
    clip_kind,
):
    micro, rows, width = tokens.shape
    output, input_grad, total, small_total = pipeline(
        tokens,
        cotangent,
        norm_gain,
        norm_shift,
        in_weight[0],
        out_bias,
        down_weight,
        hidden_bias,
        frame_device,
        tube_device,
        clip_kind,
    )
    output, input_grad, gain, shift, weight, bias, down, hidden = finish(
        total, small_total, input_grad, output, micro
    )
    return (
        output.transpose(0, 2, 1),
        input_grad.transpose(0, 2, 1),
        gain,
        shift,
        weight[None],
        bias,
        down,
        hidden,
    )


def solution(mesh):
    return jax.shard_map(
        on_device,
        mesh=mesh,
        in_specs=(
            P(None, "dp", None),
            P(None, "dp", None),
            P("section", None),
            P("section", None),
            P("section", None, None),
            P("section", None),
            P("section", None),
            P("section"),
            P(),
            P(),
            P(),
        ),
        out_specs=(
            P(None, "dp", "section"),
            P(None, "dp", "section"),
            P("section", None),
            P("section", None),
            P("section", None, None),
            P("section", None),
            P("section", None),
            P("section"),
        ),
        check_vma=False,
    )
```
